32 devices in a mesh: fsdp: 8 (over y, x, core), dp: 4 (over z).
Axes of the slice: x: 2, y: 2, z: 4, core: 2. Of those that a mesh axis runs over, the one named last changes fastest.
Arguments:
- language: bfloat16 [256, 20, 768], P(('fsdp', 'dp')), may hold values from -6 to 6
- vision: bfloat16 [256, 36, 768], P(('fsdp', 'dp')), may hold values from -6 to 6
- region_mask: int32 [256, 36], P(('fsdp', 'dp')), may hold values from 0 to 1, as said below
- cross_qkv: float32 [3, 768, 768], P(None, 'fsdp'), may hold values from -0.21875 to 0.21875
- cross_out: float32 [768, 768], P('fsdp'), may hold values from -0.875 to 0.875
- cross_bias: float32 [4, 768], P(None, 'fsdp'), may hold values from -3 to 3
- cross_gain: float32 [768], P('fsdp'), may hold values from 0.5 to 1.5
- self_qkv: float32 [2, 3, 768, 768], P(None, None, 'fsdp'), may hold values from -0.21875 to 0.21875
- self_out: float32 [2, 768, 768], P(None, 'fsdp'), may hold values from -0.875 to 0.875
- self_bias: float32 [2, 4, 768], P(None, None, 'fsdp'), may hold values from -3 to 3
- self_gain: float32 [2, 768], P(None, 'fsdp'), may hold values from 0.5 to 1.5
- ffn_up: float32 [2, 768, 3072], P(None, 'fsdp'), may hold values from -0.21875 to 0.21875
- ffn_up_bias: float32 [2, 3072], P(None, 'fsdp'), may hold values from -3 to 3
- ffn_down: float32 [2, 3072, 768], P(None, 'fsdp'), may hold values from -0.109375 to 0.109375
- ffn_bias: float32 [2, 2, 768], P(None, None, 'fsdp'), may hold values from -3 to 3
- ffn_gain: float32 [2, 768], P(None, 'fsdp'), may hold values from 0.5 to 1.5
- language_cotangent: bfloat16 [256, 20, 768], P(('fsdp', 'dp')), may hold values from -6 to 6
- vision_cotangent: bfloat16 [256, 36, 768], P(('fsdp', 'dp')), may hold values from -6 to 6
Outputs:
- language_output: bfloat16 [256, 20, 768], P(('fsdp', 'dp'))
- vision_output: bfloat16 [256, 36, 768], P(('fsdp', 'dp'))
- language_gradient: float32 [256, 20, 768], P(('fsdp', 'dp'))
- vision_gradient: float32 [256, 36, 768], P(('fsdp', 'dp'))
- grad_cross_qkv: float32 [3, 768, 768], P(None, 'fsdp')
- grad_cross_out: float32 [768, 768], P('fsdp')
- grad_cross_bias: float32 [4, 768], P(None, 'fsdp')
- grad_cross_gain: float32 [768], P('fsdp')
- grad_self_qkv: float32 [2, 3, 768, 768], P(None, None, 'fsdp')
- grad_self_out: float32 [2, 768, 768], P(None, 'fsdp')
- grad_self_bias: float32 [2, 4, 768], P(None, None, 'fsdp')
- grad_self_gain: float32 [2, 768], P(None, 'fsdp')
- grad_ffn_up: float32 [2, 768, 3072], P(None, 'fsdp')
- grad_ffn_up_bias: float32 [2, 3072], P(None, 'fsdp')
- grad_ffn_down: float32 [2, 3072, 768], P(None, 'fsdp')
- grad_ffn_bias: float32 [2, 2, 768], P(None, None, 'fsdp')
- grad_ffn_gain: float32 [2, 768], P(None, 'fsdp')
The draws below stay inside these ranges and needn't reach their ends.
Inputs may be any that keep to these rules, and one draw needn't show every extreme that they name: `region_mask`: each item's row is 1 on its first r positions and 0 after, r from 10 to 36 and mostly near 10; some item has all 36 regions.
All inputs are finite; a program needn't handle non-finite values.
Results may differ from the reference program's by a relative error of at most 0.022.
Values may be sent and summed in bfloat16 or wider, within the bound.
No kernel may reach another device: no remote copies, remote signals or barrier semaphores. Data moves between devices by JAX's collectives and lax.ppermute only.
A program may use at most 192 MiB of HBM per device.

```python
import math
import jax
import jax.numpy as jnp
from jax import lax

HEADS = 12
HEAD_DIM = 64
FF = 3072
WORDS = 20
REGIONS = 36
MIN_REGIONS = 10
D = 768
ITEMS = 256


def draw_region_mask(key, part):
    key = jax.random.fold_in(key, 7)
    key_one, key_two, key_three, key_full = jax.random.split(key, 4)
    spread = REGIONS - MIN_REGIONS + 1
    added_count = jnp.minimum(jax.random.randint(key_one, (ITEMS,), 0, spread), jax.random.randint(key_two, (ITEMS,), 0, spread))
    added_count = jnp.minimum(added_count, jax.random.randint(key_three, (ITEMS,), 0, spread))
    full_item = jax.random.randint(key_full, (), 0, ITEMS)
    counts = jnp.where(jnp.arange(ITEMS) == full_item, REGIONS, MIN_REGIONS + added_count)
    return (jnp.arange(REGIONS)[None, :] < counts[:, None]).astype(jnp.int32)


def raised(values, own_key, source, target, parts, factor):
    owner, partner = [(jnp.arange(values.shape[dim]) // (values.shape[dim] // parts)).reshape([-1 if axis == dim else 1 for axis in range(values.ndim)]) for dim in (source, target)]
    chosen = jax.random.permutation(own_key, parts)[partner]
    strong = (owner == chosen) | (owner == (partner + parts // 2) % parts)
    return jnp.where(strong, factor * values, values)


def level_of(key, shape, cuts, low, high):
    level, own = 1.0, jax.random.fold_in(key, 6)
    for position, blocks in cuts:
        draws = jnp.exp(jax.random.uniform(jax.random.fold_in(own, position), (blocks,), jnp.float32, low / len(cuts), high / len(cuts)))
        level = level * jnp.repeat(draws, shape[position] // blocks).reshape([-1 if axis == position else 1 for axis in range(len(shape))])
    return level


def bell_draw(rng, extent, scale, most, shards=(), held_as=jnp.bfloat16):
    values = scale * jax.random.normal(rng, extent, jnp.float32)
    if shards:
        values = values * level_of(rng, extent, shards, -0.22, 0.18)
    return jnp.clip(values, -most, most).astype(held_as)


def heavy_noise(stream_key, shape, scale, reach, shards, heavy, kind=jnp.bfloat16):
    entries = scale * jax.random.normal(stream_key, shape, jnp.float32)
    if shards:
        entries = entries * level_of(stream_key, shape, shards, -0.22, 0.18)
    return jnp.clip(raised(entries, jax.random.fold_in(stream_key, 3), *heavy), -reach, reach).astype(kind)


def setup_inputs(seed: int = 0) -> dict:
    splits = jax.random.split(jax.random.key(seed), 19)
    return {
        "language": bell_draw(splits[0], (ITEMS, WORDS, D), 1.0, 6.0, ((0, 32),)),
        "vision": bell_draw(splits[1], (ITEMS, REGIONS, D), 1.0, 6.0, ((0, 32),)),
        "region_mask": draw_region_mask(jax.random.fold_in(splits[18], 71), 0),
        "cross_qkv": bell_draw(splits[3], (3, D, D), D ** -0.5, 0.21875, ((1, 8),), jnp.float32),
        "cross_out": bell_draw(splits[4], (D, D), (D // 16) ** -0.5, 0.875, ((0, 8),), jnp.float32),
        "cross_bias": bell_draw(splits[5], (4, D), 0.5, 3.0, ((1, 8),), jnp.float32),
        "cross_gain": jnp.clip(1.0 + 0.1 * jax.random.normal(splits[6], (D,), jnp.float32), 0.5, 1.5),
        "self_qkv": bell_draw(splits[7], (2, 3, D, D), D ** -0.5, 0.21875, ((2, 8),), jnp.float32),
        "self_out": bell_draw(splits[8], (2, D, D), (D // 16) ** -0.5, 0.875, ((1, 8),), jnp.float32),
        "self_bias": bell_draw(splits[9], (2, 4, D), 0.5, 3.0, ((2, 8),), jnp.float32),
        "self_gain": jnp.clip(1.0 + 0.1 * jax.random.normal(splits[10], (2, D), jnp.float32), 0.5, 1.5),
        "ffn_up": bell_draw(splits[11], (2, D, FF), D ** -0.5, 0.21875, ((1, 8),), jnp.float32),
        "ffn_up_bias": bell_draw(splits[12], (2, FF), 0.5, 3.0, ((1, 8),), jnp.float32),
        "ffn_down": bell_draw(splits[13], (2, FF, D), FF ** -0.5, 0.109375, ((1, 8),), jnp.float32),
        "ffn_bias": bell_draw(splits[14], (2, 2, D), 0.5, 3.0, ((2, 8),), jnp.float32),
        "ffn_gain": jnp.clip(1.0 + 0.1 * jax.random.normal(splits[15], (2, D), jnp.float32), 0.5, 1.5),
        "language_cotangent": heavy_noise(splits[16], (ITEMS, WORDS, D), 1.0, 6.0, ((0, 32),), (0, 2, 32, 2.75)),
        "vision_cotangent": heavy_noise(splits[17], (ITEMS, REGIONS, D), 1.0, 6.0, ((0, 32),), (0, 2, 32, 2.75)),
    }


@jax.custom_vjp
def low(v):
    return lax.optimization_barrier(v.astype(jnp.bfloat16)).astype(jnp.float32)

@jax.custom_vjp
def low_back(v):
    return v

def low_keep(v):
    return (low(v), None)

def low_pass(kept, grad):
    return (grad,)

def back_keep(v):
    return (v, None)

def back_low(kept, grad):
    return (low(grad),)
low.defvjp(low_keep, low_pass)
low_back.defvjp(back_keep, back_low)
highest = lax.Precision.HIGHEST
epsilon = 1e-06

def linear(inputs, weight):
    return jnp.einsum('...i,io->...o', inputs, weight, precision=highest)

def split_heads(values):
    return values.reshape(values.shape[:-1] + (HEADS, HEAD_DIM))

def layer_norm(values, norm_gain, norm_shift):
    centre = values - lax.optimization_barrier(jnp.mean(values, axis=-1, keepdims=True))
    spread = lax.optimization_barrier(jnp.mean(centre * centre, axis=-1, keepdims=True))
    return centre * lax.rsqrt(spread + epsilon) * norm_gain + norm_shift

def attend(query_rows, key_rows, key_mask, projections, out_weight, biases):
    query_vectors = low(low_back(linear(query_rows, projections[0]) + biases[0]))
    key_vectors = low(low_back(linear(key_rows, projections[1])))
    value_vectors = low(low_back(linear(key_rows, projections[2]) + biases[1]))
    scores = jnp.einsum('bqhe,bkhe->bhqk', split_heads(query_vectors), split_heads(key_vectors), precision=highest)
    scores = low_back(scores * HEAD_DIM ** (-0.5))
    if key_mask is not None:
        scores = jnp.where(key_mask[:, None, None, :] > 0, scores, -1000000000.0)
    attention = low(jax.nn.softmax(scores, axis=-1))
    context = jnp.einsum('bhqk,bkhe->bqhe', attention, split_heads(value_vectors), precision=highest)
    context = low(low_back(context.reshape(query_rows.shape)))
    return low_back(linear(context, out_weight) + biases[2])

def feed(token_rows, up_weight, up_bias, down_weight, down_bias):
    before = low_back(linear(token_rows, up_weight) + up_bias)
    hidden = low(jax.nn.gelu(before, approximate=False))
    return low_back(linear(hidden, down_weight) + down_bias)

def forward(language, vision, mask_float, params):
    cross_qkv, cross_out, cross_bias, cross_gain, self_qkv, self_out, self_bias, self_gain, ffn_up, ffn_up_bias, ffn_down, ffn_bias, ffn_gain = jax.tree.map(low, params)
    language_in = low(language)
    vision_in = low(vision)
    language_a = layer_norm(language + attend(language_in, vision_in, mask_float, cross_qkv, cross_out, cross_bias), cross_gain, cross_bias[3])
    vision_a = layer_norm(vision + attend(vision_in, language_in, None, cross_qkv, cross_out, cross_bias), cross_gain, cross_bias[3])
    language_a_in = low(language_a)
    vision_a_in = low(vision_a)
    language_b = layer_norm(language_a + attend(language_a_in, language_a_in, None, self_qkv[0], self_out[0], self_bias[0]), self_gain[0], self_bias[0, 3])
    vision_b = layer_norm(vision_a + attend(vision_a_in, vision_a_in, mask_float, self_qkv[1], self_out[1], self_bias[1]), self_gain[1], self_bias[1, 3])
    language_c = layer_norm(language_b + feed(low(language_b), ffn_up[0], ffn_up_bias[0], ffn_down[0], ffn_bias[0, 0]), ffn_gain[0], ffn_bias[0, 1])
    vision_c = layer_norm(vision_b + feed(low(vision_b), ffn_up[1], ffn_up_bias[1], ffn_down[1], ffn_bias[1, 0]), ffn_gain[1], ffn_bias[1, 1])
    return (language_c, vision_c * mask_float[:, :, None])

def reference(language, vision, region_mask, cross_qkv, cross_out, cross_bias, cross_gain, self_qkv, self_out, self_bias, self_gain, ffn_up, ffn_up_bias, ffn_down, ffn_bias, ffn_gain, language_cotangent, vision_cotangent):
    params = (cross_qkv, cross_out, cross_bias, cross_gain, self_qkv, self_out, self_bias, self_gain, ffn_up, ffn_up_bias, ffn_down, ffn_bias, ffn_gain)
    block = math.gcd(ITEMS, 64)
    groups = ITEMS // block

    def regroup(array):
        return array.reshape((groups, block) + array.shape[1:])

    def ungroup(array):
        return array.reshape((ITEMS,) + array.shape[2:])

    def one_block(totals, pieces):
        language_piece, vision_piece, mask_piece, language_tangent, vision_tangent = pieces
        mask_float = mask_piece.astype(jnp.float32)

        def local(language_value, vision_value, param_values):
            return forward(language_value, vision_value, mask_float, param_values)
        outputs, pull_back = jax.vjp(local, language_piece.astype(jnp.float32), vision_piece.astype(jnp.float32), params)
        grad_language, grad_vision, grad_params = pull_back((language_tangent.astype(jnp.float32), vision_tangent.astype(jnp.float32)))
        totals = jax.tree.map(jnp.add, totals, grad_params)
        return (totals, (outputs[0].astype(jnp.bfloat16), outputs[1].astype(jnp.bfloat16), grad_language, grad_vision))
    start = jax.tree.map(jnp.zeros_like, params)
    totals, results = lax.scan(one_block, start, (regroup(language), regroup(vision), regroup(region_mask), regroup(language_cotangent), regroup(vision_cotangent)))
    return (ungroup(results[0]), ungroup(results[1]), ungroup(results[2]), ungroup(results[3]), totals[0], totals[1], totals[2], totals[3], totals[4], totals[5], totals[6], totals[7], totals[8], totals[9], totals[10], totals[11], totals[12])
```

```python
import jax
import jax.numpy as jnp
from jax import lax
from jax.sharding import PartitionSpec as P

HEADS = 12
HEAD_DIM = 64


epsilon = 1e-06
masked_score = -1000000000.0


def rounded(values):
    return values.astype(jnp.bfloat16)


def widened(values):
    return values.astype(jnp.float32)


def matmul(inputs, weight):
    return jnp.einsum("...i,io->...o", inputs, weight, preferred_element_type=jnp.float32)


def matmul_back(gradient, weight):
    return jnp.einsum("...o,io->...i", gradient, weight, preferred_element_type=jnp.float32)


def weight_grad(inputs, gradient):
    flat_inputs = inputs.reshape(-1, inputs.shape[-1])
    flat_gradient = gradient.reshape(-1, gradient.shape[-1])
    return jnp.einsum("ni,no->io", flat_inputs, flat_gradient, preferred_element_type=jnp.float32)


def column_sum(gradient):
    return jnp.sum(widened(gradient).reshape(-1, gradient.shape[-1]), axis=0)


def split_heads(values):
    return values.reshape(values.shape[:-1] + (HEADS, HEAD_DIM))


def norm_apply(values, norm_gain, norm_shift):
    centre = values - jnp.mean(values, axis=-1, keepdims=True)
    spread = jnp.mean(centre * centre, axis=-1, keepdims=True)
    return centre * lax.rsqrt(spread + epsilon) * norm_gain + norm_shift


def gelu_exact(values):
    return jax.nn.gelu(values, approximate=False)


def masked_scores(query_heads, key_heads, key_mask):
    scores = jnp.einsum(
        "bqhe,bkhe->bhqk", query_heads, key_heads, preferred_element_type=jnp.float32
    ) * HEAD_DIM ** (-0.5)
    if key_mask is None:
        return scores
    return jnp.where(key_mask[:, None, None, :] > 0, scores, masked_score)


def attend_forward(query_in, key_in, key_mask, projections, out_weight, biases):
    query_vectors = rounded(matmul(query_in, projections[0]) + widened(biases[0]))
    key_vectors = rounded(matmul(key_in, projections[1]))
    value_vectors = rounded(matmul(key_in, projections[2]) + widened(biases[1]))
    scores = masked_scores(split_heads(query_vectors), split_heads(key_vectors), key_mask)
    top_score = jnp.max(scores, axis=-1, keepdims=True)
    shifted = jnp.exp(scores - top_score)
    totals = jnp.sum(shifted, axis=-1, keepdims=True)
    attention = rounded(shifted / totals)
    log_total = top_score + jnp.log(totals)
    context = jnp.einsum(
        "bhqk,bkhe->bqhe", attention, split_heads(value_vectors), preferred_element_type=jnp.float32
    )
    context = rounded(context.reshape(query_in.shape))
    branch = matmul(context, out_weight) + widened(biases[2])
    return (branch, (query_vectors, key_vectors, value_vectors, log_total, context))


def attend_backward(d_branch, query_in, key_in, key_mask, projections, out_weight, kept):
    query_vectors, key_vectors, value_vectors, log_total, context = kept
    d_branch_low = rounded(d_branch)
    grad_final = weight_grad(context, d_branch_low)
    grad_final_bias = column_sum(d_branch_low)
    d_context = split_heads(rounded(matmul_back(d_branch_low, out_weight)))
    query_heads = split_heads(query_vectors)
    key_heads = split_heads(key_vectors)
    value_heads = split_heads(value_vectors)
    attention = jnp.exp(masked_scores(query_heads, key_heads, key_mask) - log_total)
    d_attention = jnp.einsum(
        "bqhe,bkhe->bhqk", d_context, value_heads, preferred_element_type=jnp.float32
    )
    d_values = jnp.einsum(
        "bhqk,bqhe->bkhe", rounded(attention), d_context, preferred_element_type=jnp.float32
    )
    d_scores = attention * (d_attention - jnp.sum(d_attention * attention, axis=-1, keepdims=True))
    d_scores = rounded(d_scores)
    scale = HEAD_DIM ** (-0.5)
    d_queries = rounded(
        jnp.einsum("bhqk,bkhe->bqhe", d_scores, key_heads, preferred_element_type=jnp.float32)
        * scale
    ).reshape(query_vectors.shape)
    d_keys = rounded(
        jnp.einsum("bhqk,bqhe->bkhe", d_scores, query_heads, preferred_element_type=jnp.float32)
        * scale
    ).reshape(key_vectors.shape)
    d_values = rounded(d_values).reshape(value_vectors.shape)
    projection_grads = jnp.stack(
        [
            weight_grad(query_in, d_queries),
            weight_grad(key_in, d_keys),
            weight_grad(key_in, d_values),
        ]
    )
    d_query_in = matmul_back(d_queries, projections[0])
    d_key_in = matmul_back(d_keys, projections[1]) + matmul_back(d_values, projections[2])
    return (
        d_query_in,
        d_key_in,
        projection_grads,
        grad_final,
        (column_sum(d_queries), column_sum(d_values), grad_final_bias),
    )


def feed_forward(token_in, up_weight, up_bias, down_weight, down_bias):
    before = matmul(token_in, up_weight) + widened(up_bias)
    hidden, gelu_pull = jax.vjp(gelu_exact, before)
    hidden = rounded(hidden)
    branch = matmul(hidden, down_weight) + widened(down_bias)
    return (branch, (hidden, gelu_pull))


def feed_backward(d_branch, token_in, up_weight, down_weight, kept):
    hidden, gelu_pull = kept
    d_branch_low = rounded(d_branch)
    d_hidden = matmul_back(d_branch_low, down_weight)
    d_before = rounded(gelu_pull(d_hidden)[0])
    grads = (
        weight_grad(token_in, d_before),
        column_sum(d_before),
        weight_grad(hidden, d_branch_low),
        column_sum(d_branch_low),
    )
    return (matmul_back(d_before, up_weight), grads)


def swap(values, axis, mask, size):
    return lax.ppermute(values, axis, [(place, place ^ mask) for place in range(size)])


def gather_pieces(shard):
    half = shard.shape[0] // 2
    pieces = {0: shard}
    pieces[2] = swap(shard, "fsdp", 2, 8)
    pieces[4] = swap(shard, "fsdp", 4, 8)
    first = swap(pieces[4][:half], "fsdp", 2, 8)
    second = swap(pieces[2][half:], "fsdp", 4, 8)
    pieces[6] = jnp.concatenate([first, second])
    for place in (0, 2, 4, 6):
        pieces[place + 1] = swap(pieces[place], "fsdp", 1, 8)
    return pieces


def gathered(shard, plane):
    if plane != 8:
        return lax.all_gather(shard, "fsdp", axis=1, tiled=True)
    me = lax.axis_index("fsdp")
    pieces = gather_pieces(shard)
    count, rows, width = shard.shape
    whole = jnp.zeros((count, 8 * rows, width), shard.dtype)
    for place, piece in pieces.items():
        whole = lax.dynamic_update_slice(whole, piece, (0, (me ^ place) * rows, 0))
    return whole


def line_sum(own, length):
    up, down = None, None
    for hop in range(length - 1):
        there = own if up is None else rounded(widened(own) + widened(up))
        back = own if down is None else rounded(widened(own) + widened(down))
        new_up = lax.ppermute(there, "dp", [(hop, hop + 1)])
        new_down = lax.ppermute(back, "dp", [(length - 1 - hop, length - 2 - hop)])
        up = new_up if up is None else up + new_up
        down = new_down if down is None else down + new_down
    return widened(own) + widened(up) + widened(down)


def owned_sum(grad, plane, length):
    grad = rounded(grad)
    if plane != 8:
        return widened(lax.psum(lax.psum_scatter(grad, "fsdp", scatter_dimension=1, tiled=True), "dp"))
    me = lax.axis_index("fsdp")
    count, rows, width = grad.shape[0], grad.shape[1] // 8, grad.shape[2]
    half = count // 2
    part = lambda place: lax.dynamic_slice(grad, (0, (me ^ place) * rows, 0), (count, rows, width))
    sums = {}
    for place in (6, 4, 2, 0):
        sums[place] = rounded(widened(part(place)) + widened(swap(part(place + 1), "fsdp", 1, 8)))
    from_x = swap(sums[6][:half], "fsdp", 2, 8)
    from_y = swap(sums[6][half:], "fsdp", 4, 8)
    to_y = jnp.concatenate([rounded(widened(sums[4][:half]) + widened(from_x)), sums[4][half:]])
    to_x = jnp.concatenate([sums[2][:half], rounded(widened(sums[2][half:]) + widened(from_y))])
    from_x = swap(to_x, "fsdp", 2, 8)
    from_y = swap(to_y, "fsdp", 4, 8)
    own = rounded(widened(sums[0]) + widened(from_x) + widened(from_y))
    return line_sum(own, length)


def body(
    language,
    vision,
    region_mask,
    cross_qkv,
    cross_out,
    cross_bias,
    cross_gain,
    self_qkv,
    self_out,
    self_bias,
    self_gain,
    ffn_up,
    ffn_up_bias,
    ffn_down,
    ffn_bias,
    ffn_gain,
    language_cotangent,
    vision_cotangent,
):
    mask_float = widened(region_mask)
    mask_rows = mask_float[:, :, None]
    plane, length = lax.axis_size("fsdp"), lax.axis_size("dp")
    me = lax.axis_index("fsdp")
    local = cross_gain.shape[0]
    small = [cross_bias, cross_gain[None], self_bias.reshape(8, local), self_gain, ffn_bias.reshape(4, local), ffn_gain, ffn_up_bias.reshape(2, 4, local).reshape(8, local)]
    small = rounded(jnp.concatenate(small))
    vectors = lax.all_gather(small, "fsdp", axis=1, tiled=True)
    up_vec = vectors[21:29].reshape(2, 4, plane, local).transpose(0, 2, 1, 3).reshape(2, -1)
    cross_vec, cross_norm = vectors[0:4], vectors[4]
    self_vec, self_norm = vectors[5:13].reshape(2, 4, -1), vectors[13:15]
    ffn_vec, ffn_norm = vectors[15:19].reshape(2, 2, -1), vectors[19:21]
    width = cross_out.shape[1]
    cross_all = gathered(jnp.concatenate([rounded(cross_qkv), rounded(cross_out)[None]]), plane)
    cross_proj, cross_final = cross_all[:3], cross_all[3]
    self_all = gathered(jnp.concatenate([rounded(self_qkv).reshape(6, local, width), rounded(self_out)]), plane)
    self_proj, self_final = self_all[:6].reshape(2, 3, width, width), self_all[6:]
    ups, downs = [], []
    for stream in range(2):
        up_shard = rounded(ffn_up[stream]).reshape(local, 4, width).transpose(1, 0, 2)
        down_shard = rounded(ffn_down[stream]).reshape(4, local, width)
        ffn_all = gathered(jnp.concatenate([up_shard, down_shard]), plane)
        ups.append(ffn_all[:4].transpose(1, 0, 2).reshape(width, 4 * width))
        downs.append(ffn_all[4:].reshape(4, plane, local, width).transpose(1, 0, 2, 3).reshape(4 * width, width))
    language_branch, language_cross_kept = attend_forward(
        language, vision, mask_float, cross_proj, cross_final, cross_vec
    )
    vision_branch, vision_cross_kept = attend_forward(
        vision, language, None, cross_proj, cross_final, cross_vec
    )
    language_a, language_cross_pull = jax.vjp(
        norm_apply, widened(language) + language_branch, widened(cross_norm), widened(cross_vec[3])
    )
    vision_a, vision_cross_pull = jax.vjp(
        norm_apply, widened(vision) + vision_branch, widened(cross_norm), widened(cross_vec[3])
    )
    language_a_in = rounded(language_a)
    vision_a_in = rounded(vision_a)
    language_branch, language_self_kept = attend_forward(
        language_a_in, language_a_in, None, self_proj[0], self_final[0], self_vec[0]
    )
    vision_branch, vision_self_kept = attend_forward(
        vision_a_in, vision_a_in, mask_float, self_proj[1], self_final[1], self_vec[1]
    )
    language_b, language_self_pull = jax.vjp(
        norm_apply, language_a + language_branch, widened(self_norm[0]), widened(self_vec[0, 3])
    )
    vision_b, vision_self_pull = jax.vjp(
        norm_apply, vision_a + vision_branch, widened(self_norm[1]), widened(self_vec[1, 3])
    )
    up_held, up_bias_held, down_held = ups, up_vec, downs
    language_b_in = rounded(language_b)
    vision_b_in = rounded(vision_b)
    language_branch, language_feed_kept = feed_forward(
        language_b_in, up_held[0], up_bias_held[0], down_held[0], ffn_vec[0, 0]
    )
    vision_branch, vision_feed_kept = feed_forward(
        vision_b_in, up_held[1], up_bias_held[1], down_held[1], ffn_vec[1, 0]
    )
    language_c, language_feed_pull = jax.vjp(
        norm_apply, language_b + language_branch, widened(ffn_norm[0]), widened(ffn_vec[0, 1])
    )
    vision_c, vision_feed_pull = jax.vjp(
        norm_apply, vision_b + vision_branch, widened(ffn_norm[1]), widened(ffn_vec[1, 1])
    )
    language_output = rounded(language_c)
    vision_output = rounded(vision_c * mask_rows)
    up_back, down_back = ups, downs
    d_sum_lang, gain_lang, shift_lang = language_feed_pull(widened(language_cotangent))
    d_sum_vis, gain_vis, shift_vis = vision_feed_pull(widened(vision_cotangent) * mask_rows)
    d_in_lang, feed_lang = feed_backward(
        d_sum_lang, language_b_in, up_back[0], down_back[0], language_feed_kept
    )
    d_in_vis, feed_vis = feed_backward(
        d_sum_vis, vision_b_in, up_back[1], down_back[1], vision_feed_kept
    )
    d_language_b = d_sum_lang + d_in_lang
    d_vision_b = d_sum_vis + d_in_vis
    ffn_sums = []
    for grads in (feed_lang, feed_vis):
        up_grad = grads[0].reshape(width, 4, width).transpose(1, 0, 2)
        down_grad = grads[2].reshape(plane, 4, local, width).transpose(1, 0, 2, 3).reshape(4, width, width)
        ffn_sums.append(owned_sum(jnp.concatenate([up_grad, down_grad]), plane, length))
    ffn_small = [feed_lang[3], shift_lang, feed_vis[3], shift_vis, gain_lang, gain_vis]
    up_small = [feed_lang[1], feed_vis[1]]
    self_proj_back, self_final_back = self_proj, self_final
    d_sum_lang, gain_lang, shift_lang = language_self_pull(d_language_b)
    d_sum_vis, gain_vis, shift_vis = vision_self_pull(d_vision_b)
    d_query_lang, d_key_lang, proj_lang, final_lang, vec_lang = attend_backward(
        d_sum_lang,
        language_a_in,
        language_a_in,
        None,
        self_proj_back[0],
        self_final_back[0],
        language_self_kept,
    )
    d_query_vis, d_key_vis, proj_vis, final_vis, vec_vis = attend_backward(
        d_sum_vis,
        vision_a_in,
        vision_a_in,
        mask_float,
        self_proj_back[1],
        self_final_back[1],
        vision_self_kept,
    )
    d_language_a = d_sum_lang + d_query_lang + d_key_lang
    d_vision_a = d_sum_vis + d_query_vis + d_key_vis
    self_sum = owned_sum(jnp.concatenate([proj_lang, proj_vis, final_lang[None], final_vis[None]]), plane, length)
    self_small = [*vec_lang, shift_lang, *vec_vis, shift_vis, gain_lang, gain_vis]
    cross_proj_back, cross_final_back = cross_proj, cross_final
    d_sum_lang, gain_lang, shift_lang = language_cross_pull(d_language_a)
    d_sum_vis, gain_vis, shift_vis = vision_cross_pull(d_vision_a)
    d_query_lang, d_key_from_vis, proj_lang, final_lang, vec_lang = attend_backward(
        d_sum_lang,
        language,
        vision,
        mask_float,
        cross_proj_back,
        cross_final_back,
        language_cross_kept,
    )
    d_query_vis, d_key_from_lang, proj_vis, final_vis, vec_vis = attend_backward(
        d_sum_vis, vision, language, None, cross_proj_back, cross_final_back, vision_cross_kept
    )
    language_gradient = d_sum_lang + d_query_lang + d_key_from_lang
    vision_gradient = d_sum_vis + d_query_vis + d_key_from_vis
    cross_sum = owned_sum(jnp.concatenate([proj_lang + proj_vis, (final_lang + final_vis)[None]]), plane, length)
    cross_small = [a + b for a, b in zip(vec_lang, vec_vis)] + [shift_lang + shift_vis, gain_lang + gain_vis]
    small = jnp.stack(cross_small + self_small + ffn_small)
    up_small = jnp.stack(up_small).reshape(2, plane, 4, local).transpose(0, 2, 1, 3).reshape(8, width)
    small = lax.psum(jnp.concatenate([small, up_small]), ("fsdp", "dp"))
    small = lax.dynamic_slice(small, (0, me * local), (29, local))
    up_sum = jnp.stack([ffn_sums[0][:4], ffn_sums[1][:4]]).transpose(0, 2, 1, 3).reshape(2, local, 4 * width)
    down_sum = jnp.stack([ffn_sums[0][4:], ffn_sums[1][4:]]).reshape(2, 4 * local, width)
    return (
        language_output,
        vision_output,
        language_gradient,
        vision_gradient,
        cross_sum[:3],
        cross_sum[3],
        small[0:4],
        small[4],
        self_sum[:6].reshape(2, 3, local, width),
        self_sum[6:],
        small[5:13].reshape(2, 4, local),
        small[13:15],
        up_sum,
        small[21:29].reshape(2, 4 * local),
        down_sum,
        small[15:19].reshape(2, 2, local),
        small[19:21],
    )


def solution(mesh):
    return jax.shard_map(
        body,
        mesh=mesh,
        in_specs=(
            P(("fsdp", "dp"), None, None),
            P(("fsdp", "dp"), None, None),
            P(("fsdp", "dp"), None),
            P(None, "fsdp", None),
            P("fsdp", None),
            P(None, "fsdp"),
            P("fsdp"),
            P(None, None, "fsdp", None),
            P(None, "fsdp", None),
            P(None, None, "fsdp"),
            P(None, "fsdp"),
            P(None, "fsdp", None),
            P(None, "fsdp"),
            P(None, "fsdp", None),
            P(None, None, "fsdp"),
            P(None, "fsdp"),
            P(("fsdp", "dp"), None, None),
            P(("fsdp", "dp"), None, None),
        ),
        out_specs=(
            P(("fsdp", "dp"), None, None),
            P(("fsdp", "dp"), None, None),
            P(("fsdp", "dp"), None, None),
            P(("fsdp", "dp"), None, None),
            P(None, "fsdp", None),
            P("fsdp", None),
            P(None, "fsdp"),
            P("fsdp"),
            P(None, None, "fsdp", None),
            P(None, "fsdp", None),
            P(None, None, "fsdp"),
            P(None, "fsdp"),
            P(None, "fsdp", None),
            P(None, "fsdp"),
            P(None, "fsdp", None),
            P(None, None, "fsdp"),
            P(None, "fsdp"),
        ),
        check_vma=False,
    )
```

```python
import functools

import jax
import jax.numpy as jnp
from jax import lax
from jax.experimental import pallas as pl
from jax.experimental.pallas import tpu as pltpu
from jax.sharding import PartitionSpec as P

HEADS = 12
HEAD_DIM = 64
PAIR = 2 * HEAD_DIM
D = HEADS * HEAD_DIM
VECTORS = 32
BLOCK = 256

epsilon = 1e-06
hidden_score = -1e30

BF = jnp.bfloat16
F32 = jnp.float32


def rounded(values):
    return values.astype(BF)


def widened(values):
    return values.astype(F32)


def mm(left, right):
    return jnp.dot(left, right, preferred_element_type=F32)


def mm_nt(left, right):
    return lax.dot_general(left, right, (((1,), (1,)), ((), ())), preferred_element_type=F32)


def mm_tn(left, right):
    return lax.dot_general(left, right, (((0,), (0,)), ((), ())), preferred_element_type=F32)


def flat(block):
    return block.reshape(block.shape[0] * block.shape[1], block.shape[2])


def matrix(held, order, columns=slice(None)):
    rows = D // held.shape[0]
    return flat(held[:, order * rows : (order + 1) * rows, columns])


def column_sum(values):
    return jnp.sum(values, axis=0, keepdims=True)


def norm_forward(total, gain, shift):
    centre = total - jnp.mean(total, axis=-1, keepdims=True)
    spread = jnp.mean(centre * centre, axis=-1, keepdims=True)
    return centre * lax.rsqrt(spread + epsilon) * gain + shift


def norm_backward(total, gradient, gain):
    centre = total - jnp.mean(total, axis=-1, keepdims=True)
    spread = jnp.mean(centre * centre, axis=-1, keepdims=True)
    scale = lax.rsqrt(spread + epsilon)
    unit = centre * scale
    inner = gradient * gain
    mean_inner = jnp.mean(inner, axis=-1, keepdims=True)
    mean_product = jnp.mean(inner * unit, axis=-1, keepdims=True)
    back = scale * (inner - mean_inner - unit * mean_product)
    return back, column_sum(gradient * unit), column_sum(gradient)


def item_of(shape, axis, length):
    place = lax.broadcasted_iota(jnp.int32, shape, axis).astype(F32)
    return jnp.floor((place + 0.5) * (1.0 / length))


def score_bias(rows, row_length, keys, key_length, present):
    row_item = item_of((rows, keys), 0, row_length)
    key_item = item_of((rows, keys), 1, key_length) if present is None else present
    return jnp.where(row_item == key_item, 0.0, hidden_score)


def attend(query, key, value, context, query_rows, key_rows, bias):
    low = lax.broadcasted_iota(jnp.int32, (1, PAIR), 1) < HEAD_DIM

    def pair(number, carry):
        columns = pl.ds(pl.multiple_of(number * PAIR, PAIR), PAIR)
        queries = query[query_rows, columns] * HEAD_DIM ** (-0.5)
        keys = key[key_rows, columns]
        values = value[key_rows, columns]
        total = None
        for half in (low, ~low):
            scores = mm_nt(jnp.where(half, queries, 0), keys) + bias[...]
            shifted = jnp.exp(scores - jnp.max(scores, axis=-1, keepdims=True))
            weight = rounded(shifted / jnp.sum(shifted, axis=-1, keepdims=True))
            part = mm(weight, jnp.where(half, values, 0))
            total = part if total is None else total + part
        context[query_rows, columns] = rounded(total)
        return carry

    lax.fori_loop(0, HEADS // 2, pair, 0)


def attend_back(query, key, value, d_context, query_rows, key_rows, bias, d_query, d_key, d_value):
    low = lax.broadcasted_iota(jnp.int32, (1, PAIR), 1) < HEAD_DIM
    scale = HEAD_DIM ** (-0.5)

    def pair(number, carry):
        columns = pl.ds(pl.multiple_of(number * PAIR, PAIR), PAIR)
        queries = query[query_rows, columns] * scale
        keys = key[key_rows, columns]
        values = value[key_rows, columns]
        arriving = d_context[query_rows, columns]
        d_queries, d_keys, d_values = None, None, None
        for half in (low, ~low):
            own_queries = jnp.where(half, queries, 0)
            own_arriving = jnp.where(half, arriving, 0)
            scores = mm_nt(own_queries, keys) + bias[...]
            shifted = jnp.exp(scores - jnp.max(scores, axis=-1, keepdims=True))
            weight = shifted / jnp.sum(shifted, axis=-1, keepdims=True)
            d_weight = mm_nt(own_arriving, values)
            inner = jnp.sum(d_weight * weight, axis=-1, keepdims=True)
            d_scores = rounded(weight * (d_weight - inner))
            part_values = mm_tn(rounded(weight), own_arriving)
            part_queries = mm(d_scores, jnp.where(half, keys * scale, 0))
            part_keys = mm_tn(d_scores, own_queries)
            d_queries = part_queries if d_queries is None else d_queries + part_queries
            d_keys = part_keys if d_keys is None else d_keys + part_keys
            d_values = part_values if d_values is None else d_values + part_values
        d_query[query_rows, columns] = rounded(d_queries)
        d_key[key_rows, columns] = rounded(d_keys)
        d_value[key_rows, columns] = rounded(d_values)
        return carry

    lax.fori_loop(0, HEADS // 2, pair, 0)


def blocks():
    return [slice(start, start + BLOCK) for start in range(0, D, BLOCK)]


class Chunk:
    def __init__(self, plane):
        self.split = plane == 8
        self.owners = plane

    def load_start(self, me, sources, held, sems, half=None):
        copies = []
        if self.split:
            count = held.shape[1]
            low, high = pl.ds(0, count // 2), pl.ds(count // 2, count // 2)
            every = pl.ds(0, count)
            spans = [every] * 6 + [low] * 2 + [high] * 2
            for part, (place, span) in enumerate(zip((0, 1, 2, 3, 4, 5, 6, 7, 6, 7), spans)):
                source = sources[part]
                if half is not None:
                    if part > 5 and part // 2 - 3 != half:
                        continue
                    span = every
                    source = source if part > 5 else source.at[pl.ds(half * count, count)]
                copies.append(pltpu.make_async_copy(source, held.at[me ^ place, span], sems.at[part]))
        else:
            copies.append(pltpu.make_async_copy(sources[0], held, sems.at[0]))
        for copy in copies:
            copy.start()
        return copies

    def store(self, me, held, targets, sems):
        if not self.split:
            copy = pltpu.make_async_copy(held, targets[0], sems.at[0])
            copy.start()
            copy.wait()
            return

        def each(owner, action):
            place = me ^ owner
            for target, odd in zip(targets, (0, 1)):

                @pl.when(lax.rem(place, 2) == odd)
                def _():
                    action(pltpu.make_async_copy(held.at[owner], target.at[place // 2], sems.at[owner]))

        for owner in range(8):
            each(owner, lambda copy: copy.start())
        for owner in range(8):
            each(owner, lambda copy: copy.wait())

    def sources(self):
        return 10 if self.split else 1

    def held(self, rows):
        return pltpu.VMEM((self.owners, rows, D), BF)

    def targets(self, rows):
        if self.split:
            return [jax.ShapeDtypeStruct((4, rows, D), BF)] * 2
        return [jax.ShapeDtypeStruct((self.owners, rows, D), BF)]


def run(kernel, name, me, values, chunks, outs, targets, scratch, flops, vmem=60):
    in_specs = [pl.BlockSpec(memory_space=pltpu.SMEM)]
    in_specs += [pl.BlockSpec(memory_space=pltpu.VMEM)] * len(values)
    pieces = [piece for chunk in chunks for piece in chunk]
    in_specs += [pl.BlockSpec(memory_space=pl.ANY)] * len(pieces)
    out_specs = [pl.BlockSpec(memory_space=pltpu.VMEM)] * len(outs)
    out_specs += [pl.BlockSpec(memory_space=pl.ANY)] * len(targets)
    sizes = [leaf.size * leaf.dtype.itemsize for leaf in values + pieces + outs + targets]
    return pl.pallas_call(
        kernel,
        out_shape=outs + targets,
        in_specs=in_specs,
        out_specs=out_specs,
        scratch_shapes=scratch,
        compiler_params=pltpu.CompilerParams(vmem_limit_bytes=vmem * 1024 * 1024),
        cost_estimate=pl.CostEstimate(flops=0, bytes_accessed=1024, transcendentals=0),
        name=name,
    )(me, *values, *pieces)


def shift_matrix(owner, local):
    row = lax.broadcasted_iota(jnp.int32, (128, D), 0)
    column = lax.broadcasted_iota(jnp.int32, (128, D), 1)
    return jnp.where((column == row + owner * local) & (row < local), 1.0, 0.0).astype(BF)


def shape(*sizes, dtype=F32):
    return jax.ShapeDtypeStruct(sizes, dtype)


def cross_forward_kernel(words, regions, items, chunk, refs):
    refs = list(refs)
    me = refs.pop(0)[0]
    language, vision, present = refs[:3]
    refs = refs[3:]
    if not chunk.split:
        vectors_in, up_in = refs[:2]
        refs = refs[2:]
    sources = refs[: chunk.sources()]
    refs = refs[chunk.sources() :]
    language_a, vision_a, total, query, key, value, context, vectors, up_bias = refs[:9]
    held, rows_in, bias_l, bias_v, sems = refs[9:]
    copies = chunk.load_start(me, sources, held, sems)
    split = words * items
    every = split + regions * items
    own = (slice(0, split), slice(split, every))
    rows_in[own[0]] = language[...]
    rows_in[own[1]] = vision[...]
    bias_l[...] = score_bias(split, words, every - split, regions, present[...])
    bias_v[...] = score_bias(every - split, regions, split, words, None)
    for copy in copies:
        copy.wait()
    if chunk.split:
        local = D // 8
        first = 4 * local
        found = None
        for owner in range(8):
            part = mm(held[owner, first : first + VECTORS, :128], shift_matrix(owner, local))
            found = part if found is None else found + part
        vectors[...] = found
        for stream in range(2):
            for quarter in range(4):
                line = slice(first + 21 + stream, first + 22 + stream)
                wide = [widened(held[2 * quarter + side])[line, : D // 2] for side in range(2)]
                up_bias[4 * stream + quarter : 4 * stream + quarter + 1, :] = jnp.concatenate(wide, axis=1)
    else:
        vectors[...] = vectors_in[...]
        up_bias[...] = up_in[...]
    for columns in blocks():
        query[:, columns] = rounded(mm(rows_in[...], matrix(held, 0, columns)) + vectors[0:1, columns])
        key[:, columns] = rounded(mm(rows_in[...], matrix(held, 1, columns)))
        value[:, columns] = rounded(mm(rows_in[...], matrix(held, 2, columns)) + vectors[1:2, columns])
    attend(query, key, value, context, own[0], own[1], bias_l)
    attend(query, key, value, context, own[1], own[0], bias_v)
    for columns in blocks():
        branch = mm(context[...], matrix(held, 3, columns)) + vectors[2:3, columns]
        total[:, columns] = widened(rows_in[:, columns]) + branch
    for rows, target in zip(own, (language_a, vision_a)):
        target[...] = norm_forward(total[rows], vectors[4:5], vectors[3:4])


def self_forward_kernel(stream, length, chunk, refs):
    refs = list(refs)
    me = refs.pop(0)[0]
    inputs, vectors = refs[:2]
    refs = refs[2:]
    present = refs.pop(0) if stream else None
    sources = refs[: chunk.sources()]
    outputs, total, query, key, value, context = refs[chunk.sources() : chunk.sources() + 6]
    held, bias, sems = refs[chunk.sources() + 6 :]
    copies = chunk.load_start(me, sources, held, sems, stream)
    rows = inputs.shape[0]
    bias[...] = score_bias(rows, length, rows, length, present[...] if stream else None)
    first = 5 + 4 * stream
    low_inputs = rounded(inputs[...])
    for copy in copies:
        copy.wait()
    for columns in blocks():
        query[:, columns] = rounded(mm(low_inputs, matrix(held, 0, columns)) + vectors[first : first + 1, columns])
        key[:, columns] = rounded(mm(low_inputs, matrix(held, 1, columns)))
        value[:, columns] = rounded(mm(low_inputs, matrix(held, 2, columns)) + vectors[first + 1 : first + 2, columns])
    attend(query, key, value, context, slice(0, rows), slice(0, rows), bias)
    for columns in blocks():
        branch = mm(context[...], matrix(held, 3, columns)) + vectors[first + 2 : first + 3, columns]
        total[:, columns] = inputs[:, columns] + branch
    gain = 13 + stream
    outputs[...] = norm_forward(total[...], vectors[gain : gain + 1], vectors[first + 3 : first + 4])


def feed_kernel(stream, chunk, refs):
    refs = list(refs)
    me = refs.pop(0)[0]
    inputs, cotangent, vectors, up_bias = refs[:4]
    refs = refs[4:]
    present = refs.pop(0) if stream else None
    sources = refs[: chunk.sources()]
    refs = refs[chunk.sources() :]
    outputs, d_inputs, small, d_up_bias = refs[:4]
    refs = refs[4:]
    width = len(chunk.targets(1))
    targets = refs[:width]
    held, grad, slope, hidden, total, sems, out_sems = refs[width:]
    copies = chunk.load_start(me, sources, held, sems)
    owners = chunk.owners // 4
    local = D // chunk.owners
    line = 15 + 2 * stream
    gain = vectors[19 + stream : 20 + stream]
    low_inputs = rounded(inputs[...])
    for copy in copies:
        copy.wait()

    def up_matrix(quarter):
        return flat(held[:, pl.ds(pl.multiple_of(quarter * local, local), local), :])

    def down_matrix(quarter):
        return flat(held[pl.ds(quarter * owners, owners), 4 * local :, :])

    total[...] = inputs[...] + vectors[line : line + 1]

    def onward(quarter, carry):
        before = mm(low_inputs, up_matrix(quarter)) + up_bias[pl.ds(4 * stream + quarter, 1), :]
        spread = 0.5 * (1.0 + lax.erf(before * 0.5**0.5))
        slope[quarter] = spread + before * jnp.exp(-0.5 * before * before) * (0.5 / 3.141592653589793) ** 0.5
        hidden[quarter] = rounded(before * spread)
        total[...] += mm(hidden[quarter], down_matrix(quarter))
        return carry

    lax.fori_loop(0, 4, onward, 0)
    result = norm_forward(total[...], gain, vectors[line + 1 : line + 2])
    arriving = widened(cotangent[...])
    if stream:
        result = result * present[...]
        arriving = arriving * present[...]
    outputs[...] = rounded(result)
    back, d_gain, d_shift = norm_backward(total[...], arriving, gain)
    d_inputs[...] = back
    low_back = rounded(back)
    small[...] = jnp.zeros_like(small)
    small[0:1] = column_sum(widened(low_back))
    small[1:2] = d_shift
    small[2:3] = d_gain

    def backward(quarter, carry):
        d_hidden = mm_nt(low_back, down_matrix(quarter))
        d_before = rounded(d_hidden * slope[quarter])
        d_up_bias[pl.ds(quarter, 1), :] = column_sum(widened(d_before))
        rows = pl.ds(pl.multiple_of(quarter * local, local), local)
        found = rounded(mm_tn(low_inputs, d_before))
        grad[:, rows, :] = found.reshape(chunk.owners, local, D)
        found = rounded(mm_tn(hidden[quarter], low_back))
        grad[pl.ds(quarter * owners, owners), 4 * local :, :] = found.reshape(owners, 4 * local, D)
        d_inputs[...] += mm_nt(d_before, up_matrix(quarter))
        return carry

    lax.fori_loop(0, 4, backward, 0)
    chunk.store(me, grad, targets, out_sems)


def layer_back(low_inputs, total, context, held, gain, d_norm, d_inputs, grad, d_context, low_back):
    back, d_gain, d_shift = norm_backward(total, d_norm, gain)
    d_inputs[...] = back
    low_back[...] = rounded(back)
    for columns in blocks():
        put(grad, 3, columns, mm_tn(context[...], low_back[:, columns]))
    d_context[...] = rounded(mm_nt(low_back[...], matrix(held, 3)))
    return d_gain, d_shift, column_sum(widened(low_back[...]))


def put(grad, order, columns, values):
    rows = D // grad.shape[0]
    grad[:, order * rows : (order + 1) * rows, columns] = rounded(values).reshape(grad.shape[0], rows, values.shape[1])


def projections_back(low_inputs, held, grad, d_all, d_inputs):
    for order, gradient in enumerate(d_all):
        for columns in blocks():
            put(grad, order, columns, mm_tn(low_inputs, gradient[:, columns]))
        d_inputs[...] += mm_nt(gradient[...], matrix(held, order))


def self_backward_kernel(stream, length, chunk, refs):
    refs = list(refs)
    me = refs.pop(0)[0]
    d_outputs, inputs, total, query, key, value, context, vectors = refs[:8]
    refs = refs[8:]
    present = refs.pop(0) if stream else None
    sources = refs[: chunk.sources()]
    refs = refs[chunk.sources() :]
    d_inputs, small = refs[:2]
    width = len(chunk.targets(1))
    targets = refs[2 : 2 + width]
    held, grad, bias, d_context, low_back, d_query, d_key, d_value, sems, out_sems = refs[2 + width :]
    copies = chunk.load_start(me, sources, held, sems, stream)
    rows = inputs.shape[0]
    bias[...] = score_bias(rows, length, rows, length, present[...] if stream else None)
    low_inputs = rounded(inputs[...])
    for copy in copies:
        copy.wait()
    gain = vectors[13 + stream : 14 + stream]
    d_gain, d_shift, d_out = layer_back(low_inputs, total[...], context, held, gain, d_outputs[...], d_inputs, grad, d_context, low_back)
    every = slice(0, rows)
    attend_back(query, key, value, d_context, every, every, bias, d_query, d_key, d_value)
    projections_back(low_inputs, held, grad, (d_query, d_key, d_value), d_inputs)
    small[...] = jnp.zeros_like(small)
    lines = (column_sum(widened(d_query[...])), column_sum(widened(d_value[...])), d_out, d_shift, d_gain)
    for place, line in enumerate(lines):
        small[place : place + 1] = line
    chunk.store(me, grad, targets, out_sems)


def cross_backward_kernel(words, regions, items, chunk, refs):
    refs = list(refs)
    me = refs.pop(0)[0]
    d_language, d_vision, language, vision, total, query, key, value, context, vectors, present = refs[:11]
    smalls = refs[11:15]
    ups = refs[15:17]
    refs = refs[17:]
    sources = refs[: chunk.sources()]
    refs = refs[chunk.sources() :]
    language_gradient, vision_gradient = refs[:2]
    refs = refs[2:]
    if not chunk.split:
        small_out, up_out = refs[:2]
        refs = refs[2:]
    width = len(chunk.targets(1))
    targets = refs[:width]
    held, grad, rows_in, d_norm, d_inputs, lines, bias_l, bias_v = refs[width : width + 8]
    d_context, low_back, d_query, d_key, d_value, sems, out_sems = refs[width + 8 :]
    copies = chunk.load_start(me, sources, held, sems)
    split = words * items
    every = split + regions * items
    own = (slice(0, split), slice(split, every))
    rows_in[own[0]] = language[...]
    rows_in[own[1]] = vision[...]
    d_norm[own[0]] = d_language[...]
    d_norm[own[1]] = d_vision[...]
    bias_l[...] = score_bias(split, words, every - split, regions, present[...])
    bias_v[...] = score_bias(every - split, regions, split, words, None)
    for copy in copies:
        copy.wait()
    d_gain, d_shift, d_out = layer_back(
        rows_in, total[...], context, held, vectors[4:5], d_norm[...], d_inputs, grad, d_context, low_back
    )
    attend_back(query, key, value, d_context, own[0], own[1], bias_l, d_query, d_key, d_value)
    attend_back(query, key, value, d_context, own[1], own[0], bias_v, d_query, d_key, d_value)
    projections_back(rows_in[...], held, grad, (d_query, d_key, d_value), d_inputs)
    language_gradient[...] = d_inputs[own[0]]
    vision_gradient[...] = d_inputs[own[1]]
    lines[...] = jnp.zeros_like(lines)
    found = (column_sum(widened(d_query[...])), column_sum(widened(d_value[...])), d_out, d_shift, d_gain)
    for place, line in enumerate(found):
        lines[place : place + 1] = line
    self_l, self_v, feed_l, feed_v = smalls
    moves = [(self_l, place, 5 + place) for place in range(4)] + [(self_v, place, 9 + place) for place in range(4)]
    moves += [(self_l, 4, 13), (self_v, 4, 14), (feed_l, 0, 15), (feed_l, 1, 16), (feed_v, 0, 17), (feed_v, 1, 18)]
    moves += [(feed_l, 2, 19), (feed_v, 2, 20)]
    for source, place, target in moves:
        lines[target : target + 1] = source[place : place + 1]
    if chunk.split:
        local = D // 8
        first = 4 * local
        low_lines = rounded(lines[...])
        zeros = jnp.zeros((1, D // 2), F32)
        for owner in range(8):
            narrow = mm_nt(low_lines, shift_matrix(owner, local))
            block = jnp.concatenate([narrow, jnp.zeros((VECTORS, D - 128), F32)], axis=1)
            side = slice(owner % 2 * (D // 2), (owner % 2 + 1) * (D // 2))
            for stream in range(2):
                wide = ups[stream][owner // 2 : owner // 2 + 1, side]
                wide = jnp.concatenate([wide, zeros], axis=1)
                here = lax.broadcasted_iota(jnp.int32, (VECTORS, 1), 0) == 21 + stream
                block = jnp.where(here, wide, block)
            grad[owner, first : first + VECTORS, :] = rounded(block)
    else:
        small_out[...] = lines[...]
        up_out[0:4] = ups[0][0:4]
        up_out[4:8] = ups[1][0:4]
    chunk.store(me, grad, targets, out_sems)


def after(values, *others):
    return lax.optimization_barrier((values, *others))[0] if others else values


class Order:
    depths = {"x": 2, "y": 2, "core": 3, "one": 1, "two": 1, "three": 1}

    def __init__(self):
        self.kernel = []
        self.sent = {link: [] for link in self.depths}

    def ran(self, token, *beside):
        self.kernel = [token, *beside]

    def use(self, values):
        return after(values, *self.kernel)

    def send(self, link, values, axis, pairs, depth=None):
        sent, depth = self.sent[link], depth or self.depths[link]
        values = after(values, *self.kernel, *sent[max(len(sent) - depth, 0) : max(len(sent) - depth + 1, 0)])
        sent.append(lax.ppermute(values, axis, pairs))
        return sent[-1]

    def swap(self, link, values, depth=None):
        mask = {"core": 1, "x": 2, "y": 4}[link]
        return self.send(link, values, "fsdp", [(place, place ^ mask) for place in range(8)], depth)


def add_far_kernel(keep, got, near_x, near_y):
    for side, target in enumerate((near_x, near_y)):
        target[...] = rounded(widened(keep[0, side]) + widened(got[0, side]))


def add_near_kernel(keep_x, got_x, keep_y, got_y, from_x, from_y, to_x, to_y):
    to_x[0] = rounded(widened(keep_x[0, 0]) + widened(got_x[0, 0]))
    to_x[1] = rounded(widened(keep_x[0, 1]) + widened(got_x[0, 1]) + widened(from_y[...]))
    to_y[0] = rounded(widened(keep_y[0, 0]) + widened(got_y[0, 0]) + widened(from_x[...]))
    to_y[1] = rounded(widened(keep_y[0, 1]) + widened(got_y[0, 1]))


def add_own_kernel(keep, got, from_x, from_y, own):
    for side in range(2):
        own[side] = rounded(
            widened(keep[0, side]) + widened(got[0, side]) + widened(from_x[side]) + widened(from_y[side])
        )


def combine(kernel, places, keep, got, others, outs):
    half = keep.shape[2]
    step = half if half % 192 else 192

    def spec(values, place=0):
        if values.ndim == 4:
            return pl.BlockSpec((1, 2, step, D), lambda part: (place, 0, part, 0))
        if values.ndim == 3:
            return pl.BlockSpec((2, step, D), lambda part: (0, part, 0))
        return pl.BlockSpec((step, D), lambda part: (part, 0))

    values = [keep, got] * len(places) + others
    in_specs = [spec(values, place) for place in places for values in (keep, got)] + [spec(leaf) for leaf in others]
    sizes = [half * D * 4] * 2 * len(places) + [leaf.size * 2 for leaf in [*others, *outs]]
    return pl.pallas_call(
        kernel,
        grid=(half // step,),
        in_specs=in_specs,
        out_specs=[spec(leaf) for leaf in outs],
        out_shape=outs,
        compiler_params=pltpu.CompilerParams(vmem_limit_bytes=32 * 1024 * 1024),
        cost_estimate=pl.CostEstimate(flops=0, bytes_accessed=sum(sizes), transcendentals=0),
        name=kernel.__name__,
    )(*values)


class Gather:
    def __init__(self, order, shard):
        self.order, self.shard, self.half = order, shard, shard.shape[0] // 2

    def near(self):
        self.near_x = self.order.swap("x", self.shard, 1)
        self.near_y = self.order.swap("y", self.shard, 1)

    def far(self):
        self.far_x = self.order.swap("x", self.order.use(self.near_y)[: self.half])
        self.far_y = self.order.swap("y", self.order.use(self.near_x)[self.half :])

    def own_core(self):
        self.own = self.order.swap("core", self.shard)

    def near_core(self):
        self.cores = [self.order.swap("core", piece) for piece in (self.near_x, self.near_y)]

    def far_core(self):
        self.cores += [self.order.swap("core", piece) for piece in (self.far_x, self.far_y)]

    def pieces(self):
        pieces = [self.shard, self.own]
        for piece, core in zip((self.near_x, self.near_y, self.far_x, self.far_y), self.cores):
            pieces += [piece, core]
        return pieces


class Reduce:
    def __init__(self, order, keep, send):
        self.order, self.rows = order, keep.shape[1]
        self.half = self.rows // 2
        self.keep = keep.reshape(4, 2, self.half, D)
        self.got = order.swap("core", send).reshape(4, 2, self.half, D)

    def far(self):
        outs = [shape(self.half, D, dtype=BF)] * 2
        got = self.order.use(self.got)
        to_x, to_y = combine(add_far_kernel, (3,), self.keep, got, [], outs)
        self.from_x, self.from_y = self.order.swap("x", to_x), self.order.swap("y", to_y)

    def near(self):
        outs = [shape(2, self.half, D, dtype=BF)] * 2
        others = [self.order.use(self.from_x), self.order.use(self.from_y)]
        to_x, to_y = combine(add_near_kernel, (1, 2), self.keep, self.got, others, outs)
        self.from_x, self.from_y = self.order.swap("x", to_x), self.order.swap("y", to_y)

    def first(self):
        others = [self.order.use(self.from_x), self.order.use(self.from_y)]
        outs = [shape(2, self.half, D, dtype=BF)]
        self.own = combine(add_own_kernel, (0,), self.keep, self.got, others, outs)[0]
        self.one = self.order.send("one", self.own, "dp", [(0, 1), (3, 2)])

    def second(self):
        self.one = self.order.use(self.one)
        self.two = self.order.send("two", rounded(plus(self.own, self.one)), "dp", [(1, 2), (2, 1)])

    def third(self):
        self.two = self.order.use(self.two)
        self.three = self.order.send("three", rounded(plus(self.own, self.two)), "dp", [(1, 0), (2, 3)])

    def total(self):
        three = self.order.use(self.three)
        return plus(self.own, self.one, self.two, three).reshape(self.rows, D)


def plus(*values):
    total = widened(values[0])
    for value in values[1:]:
        total = total + widened(value)
    return total


def body(
    language,
    vision,
    region_mask,
    cross_qkv,
    cross_out,
    cross_bias,
    cross_gain,
    self_qkv,
    self_out,
    self_bias,
    self_gain,
    ffn_up,
    ffn_up_bias,
    ffn_down,
    ffn_bias,
    ffn_gain,
    language_cotangent,
    vision_cotangent,
):
    plane, line = lax.axis_size("fsdp"), lax.axis_size("dp")
    swaps = plane == 8 and line == 4
    chunk = Chunk(plane if swaps else 1)
    chunk.split = swaps
    chunk.owners = 8 if swaps else 4
    rank = lax.axis_index("fsdp")
    me = rank.astype(jnp.int32)[None]
    items, words, _ = language.shape
    regions = vision.shape[1]
    local = cross_gain.shape[0]

    small = jnp.concatenate(
        [cross_bias, cross_gain[None], self_bias.reshape(8, local), self_gain, ffn_bias.reshape(4, local), ffn_gain]
    )
    cross_shard = rounded(jnp.concatenate([cross_qkv.reshape(3 * local, D), cross_out]))
    self_shards = [rounded(jnp.concatenate([self_qkv[s].reshape(3 * local, D), self_out[s]])) for s in range(2)]
    up_shards = [rounded(ffn_up[s]).reshape(local, 4, D).transpose(1, 0, 2).reshape(4 * local, D) for s in range(2)]
    down_shards = [rounded(ffn_down[s]) for s in range(2)]
    if swaps:
        small = jnp.pad(small, ((0, 0), (0, D - local)))
        wide = jnp.pad(ffn_up_bias, ((0, VECTORS - 23), (0, D // 2)))
        cross_shard = jnp.concatenate([cross_shard, rounded(jnp.concatenate([small, wide]))])
        cross_rows, rows = 4 * local + VECTORS, 4 * local
        given = []
    else:

        def gather(shard):
            whole = lax.all_gather(shard.reshape(4, local, D), "fsdp", axis=1, tiled=True)
            return [whole.reshape(4, 4, D // 4, D).transpose(1, 0, 2, 3).reshape(4, D, D)]

        cross_rows = rows = D
        vectors = widened(lax.all_gather(rounded(small), "fsdp", axis=1, tiled=True))
        up_bias = widened(lax.all_gather(rounded(ffn_up_bias), "fsdp", axis=1, tiled=True)).reshape(8, D)
        given = [jnp.pad(vectors, ((0, VECTORS - 21), (0, 0))), up_bias]
    lengths = (words, regions)
    counts = (items * words, items * regions)
    every = sum(counts)
    rows_in = (language.reshape(counts[0], D), vision.reshape(counts[1], D))
    tangents = (language_cotangent.reshape(counts[0], D), vision_cotangent.reshape(counts[1], D))
    item = lax.broadcasted_iota(jnp.int32, (items, regions), 0)
    present = widened(jnp.where(region_mask > 0, item, -1)).reshape(1, counts[1])
    mask_rows = widened(region_mask).reshape(counts[1], 1)
    sems = pltpu.SemaphoreType.DMA((10,))
    weights = D * D

    outs = [shape(counts[0], D), shape(counts[1], D), shape(every, D)] + [shape(every, D, dtype=BF)] * 4
    outs += [shape(VECTORS, D), shape(8, D)]
    scratch = [chunk.held(cross_rows), pltpu.VMEM((every, D), BF)]
    biases = [pltpu.VMEM((counts[0], counts[1]), F32), pltpu.VMEM((counts[1], counts[0]), F32)]

    def cross_forward(pieces):
        return run(
            lambda *refs: cross_forward_kernel(words, regions, items, chunk, refs),
            "cross_forward",
            me,
            [*rows_in, present, *given],
            [pieces],
            [shape(counts[0], D), shape(counts[1], D), shape(every, D)]
            + [shape(every, D, dtype=BF)] * 4
            + [shape(VECTORS, D), shape(8, D)],
            [],
            [chunk.held(cross_rows), pltpu.VMEM((every, D), BF)] + biases + [sems],
            8 * every * weights,
        )

    def self_forward(stream, inputs, vectors, pieces):
        count = counts[stream]
        return run(
            lambda *refs: self_forward_kernel(stream, lengths[stream], chunk, refs),
            f"self_forward_{stream}",
            me,
            [inputs, vectors] + ([present] if stream else []),
            [pieces],
            [shape(count, D)] * 2 + [shape(count, D, dtype=BF)] * 4,
            [],
            [chunk.held(rows), pltpu.VMEM((count, count), F32), sems],
            8 * count * weights,
        )

    def feed(stream, inputs, vectors, up_bias, pieces):
        count = counts[stream]
        return run(
            lambda *refs: feed_kernel(stream, chunk, refs),
            f"feed_{stream}",
            me,
            [inputs, tangents[stream], vectors, up_bias] + ([mask_rows] if stream else []),
            [pieces],
            [shape(count, D, dtype=BF), shape(count, D), shape(8, D), shape(4, D)],
            chunk.targets(2 * rows),
            [chunk.held(2 * rows)] * 2
            + [pltpu.VMEM((4, count, D), F32), pltpu.VMEM((4, count, D), BF), pltpu.VMEM((count, D), F32)]
            + [sems] * 2,
            48 * count * weights,
        )

    def self_backward(stream, gradient, inputs, kept, vectors, pieces):
        count = counts[stream]
        return run(
            lambda *refs: self_backward_kernel(stream, lengths[stream], chunk, refs),
            f"self_backward_{stream}",
            me,
            [gradient, inputs, *kept, vectors] + ([present] if stream else []),
            [pieces],
            [shape(count, D), shape(8, D)],
            chunk.targets(rows),
            [chunk.held(rows)] * 2
            + [pltpu.VMEM((count, count), F32)]
            + [pltpu.VMEM((count, D), BF)] * 5
            + [sems] * 2,
            16 * count * weights,
        )

    def cross_backward(gradients, kept, vectors, smalls, pieces):
        return run(
            lambda *refs: cross_backward_kernel(words, regions, items, chunk, refs),
            "cross_backward",
            me,
            [*gradients, *rows_in, *kept, vectors, present, *smalls],
            [pieces],
            [shape(counts[0], D), shape(counts[1], D)] + ([] if swaps else [shape(VECTORS, D), shape(8, D)]),
            chunk.targets(cross_rows),
            [chunk.held(cross_rows)] * 2
            + [pltpu.VMEM((every, D), BF), pltpu.VMEM((every, D), F32), pltpu.VMEM((every, D), F32)]
            + [pltpu.VMEM((VECTORS, D), F32)]
            + biases
            + [pltpu.VMEM((every, D), BF)] * 5
            + [sems] * 2,
            16 * every * weights,
        )

    biases = [pltpu.VMEM((counts[0], counts[1]), F32), pltpu.VMEM((counts[1], counts[0]), F32)]
    feed_shards = [jnp.concatenate(shards) for shards in zip(up_shards, down_shards)]
    if swaps:
        order = Order()
        cross = Gather(order, cross_shard)
        own = Gather(order, jnp.concatenate(self_shards))
        feed_l, feed_v = [Gather(order, shard) for shard in feed_shards]
        cross.near()
        cross.own_core()
        cross.far()
        cross.near_core()
        cross.far_core()
        own.near()
        made = cross_forward(cross.pieces())
        first_a, cross_kept, (vectors, up_bias) = made[:2], made[2:7], made[7:]
        order.ran(up_bias, own.near_x, own.near_y)

        own.far()
        own.own_core()
        own.near_core()
        own.far_core()
        feed_l.near()
        second_l = self_forward(0, first_a[0], vectors, own.pieces())
        second_v = self_forward(1, after(first_a[1], second_l[0]), vectors, own.pieces())
        order.ran(second_v[0], feed_l.near_x, feed_l.near_y)

        feed_l.far()
        feed_l.own_core()
        feed_l.near_core()
        feed_l.far_core()
        feed_v.near()
        fed_l = feed(0, second_l[0], order.use(vectors), up_bias, feed_l.pieces())
        order.ran(fed_l[2], feed_v.near_x, feed_v.near_y)

        feed_v.far()
        feed_v.own_core()
        feed_v.near_core()
        sum_feed_l = Reduce(order, *fed_l[4:])
        back_l = self_backward(0, fed_l[1], first_a[0], second_l[1:], vectors, own.pieces())
        order.ran(back_l[1], feed_v.far_x, feed_v.far_y, sum_feed_l.got)

        sum_feed_l.far()
        feed_v.far_core()
        sum_self_l = Reduce(order, *back_l[2:])
        sum_self_l.far()
        fed_v = feed(1, second_v[0], order.use(vectors), up_bias, feed_v.pieces())
        order.ran(fed_v[2], sum_feed_l.from_x, sum_feed_l.from_y, sum_self_l.from_x, sum_self_l.from_y)

        sum_feed_l.near()
        sum_feed_v = Reduce(order, *fed_v[4:])
        back_v = self_backward(1, fed_v[1], first_a[1], second_v[1:], vectors, own.pieces())
        order.ran(back_v[1], sum_feed_l.from_x, sum_feed_l.from_y, sum_feed_v.got)

        sum_feed_v.far()
        sum_self_l.near()
        sum_self_v = Reduce(order, *back_v[2:])
        sum_feed_l.first()
        smalls = [back_l[1], back_v[1], fed_l[2], fed_v[2], fed_l[3], fed_v[3]]
        made = cross_backward([back_l[0], back_v[0]], cross_kept, vectors, smalls, cross.pieces())
        gradients = made[:2]
        order.ran(
            made[1], sum_feed_v.from_x, sum_feed_v.from_y, sum_self_l.from_x, sum_self_l.from_y, sum_feed_l.one
        )

        sum_self_v.far()
        sum_feed_v.near()
        sum_cross = Reduce(order, *made[2:])
        sum_feed_l.second()
        sum_self_l.first()
        sum_cross.far()
        sum_self_v.near()
        sum_feed_l.third()
        sum_self_l.second()
        sum_feed_v.first()
        sum_cross.near()
        sum_self_l.third()
        sum_feed_v.second()
        sum_self_v.first()
        sum_feed_v.third()
        sum_self_v.second()
        sum_cross.first()
        sum_self_v.third()
        sum_cross.second()
        sum_cross.third()
        feed_done = [sum_feed_l.total(), sum_feed_v.total()]
        self_done = [sum_self_l.total(), sum_self_v.total()]
        cross_done = sum_cross.total()
        up_done = [done[: 4 * local] for done in feed_done]
        down_done = [done[4 * local :] for done in feed_done]
        outputs = fed_l[0], fed_v[0]
        small = cross_done[4 * local : 4 * local + 21, :local]
        up_small = cross_done[4 * local + 21 : 4 * local + 23, : 4 * local]
    else:
        cross_pieces = gather(cross_shard)
        self_pieces = [gather(shard) for shard in self_shards]
        feed_pieces = []
        for up, down in zip(up_shards, down_shards):
            down = lax.all_gather(down, "fsdp", axis=0, tiled=True).reshape(4, D, D)
            feed_pieces.append([jnp.concatenate(gather(up) + [down], axis=1)])
        made = cross_forward(cross_pieces)
        first_a, cross_kept, (vectors, up_bias) = made[:2], made[2:7], made[7:]
        second = [self_forward(s, first_a[s], vectors, self_pieces[s]) for s in range(2)]
        fed = [feed(s, second[s][0], vectors, up_bias, feed_pieces[s]) for s in range(2)]
        back = [self_backward(s, fed[s][1], first_a[s], second[s][1:], vectors, self_pieces[s]) for s in range(2)]
        smalls = [back[0][1], back[1][1], fed[0][2], fed[1][2], fed[0][3], fed[1][3]]
        made = cross_backward([back[0][0], back[1][0]], cross_kept, vectors, smalls, cross_pieces)
        gradients = made[:2]
        outputs = fed[0][0], fed[1][0]

        def whole(grad, by_owner=True):
            if by_owner:
                grad = grad.reshape(4, 4, D // 4, D).transpose(1, 0, 2, 3).reshape(4, D, D)
                own = lax.psum_scatter(grad, "fsdp", scatter_dimension=1, tiled=True)
            else:
                own = lax.psum_scatter(grad.reshape(4 * D, D), "fsdp", scatter_dimension=0, tiled=True)
            return widened(lax.psum(own, "dp")).reshape(4 * local, D)

        up_done = [whole(made_s[4][:, :D]) for made_s in fed]
        down_done = [whole(made_s[4][:, D:], False) for made_s in fed]
        self_done = [whole(made_s[2]) for made_s in back]
        cross_done = whole(made[4])
        small = lax.dynamic_slice(lax.psum(made[2], ("fsdp", "dp")), (0, rank * local), (21, local))
        up_small = lax.psum(made[3], ("fsdp", "dp")).reshape(2, 4 * D)
        up_small = lax.dynamic_slice(up_small, (0, 4 * rank * local), (2, 4 * local))

    up_grads = [done.reshape(4, local, D).transpose(1, 0, 2).reshape(local, 4 * D) for done in up_done]
    return (
        outputs[0].reshape(language.shape),
        outputs[1].reshape(vision.shape),
        gradients[0].reshape(language.shape),
        gradients[1].reshape(vision.shape),
        cross_done[: 3 * local].reshape(3, local, D),
        cross_done[3 * local : 4 * local],
        small[0:4],
        small[4],
        jnp.stack([done[: 3 * local].reshape(3, local, D) for done in self_done]),
        jnp.stack([done[3 * local :] for done in self_done]),
        small[5:13].reshape(2, 4, local),
        small[13:15],
        jnp.stack(up_grads),
        up_small,
        jnp.stack(down_done),
        small[15:19].reshape(2, 2, local),
        small[19:21],
    )


def solution(mesh):
    return jax.shard_map(
        body,
        mesh=mesh,
        in_specs=(
            P(("fsdp", "dp"), None, None),
            P(("fsdp", "dp"), None, None),
            P(("fsdp", "dp"), None),
            P(None, "fsdp", None),
            P("fsdp", None),
            P(None, "fsdp"),
            P("fsdp"),
            P(None, None, "fsdp", None),
            P(None, "fsdp", None),
            P(None, None, "fsdp"),
            P(None, "fsdp"),
            P(None, "fsdp", None),
            P(None, "fsdp"),
            P(None, "fsdp", None),
            P(None, None, "fsdp"),
            P(None, "fsdp"),
            P(("fsdp", "dp"), None, None),
            P(("fsdp", "dp"), None, None),
        ),
        out_specs=(
            P(("fsdp", "dp"), None, None),
            P(("fsdp", "dp"), None, None),
            P(("fsdp", "dp"), None, None),
            P(("fsdp", "dp"), None, None),
            P(None, "fsdp", None),
            P("fsdp", None),
            P(None, "fsdp"),
            P("fsdp"),
            P(None, None, "fsdp", None),
            P(None, "fsdp", None),
            P(None, None, "fsdp"),
            P(None, "fsdp"),
            P(None, "fsdp", None),
            P(None, "fsdp"),
            P(None, "fsdp", None),
            P(None, None, "fsdp"),
            P(None, "fsdp"),
        ),
        check_vma=False,
    )
```

```python
import functools

import jax
import jax.numpy as jnp
from jax import lax
from jax.experimental import pallas as pl
from jax.experimental.pallas import tpu as pltpu
from jax.sharding import PartitionSpec as P

HEADS = 12
HEAD_DIM = 64
PAIR = 2 * HEAD_DIM
D = HEADS * HEAD_DIM
NARROW = 21
VECTORS = 32
BLOCK = 256
VMEM_MIB = dict(cross_forward=60, self_forward_0=60, self_forward_1=60, feed_0=60, feed_1=60)
VMEM_MIB.update(self_backward_0=60, self_backward_1=60, cross_backward=60)

epsilon = 1e-06
hidden_score = -1e30

BF = jnp.bfloat16
F32 = jnp.float32


def rounded(values):
    return values.astype(BF)


def widened(values):
    return values.astype(F32)


def shape(*sizes, dtype=F32):
    return jax.ShapeDtypeStruct(sizes, dtype)


def plus(*values):
    total = widened(values[0])
    for value in values[1:]:
        total = total + widened(value)
    return total


def mm(left, right):
    return jnp.dot(left, right, preferred_element_type=F32)


def mm_nt(left, right):
    return lax.dot_general(left, right, (((1,), (1,)), ((), ())), preferred_element_type=F32)


def mm_tn(left, right):
    return lax.dot_general(left, right, (((0,), (0,)), ((), ())), preferred_element_type=F32)


def flat(block):
    return block.reshape(block.shape[0] * block.shape[1], block.shape[2])


def column_sum(values):
    return jnp.sum(values, axis=0, keepdims=True)


def blocks():
    return [slice(start, start + BLOCK) for start in range(0, D, BLOCK)]


def norm_forward(total, gain, shift):
    centre = total - jnp.mean(total, axis=-1, keepdims=True)
    spread = jnp.mean(centre * centre, axis=-1, keepdims=True)
    return centre * lax.rsqrt(spread + epsilon) * gain + shift


def norm_backward(total, gradient, gain):
    centre = total - jnp.mean(total, axis=-1, keepdims=True)
    spread = jnp.mean(centre * centre, axis=-1, keepdims=True)
    scale = lax.rsqrt(spread + epsilon)
    unit = centre * scale
    inner = gradient * gain
    mean_inner = jnp.mean(inner, axis=-1, keepdims=True)
    mean_product = jnp.mean(inner * unit, axis=-1, keepdims=True)
    back = scale * (inner - mean_inner - unit * mean_product)
    return back, column_sum(gradient * unit), column_sum(gradient)


def place_of(extent, axis, items):
    number = lax.broadcasted_iota(jnp.int32, extent, axis).astype(F32)
    place = jnp.floor((number + 0.5) * (1.0 / items))
    return number - place * items, place


def present_item(extent, axis, counts):
    item, place = place_of(extent, axis, len(counts))
    limit = jnp.zeros_like(place)
    for number, count in enumerate(counts):
        limit = jnp.where(item == number, count.astype(F32), limit)
    return jnp.where(place < limit, item, -1.0)


def fill_bias(bias, items, counts=None):
    rows, keys = bias.shape
    key_item = place_of((1, keys), 1, items)[0] if counts is None else present_item((1, keys), 1, counts)
    bias[...] = jnp.where(place_of((rows, 1), 0, items)[0] == key_item, 0.0, hidden_score)


def attend(query, key, value, context, query_rows, key_rows, bias, kept):
    low = lax.broadcasted_iota(jnp.int32, (1, PAIR), 1) < HEAD_DIM
    for number in range(HEADS // 2):
        columns = slice(number * PAIR, (number + 1) * PAIR)
        rows, others = query_rows, key_rows
        queries = query[rows, columns] * HEAD_DIM ** (-0.5)
        keys = key[others, columns]
        values = value[others, columns]
        total = None
        for side, half in enumerate((low, ~low)):
            scores = mm_nt(jnp.where(half, queries, 0), keys) + bias[...]
            shifted = jnp.exp(scores - jnp.max(scores, axis=-1, keepdims=True))
            weight = rounded(shifted / jnp.sum(shifted, axis=-1, keepdims=True))
            kept[2 * number + side] = weight
            found = mm(weight, jnp.where(half, values, 0))
            total = found if total is None else total + found
        context[rows, columns] = rounded(total)


def attend_back(query, key, value, kept, d_context, query_rows, key_rows, d_query, d_key, d_value):
    low = lax.broadcasted_iota(jnp.int32, (1, PAIR), 1) < HEAD_DIM
    scale = HEAD_DIM ** (-0.5)
    for number in range(HEADS // 2):
        columns = slice(number * PAIR, (number + 1) * PAIR)
        rows, others = query_rows, key_rows
        queries = query[rows, columns] * scale
        keys = key[others, columns]
        values = value[others, columns]
        arriving = d_context[rows, columns]
        sums = [None] * 3
        for side, half in enumerate((low, ~low)):
            own_arriving = jnp.where(half, arriving, 0)
            weight = kept[2 * number + side]
            d_weight = mm_nt(own_arriving, values)
            weighed = d_weight * weight
            inner = jnp.sum(weighed, axis=-1, keepdims=True)
            d_scores = rounded(weighed - weight * inner)
            found = [
                mm(d_scores, jnp.where(half, keys * scale, 0)),
                mm_tn(d_scores, jnp.where(half, queries, 0)),
                mm_tn(weight, own_arriving),
            ]
            sums = [one if total is None else total + one for one, total in zip(found, sums)]
        d_query[rows, columns] = rounded(sums[0])
        d_key[others, columns] = rounded(sums[1])
        d_value[others, columns] = rounded(sums[2])


def shift_matrix(owner, local):
    row = lax.broadcasted_iota(jnp.int32, (128, D), 0)
    column = lax.broadcasted_iota(jnp.int32, (128, D), 1)
    return jnp.where((column == row + owner * local) & (row < local), 1.0, 0.0).astype(BF)


class Chunk:
    def __init__(self, owners, split_in, split_out, rows, spans, base=0, middle=None, cut=None):
        self.owners, self.split_in, self.split_out, self.rows, self.spans = owners, split_in, split_out, rows, spans
        self.base, self.middle, self.cut = base, middle, cut
        self.sources = (8 if middle is None else 10) if split_in else 1
        sizes = [rows] if cut is None else [cut, rows - cut]
        self.targets = [shape(owners, rows, D, dtype=BF)]
        if split_out:
            self.targets = [shape(4, size, D, dtype=BF) for size in sizes for _ in range(2)]
        self.held = pltpu.VMEM((owners, rows, D), BF)
        self.sems = pltpu.SemaphoreType.DMA((len(spans), owners))

    def load(self, me, sources, held, sems, order):
        copies = {}
        for number in order:
            start, size = self.spans[number]
            span = pl.ds(start, size)
            copies[number] = []
            for place in range(8 if self.split_in else 1):
                sem = sems.at[number, place]
                if not self.split_in:
                    copies[number].append(pltpu.make_async_copy(sources[0].at[:, span], held.at[:, span], sem))
                    continue
                pieces = [(start, size)]
                if place > 5 and self.middle is not None and start < self.middle < start + size:
                    pieces = [(start, self.middle - start), (self.middle, start + size - self.middle)]
                for first, count in pieces:
                    if place < 6:
                        source = sources[place].at[pl.ds(self.base + first, count)]
                    elif self.middle is None:
                        source = sources[place].at[pl.ds(first, count)]
                    else:
                        above = first >= self.middle
                        source = sources[place + 2 * above].at[pl.ds(first - self.middle * above, count)]
                    copies[number].append(pltpu.make_async_copy(source, held.at[me ^ place, pl.ds(first, count)], sem))
            for copy in copies[number]:
                copy.start()

        def wait(number):
            for copy in copies[number]:
                copy.wait()

        return wait

    def copy_out(self, me, grad, targets, sem, owner, span, action):
        if not self.split_out:
            span = pl.ds(*span)
            action(pltpu.make_async_copy(grad.at[owner, span], targets[0].at[owner, span], sem))
            return
        place = me ^ owner
        first, size = span
        second = self.cut is not None and first >= self.cut
        there = pl.ds(first - (self.cut if second else 0), size)
        span = pl.ds(first, size)
        for target, odd in zip(targets[2:] if second else targets, (0, 1)):

            @pl.when(lax.rem(place, 2) == odd)
            def _():
                action(pltpu.make_async_copy(grad.at[owner, span], target.at[place // 2, there], sem))

    def store(self, me, grad, targets, sems, number, owners=None):
        span = self.spans[number]
        owners = range(self.owners) if owners is None else owners
        for owner in owners:
            self.copy_out(me, grad, targets, sems.at[number, owner], owner, span, lambda copy: copy.start())

        def wait():
            for owner in owners:
                self.copy_out(me, grad, targets, sems.at[number, owner], owner, span, lambda copy: copy.wait())

        return wait

    def matrix(self, held, number, columns=slice(None)):
        start, size = self.spans[number]
        return flat(held[:, start : start + size, columns])

    def put(self, grad, number, columns, values):
        start, size = self.spans[number]
        grad[:, start : start + size, columns] = rounded(values).reshape(self.owners, size, values.shape[1])


def run(kernel, name, numbers, values, pieces, outs, targets, scratch):
    in_specs = [pl.BlockSpec(memory_space=pltpu.SMEM)]
    in_specs += [pl.BlockSpec(memory_space=pltpu.VMEM)] * len(values)
    in_specs += [pl.BlockSpec(memory_space=pl.ANY)] * len(pieces)
    out_specs = [pl.BlockSpec(memory_space=pltpu.VMEM)] * len(outs)
    out_specs += [pl.BlockSpec(memory_space=pl.ANY)] * len(targets)
    return pl.pallas_call(
        kernel,
        out_shape=outs + targets,
        in_specs=in_specs,
        out_specs=out_specs,
        scratch_shapes=scratch,
        compiler_params=pltpu.CompilerParams(vmem_limit_bytes=VMEM_MIB[name] * 1024 * 1024),
        cost_estimate=pl.CostEstimate(flops=0, bytes_accessed=1024, transcendentals=0),
        name=name,
    )(numbers, *values, *pieces)


class Refs:
    def __init__(self, refs):
        self.refs = list(refs)

    def take(self, count):
        taken, self.refs = self.refs[:count], self.refs[count:]
        return taken


def cross_forward_kernel(chunk, given, *refs):
    refs = Refs(refs)
    numbers, language, vision = refs.take(3)
    given = refs.take(given)
    sources = refs.take(chunk.sources)
    language_a, vision_a, rows_in, total, query, key, value, context, kept_l, kept_v, vectors, up_bias = refs.take(12)
    held, bias_l, bias_v, sems = refs.take(4)
    me = numbers[0]
    wait = chunk.load(me, sources, held, sems, [*range(4, len(chunk.spans)), *range(4)])
    split, every = language.shape[0], rows_in.shape[0]
    own = (slice(0, split), slice(split, every))
    rows_in[own[0]] = language[...]
    rows_in[own[1]] = vision[...]
    counts = [numbers[item] for item in range(1, numbers.shape[0])]
    fill_bias(bias_l, len(counts), counts)
    fill_bias(bias_v, len(counts))
    if chunk.split_in:
        local = D // 8
        wait(4)
        extra = slice(chunk.spans[4][0], chunk.rows)
        found = None
        for owner in range(8):
            moved = mm(held[owner, extra, :128], shift_matrix(owner, local))
            found = moved if found is None else found + moved
        vectors[...] = found
        for quarter in range(4):
            wide = [widened(held[2 * quarter + side, extra, : D // 2]) for side in range(2)]
            wide = jnp.concatenate(wide, axis=1)
            for stream in range(2):
                line = NARROW + stream
                up_bias[4 * stream + quarter : 4 * stream + quarter + 1, :] = wide[line : line + 1]
    else:
        vectors[...] = given[0][...]
        up_bias[...] = given[1][...]
    for number, target in enumerate((query, key, value)):
        wait(number)
        for columns in blocks():
            found = mm(rows_in[...], chunk.matrix(held, number, columns))
            if number != 1:
                line = number // 2
                found = found + vectors[line : line + 1, columns]
            target[:, columns] = rounded(found)
    attend(query, key, value, context, own[0], own[1], bias_l, kept_l)
    attend(query, key, value, context, own[1], own[0], bias_v, kept_v)
    wait(3)
    for columns in blocks():
        branch = mm(context[...], chunk.matrix(held, 3, columns)) + vectors[2:3, columns]
        total[:, columns] = widened(rows_in[:, columns]) + branch
    for rows, target in zip(own, (language_a, vision_a)):
        target[...] = norm_forward(total[rows], vectors[4:5], vectors[3:4])


def self_forward_kernel(stream, chunk, *refs):
    refs = Refs(refs)
    numbers, inputs, vectors = refs.take(3)
    sources = refs.take(chunk.sources)
    outputs, total, query, key, value, context, kept = refs.take(7)
    held, bias, sems = refs.take(3)
    wait = chunk.load(numbers[0], sources, held, sems, range(4))
    rows = inputs.shape[0]
    counts = [numbers[item] for item in range(1, numbers.shape[0])]
    fill_bias(bias, len(counts), counts if stream else None)
    first = 5 + 4 * stream
    low_inputs = rounded(inputs[...])
    for number, target in enumerate((query, key, value)):
        wait(number)
        for columns in blocks():
            found = mm(low_inputs, chunk.matrix(held, number, columns))
            if number != 1:
                line = first + number // 2
                found = found + vectors[line : line + 1, columns]
            target[:, columns] = rounded(found)
    every = slice(0, rows)
    attend(query, key, value, context, every, every, bias, kept)
    wait(3)
    for columns in blocks():
        branch = mm(context[...], chunk.matrix(held, 3, columns)) + vectors[first + 2 : first + 3, columns]
        total[:, columns] = inputs[:, columns] + branch
    gain = 13 + stream
    outputs[...] = norm_forward(total[...], vectors[gain : gain + 1], vectors[first + 3 : first + 4])


def feed_kernel(stream, chunk, *refs):
    refs = Refs(refs)
    numbers, inputs, cotangent, vectors, up_bias = refs.take(5)
    sources = refs.take(chunk.sources)
    outputs, d_inputs, small, d_up_bias = refs.take(4)
    targets = refs.take(len(chunk.targets))
    held, grad, slope, hidden, total, sems, out_sems = refs.take(7)
    me = numbers[0]
    wait = chunk.load(me, sources, held, sems, (0, 4, 1, 2, 3))
    owners = chunk.owners // 4
    local = D // chunk.owners
    line = 15 + 2 * stream
    gain = vectors[19 + stream : 20 + stream]
    low_inputs = rounded(inputs[...])

    def down_matrix(quarter):
        return flat(held[quarter * owners : (quarter + 1) * owners, 4 * local :, :])

    total[...] = inputs[...] + vectors[line : line + 1]
    for quarter in range(4):
        wait(quarter)
        for columns in blocks():
            before = mm(low_inputs, chunk.matrix(held, quarter, columns))
            before = before + up_bias[4 * stream + quarter : 4 * stream + quarter + 1, columns]
            spread = 0.5 * (1.0 + lax.erf(before * 0.5**0.5))
            slope[quarter, :, columns] = spread + before * jnp.exp(-0.5 * before * before) * (0.5 / 3.141592653589793) ** 0.5
            hidden[quarter, :, columns] = rounded(before * spread)
        if quarter == 0:
            wait(4)
        total[...] += mm(hidden[quarter], down_matrix(quarter))
    arriving = widened(cotangent[...])
    found = norm_forward(total[...], gain, vectors[line + 1 : line + 2])
    if stream:
        counts = [numbers[item] for item in range(1, numbers.shape[0])]
        mask = jnp.where(present_item((inputs.shape[0], 1), 0, counts) < 0, 0.0, 1.0)
        found = found * mask
        arriving = arriving * mask
    back, d_gain, d_shift = norm_backward(total[...], arriving, gain)
    outputs[...] = rounded(found)
    d_inputs[...] = back
    low_back = rounded(back)
    small[...] = jnp.zeros_like(small)
    small[0:1] = column_sum(widened(low_back))
    small[1:2] = d_shift
    small[2:3] = d_gain
    pending = []
    for quarter in range(4):
        d_hidden = mm_nt(low_back, down_matrix(quarter))
        d_before = rounded(d_hidden * slope[quarter])
        d_up_bias[quarter : quarter + 1, :] = column_sum(widened(d_before))
        for columns in blocks():
            found = rounded(mm_tn(hidden[quarter], low_back[:, columns]))
            grad[quarter * owners : (quarter + 1) * owners, 4 * local :, columns] = found.reshape(owners, 4 * local, BLOCK)
        pending.append(chunk.store(me, grad, targets, out_sems, 4, range(quarter * owners, (quarter + 1) * owners)))
        for columns in blocks():
            chunk.put(grad, quarter, columns, mm_tn(low_inputs, d_before[:, columns]))
        pending.append(chunk.store(me, grad, targets, out_sems, quarter))
        d_inputs[...] += mm_nt(d_before, chunk.matrix(held, quarter))
    for finish in pending:
        finish()


def layer_back(chunk, total, context, held, gain, d_norm, d_inputs, grad, d_context, low_back, wait):
    back, d_gain, d_shift = norm_backward(total, d_norm, gain)
    d_inputs[...] = back
    low_back[...] = rounded(back)
    wait(3)
    d_context[...] = rounded(mm_nt(low_back[...], chunk.matrix(held, 3)))
    for columns in blocks():
        chunk.put(grad, 3, columns, mm_tn(context[...], low_back[:, columns]))
    return d_gain, d_shift, column_sum(widened(low_back[...]))


def projections_back(chunk, low_inputs, held, grad, d_all, d_inputs, wait, store):
    pending = []
    for number, gradient in enumerate(d_all):
        for columns in blocks():
            chunk.put(grad, number, columns, mm_tn(low_inputs, gradient[:, columns]))
        pending.append(store(number))
    for number, gradient in enumerate(d_all):
        wait(number)
        d_inputs[...] += mm_nt(gradient[...], chunk.matrix(held, number))
    return pending


def self_backward_kernel(stream, chunk, *refs):
    refs = Refs(refs)
    numbers, d_outputs, inputs, total, query, key, value, context, kept, vectors = refs.take(10)
    sources = refs.take(chunk.sources)
    d_inputs, small = refs.take(2)
    targets = refs.take(len(chunk.targets))
    held, grad, d_context, low_back, d_query, d_key, d_value, sems, out_sems = refs.take(9)
    me = numbers[0]
    wait = chunk.load(me, sources, held, sems, (3, 0, 1, 2))
    store = functools.partial(chunk.store, me, grad, targets, out_sems)
    rows = inputs.shape[0]
    low_inputs = rounded(inputs[...])
    gain = vectors[13 + stream : 14 + stream]
    d_gain, d_shift, d_out = layer_back(
        chunk, total[...], context, held, gain, d_outputs[...], d_inputs, grad, d_context, low_back, wait
    )
    pending = [store(3)]
    every = slice(0, rows)
    attend_back(query, key, value, kept, d_context, every, every, d_query, d_key, d_value)
    pending += projections_back(chunk, low_inputs, held, grad, (d_query, d_key, d_value), d_inputs, wait, store)
    small[...] = jnp.zeros_like(small)
    lines = (column_sum(widened(d_query[...])), column_sum(widened(d_value[...])), d_out, d_shift, d_gain)
    for place, line in enumerate(lines):
        small[place : place + 1] = line
    for finish in pending:
        finish()


def cross_backward_kernel(chunk, *refs):
    refs = Refs(refs)
    numbers, d_language, d_vision, rows_in, total, query, key, value, context, kept_l, kept_v, vectors = refs.take(12)
    self_l, self_v, feed_l, feed_v = refs.take(4)
    ups = refs.take(2)
    sources = refs.take(chunk.sources)
    language_gradient, vision_gradient = refs.take(2)
    if not chunk.split_out:
        small_out, up_out = refs.take(2)
    targets = refs.take(len(chunk.targets))
    held, grad, d_norm, d_inputs, lines = refs.take(5)
    d_context, low_back, d_query, d_key, d_value, sems, out_sems = refs.take(7)
    me = numbers[0]
    wait = chunk.load(me, sources, held, sems, (3, 0, 1, 2))
    store = functools.partial(chunk.store, me, grad, targets, out_sems)
    split, every = language_gradient.shape[0], rows_in.shape[0]
    own = (slice(0, split), slice(split, every))
    d_norm[own[0]] = d_language[...]
    d_norm[own[1]] = d_vision[...]
    d_gain, d_shift, d_out = layer_back(
        chunk, total[...], context, held, vectors[4:5], d_norm[...], d_inputs, grad, d_context, low_back, wait
    )
    pending = [store(3)]
    attend_back(query, key, value, kept_l, d_context, own[0], own[1], d_query, d_key, d_value)
    attend_back(query, key, value, kept_v, d_context, own[1], own[0], d_query, d_key, d_value)
    found = (column_sum(widened(d_query[...])), column_sum(widened(d_value[...])), d_out, d_shift, d_gain)
    lines[...] = jnp.zeros_like(lines)
    for place, line in enumerate(found):
        lines[place : place + 1] = line
    moves = [(self_l, place, 5 + place) for place in range(4)] + [(self_v, place, 9 + place) for place in range(4)]
    moves += [(self_l, 4, 13), (self_v, 4, 14), (feed_l, 0, 15), (feed_l, 1, 16), (feed_v, 0, 17), (feed_v, 1, 18)]
    moves += [(feed_l, 2, 19), (feed_v, 2, 20)]
    for source, place, target in moves:
        lines[target : target + 1] = source[place : place + 1]
    if chunk.split_out:
        local = D // 8
        low_lines = rounded(lines[...])
        zeros = jnp.zeros((1, D // 2), F32)
        for owner in range(8):
            narrow = mm_nt(low_lines, shift_matrix(owner, local))
            block = jnp.concatenate([narrow, jnp.zeros((VECTORS, D - 128), F32)], axis=1)
            side = slice(owner % 2 * (D // 2), (owner % 2 + 1) * (D // 2))
            for stream in range(2):
                wide = ups[stream][owner // 2 : owner // 2 + 1, side]
                wide = jnp.concatenate([wide, zeros], axis=1)
                here = lax.broadcasted_iota(jnp.int32, (VECTORS, 1), 0) == NARROW + stream
                block = jnp.where(here, wide, block)
            grad[owner, chunk.spans[4][0] : chunk.rows, :] = rounded(block)
        pending += [store(4)]
    else:
        small_out[...] = lines[...]
        up_out[0:4] = ups[0][0:4]
        up_out[4:8] = ups[1][0:4]
    pending += projections_back(chunk, rows_in[...], held, grad, (d_query, d_key, d_value), d_inputs, wait, store)
    language_gradient[...] = d_inputs[own[0]]
    vision_gradient[...] = d_inputs[own[1]]
    for finish in pending:
        finish()


def finish_feed_kernel(*refs):
    refs = Refs(refs)
    terms_l, up_v, down_v = refs.take(4), refs.take(4), refs.take(4)
    up_grad, down_grad = refs.take(2)
    local = up_grad.shape[1]
    for quarter in range(4):
        rows, columns = slice(quarter * local, (quarter + 1) * local), slice(quarter * D, (quarter + 1) * D)
        up_grad[0, :, columns] = plus(*[term[rows] for term in terms_l])
        up_grad[1, :, columns] = plus(*[term[rows] for term in up_v])
    down_grad[0] = plus(*[term[4 * local :] for term in terms_l])
    down_grad[1] = plus(*[term[...] for term in down_v])


def finish_rest_kernel(*refs):
    refs = Refs(refs)
    terms_l = refs.take(4)
    sides = [refs.take(4) for _ in range(2)]
    self_qkv, self_out, qkv, out, bias, gain, self_bias, self_gain, up_bias, feed_bias, feed_gain = refs.take(11)
    local = out.shape[0]
    found = [plus(*[term[...] for term in terms]) for terms in sides]
    for stream in range(2):
        for number in range(4):
            target = self_out.at[stream] if number == 3 else self_qkv.at[stream, number]
            if stream:
                target[...] = found[number // 2][number % 2 * local : (number % 2 + 1) * local]
            else:
                target[...] = plus(*[term[number * local : (number + 1) * local] for term in terms_l])
    start = 2 * local
    for number in range(2):
        qkv[number] = found[0][start + number * local : start + (number + 1) * local]
    above = VECTORS // 2
    qkv[2, :above] = found[0][start + 2 * local :]
    qkv[2, above:] = found[1][start : start + local - above]
    out[...] = found[1][start + local - above : start + 2 * local - above]
    small = found[1][start + 2 * local - above :]
    bias[...] = small[0:4, :local]
    gain[...] = small[4:5, :local]
    for stream in range(2):
        self_bias[stream] = small[5 + 4 * stream : 9 + 4 * stream, :local]
        self_gain[stream : stream + 1] = small[13 + stream : 14 + stream, :local]
        feed_bias[stream] = small[15 + 2 * stream : 17 + 2 * stream, :local]
        feed_gain[stream : stream + 1] = small[19 + stream : 20 + stream, :local]
        up_bias[stream : stream + 1] = small[NARROW + stream : NARROW + stream + 1, : 4 * local]


def pack_cross_kernel(qkv, out, bias, gain, self_bias, self_gain, feed_bias, feed_gain, up_bias, shard, extra):
    local = out.shape[0]
    extra[...] = jnp.zeros_like(extra)
    extra[0:4, :local] = bias[...]
    extra[4:5, :local] = gain[...]
    for stream in range(2):
        extra[5 + 4 * stream : 9 + 4 * stream, :local] = self_bias[stream]
        extra[13 + stream : 14 + stream, :local] = self_gain[stream : stream + 1]
        extra[15 + 2 * stream : 17 + 2 * stream, :local] = feed_bias[stream]
        extra[19 + stream : 20 + stream, :local] = feed_gain[stream : stream + 1]
        extra[NARROW + stream : NARROW + stream + 1, : 4 * local] = up_bias[stream : stream + 1]
    for number in range(3):
        shard[number * local : (number + 1) * local] = rounded(qkv[number])
    shard[3 * local : 4 * local] = rounded(out[...])
    shard[4 * local :] = rounded(extra[...])


def pack_rest_kernel(token, qkv, out, up, down, own, feed_l, feed_v):
    local = out.shape[1]
    for stream, feed in enumerate((feed_l, feed_v)):
        for number in range(3):
            own[(4 * stream + number) * local : (4 * stream + number + 1) * local] = rounded(qkv[stream, number])
        own[(4 * stream + 3) * local : (4 * stream + 4) * local] = rounded(out[stream])
        for quarter in range(4):
            feed[quarter * local : (quarter + 1) * local] = rounded(up[stream, :, quarter * D : (quarter + 1) * D])
        feed[4 * local :] = rounded(down[stream])


def in_vmem(kernel, values, outs, scratch=()):
    return pl.pallas_call(
        kernel,
        out_shape=outs,
        in_specs=[pl.BlockSpec(memory_space=pltpu.VMEM)] * len(values),
        out_specs=[pl.BlockSpec(memory_space=pltpu.VMEM)] * len(outs),
        scratch_shapes=scratch,
        compiler_params=pltpu.CompilerParams(vmem_limit_bytes=60 * 1024 * 1024),
        cost_estimate=pl.CostEstimate(flops=0, bytes_accessed=1024, transcendentals=0),
        name=kernel.__name__,
    )(*values)


def finish(kernel, chunks, outs):
    return in_vmem(kernel, [term for chunk in chunks for term in chunk], outs)


def after(values, *others):
    return lax.optimization_barrier((values, *others))[0] if others else values


class Order:
    depths = {"x": 2, "y": 2, "core": 3, "one": 9, "two": 9, "three": 9}

    def __init__(self):
        self.kernel, self.last = [], []
        self.sent = {link: [] for link in self.depths}

    def ran(self, token, *beside):
        self.kernel, self.last = [token, *beside], []

    def use(self, values):
        return after(values, *self.kernel, *self.last)

    def settle(self, *values):
        self.last = [*self.last, *values]

    def did(self, values):
        self.last = [values]
        return values

    def send(self, link, values, axis, pairs, depth=None):
        sent, depth = self.sent[link], depth or self.depths[link]
        values = after(values, *self.kernel, *sent[max(len(sent) - depth, 0) : max(len(sent) - depth + 1, 0)])
        sent.append(lax.ppermute(values, axis, pairs))
        return sent[-1]

    def swap(self, link, values, depth=None):
        mask = {"core": 1, "x": 2, "y": 4}[link]
        return self.send(link, values, "fsdp", [(place, place ^ mask) for place in range(8)], depth)


def add_far_kernel(count, *refs):
    refs = Refs(refs)
    terms = [refs.take(2) for _ in range(count)]
    targets = refs.take(2)
    first = 0
    for keep, got in terms:
        rows = slice(first, first + keep.shape[2])
        first = rows.stop
        for side, target in enumerate(targets):
            target[rows] = rounded(plus(keep[0, side], got[0, side]))


def add_near_kernel(count, *refs):
    refs = Refs(refs)
    terms_x = [refs.take(2) for _ in range(count)]
    terms_y = [refs.take(2) for _ in range(count)]
    from_x, from_y, *targets = refs.refs
    joined = len(targets) == 2
    for number, (terms, side_more, more) in enumerate(((terms_x, 1, from_y), (terms_y, 0, from_x))):
        first = 0
        for keep, got in terms:
            rows = slice(first, first + keep.shape[2])
            first = rows.stop
            for side in range(2):
                extra = [more[rows]] if side == side_more else []
                target = targets[number].at[side] if joined else targets[2 * number + side].at[0]
                target[rows] = rounded(plus(keep[0, side], got[0, side], *extra))


def add_own_kernel(count, *refs):
    refs = Refs(refs)
    terms = [refs.take(2) for _ in range(count)]
    from_x, from_y = refs.take(2)
    first = 0
    for keep, got in terms:
        rows = slice(first, first + keep.shape[2])
        first = rows.stop
        for side in range(keep.shape[1]):
            target = refs.refs[0].at[side] if len(refs.refs) == 1 else refs.refs[side].at[0]
            target[rows] = rounded(plus(keep[0, side], got[0, side], from_x[side, rows], from_y[side, rows]))


def combine(kernel, places, keeps, gots, others, outs, side=None):
    half = keeps[0].shape[2]
    steps = half // 96 if half % 96 == 0 and len(keeps) == 1 else 1

    def spec(values, place=0):
        *more, rows, _ = values.shape
        if len(more) == 2:
            if side is not None:
                return pl.BlockSpec((1, 1, rows // steps, D), lambda block: (place, side, block, 0))
            return pl.BlockSpec((1, 2, rows // steps, D), lambda block: (place, 0, block, 0))
        return pl.BlockSpec((*more, rows // steps, D), lambda block: (*[0] * len(more), block, 0))

    terms = [term for keep, got in zip(keeps, gots) for term in (keep, got)]
    return pl.pallas_call(
        functools.partial(kernel, len(keeps)),
        grid=(steps,),
        in_specs=[spec(term, place) for place in places for term in terms] + [spec(leaf) for leaf in others],
        out_specs=[spec(leaf) for leaf in outs],
        out_shape=outs,
        compiler_params=pltpu.CompilerParams(vmem_limit_bytes=60 * 1024 * 1024),
        cost_estimate=pl.CostEstimate(flops=0, bytes_accessed=1024, transcendentals=0),
        name=kernel.__name__,
    )(*terms * len(places), *others)


class Gather:
    def __init__(self, order, shard, fars):
        self.order, self.shard, self.fars = order, shard, fars
        self.far_parts, self.far_cores = {}, {}

    def near(self, depth=1):
        self.near_x = self.order.swap("x", self.shard, depth)
        self.near_y = self.order.swap("y", self.shard, depth)

    def far(self, number=0):
        first, middle, last = self.fars[number]
        to_x = self.order.did(self.order.use(self.near_y)[first:middle])
        to_y = self.order.did(self.order.use(self.near_x)[middle:last])
        self.far_parts[number] = [self.order.swap("x", to_x), self.order.swap("y", to_y)]

    def own_core(self):
        self.own = self.order.swap("core", self.shard)

    def near_core(self):
        self.cores = [self.order.swap("core", piece) for piece in (self.near_x, self.near_y)]

    def far_core(self, number=0):
        self.far_cores[number] = [self.order.swap("core", piece) for piece in self.far_parts[number]]

    def pieces(self, number=0, sides=(0, 1)):
        pieces = [self.shard, self.own]
        for piece, core in zip((self.near_x, self.near_y), self.cores):
            pieces += [piece, core]
        for side in sides:
            pieces += [self.far_parts[number][side], self.far_cores[number][side]]
        return pieces


class Line:
    def __init__(self, order):
        self.order = order

    def line(self, own):
        self.own = own
        self.order.did(own[0])
        self.one, self.two, self.three = [[None] * len(own) for _ in range(3)]

    def first(self):
        self.one = [self.order.send("one", own, "dp", [(0, 1), (3, 2)]) for own in self.own]

    def second(self, number=0):
        own = self.order.did(rounded(plus(self.own[number], self.order.use(self.one[number]))))
        self.two[number] = self.order.send("two", own, "dp", [(1, 2), (2, 1)])

    def third(self, number=0):
        own = self.order.did(rounded(plus(self.own[number], self.order.use(self.two[number]))))
        self.three[number] = self.order.send("three", own, "dp", [(1, 0), (2, 3)])

    def terms(self, number=0):
        terms = self.own[number], self.one[number], self.two[number], self.three[number]
        return [term.reshape(-1, D) for term in terms]


class Reduce(Line):
    def __init__(self, order, keep, send):
        super().__init__(order)
        self.half = keep.shape[1] // 2
        self.keeps = [keep.reshape(4, 2, self.half, D)]
        self.gots = [order.swap("core", send).reshape(4, 2, self.half, D)]

    def join(self, other):
        self.half += other.half
        self.keeps += other.keeps
        self.gots += other.gots

    def far(self):
        outs = [shape(self.half, D, dtype=BF)] * 2
        gots = [self.order.use(got) for got in self.gots]
        to_x, to_y = combine(add_far_kernel, (3,), self.keeps, gots, [], outs)
        self.order.did(to_x)
        self.from_x, self.from_y = self.order.swap("x", to_x), self.order.swap("y", to_y)

    def near(self, parts=1):
        outs = [shape(2 // parts, self.half, D, dtype=BF)] * (2 * parts)
        others = [self.order.use(self.from_x), self.from_y]
        made = combine(add_near_kernel, (1, 2), self.keeps, self.gots, others, outs)
        self.order.did(made[0])
        arrived = [[], []]
        for part in range(parts):
            for number, link in enumerate("xy"):
                arrived[number].append(self.order.swap(link, made[parts * number + part]))
        self.from_x, self.from_y = arrived

    def plane(self, parts):
        others = [self.order.use(self.from_x[0]), self.from_y[0]]
        outs = [shape(2 // parts, self.half, D, dtype=BF)] * parts
        self.line(combine(add_own_kernel, (0,), self.keeps, self.gots, others, outs))

    def plane_side(self, side):
        if side == 0:
            self.own, self.one, self.two, self.three = [[None] * 2 for _ in range(4)]
        others = [self.order.use(self.from_x[side]), self.from_y[side]]
        outs = [shape(1, self.half, D, dtype=BF)]
        self.own[side] = combine(add_own_kernel, (0,), self.keeps, self.gots, others, outs, side)[0]
        self.order.did(self.own[side])
        self.one[side] = self.order.send("one", self.own[side], "dp", [(0, 1), (3, 2)])


def body(
    language,
    vision,
    region_mask,
    cross_qkv,
    cross_out,
    cross_bias,
    cross_gain,
    self_qkv,
    self_out,
    self_bias,
    self_gain,
    ffn_up,
    ffn_up_bias,
    ffn_down,
    ffn_bias,
    ffn_gain,
    language_cotangent,
    vision_cotangent,
):
    plane, line = lax.axis_size("fsdp"), lax.axis_size("dp")
    swaps = plane == 8 and line == 4
    rank = lax.axis_index("fsdp")
    items, words, _ = language.shape
    regions = vision.shape[1]
    local = cross_gain.shape[0]
    counts = (items * words, items * regions)
    every = sum(counts)
    by_place = lambda values: values.transpose(1, 0, 2).reshape(-1, D)
    by_item = lambda values: values.reshape(-1, items, D).transpose(1, 0, 2)
    tangents = (by_place(language_cotangent), by_place(vision_cotangent))
    numbers = jnp.concatenate([rank.astype(jnp.int32)[None], jnp.sum(region_mask, axis=1)])

    if swaps:
        leaves = [cross_qkv, cross_out, cross_bias, cross_gain[None], self_bias, self_gain, ffn_bias, ffn_gain, ffn_up_bias]
        scratch = [pltpu.VMEM((VECTORS, D), F32)]
        cross_shard = in_vmem(pack_cross_kernel, leaves, [shape(4 * local + VECTORS, D, dtype=BF)], scratch)[0]
        rest = [self_qkv, self_out, ffn_up, ffn_down]
        token = lax.slice(cross_shard, (4 * local, 0), (4 * local + 16, 128))
        own_shard, *feed_shards = in_vmem(pack_rest_kernel, [token, *rest], [shape(8 * local, D, dtype=BF)] * 3)
        rows = 4 * local
        spans = [(place * local, local) for place in range(4)]
        cross_chunk = Chunk(8, True, True, rows + VECTORS, spans + [(rows, VECTORS)], 0, 2 * local)
        self_chunks = [Chunk(8, True, True, rows, spans, stream * rows) for stream in range(2)]
        feed_chunks = [Chunk(8, True, out, 2 * rows, spans + [(rows, rows)], 0, rows) for out in (False, True)]
        given = []
    else:
        small = jnp.concatenate(
            [cross_bias, cross_gain[None], self_bias.reshape(8, local), self_gain, ffn_bias.reshape(4, local), ffn_gain]
        )
        self_shards = [rounded(jnp.concatenate([self_qkv[s].reshape(3 * local, D), self_out[s]])) for s in range(2)]
        up_shards = [rounded(ffn_up[s]).reshape(local, 4, D).transpose(1, 0, 2).reshape(4 * local, D) for s in range(2)]
        down_shards = [rounded(ffn_down[s]) for s in range(2)]

        def gather(shard):
            whole = lax.all_gather(shard.reshape(4, local, D), "fsdp", axis=1, tiled=True)
            return whole.reshape(4, 4, D // 4, D).transpose(1, 0, 2, 3).reshape(4, D, D)

        cross_shard = rounded(jnp.concatenate([cross_qkv.reshape(3 * local, D), cross_out]))
        spans = [(place * D // 4, D // 4) for place in range(4)]
        cross_chunk = Chunk(4, False, False, D, spans)
        self_chunks = [Chunk(4, False, False, D, spans)] * 2
        feed_chunks = [Chunk(4, False, False, 2 * D, spans + [(D, D)])] * 2
        vectors = widened(lax.all_gather(rounded(small), "fsdp", axis=1, tiled=True))
        up_bias = widened(lax.all_gather(rounded(ffn_up_bias), "fsdp", axis=1, tiled=True)).reshape(8, D)
        given = [jnp.pad(vectors, ((0, VECTORS - NARROW), (0, 0))), up_bias]

    def biases(rows, keys):
        return pltpu.VMEM((rows, keys), F32)

    def kept(rows, keys):
        return shape(HEADS, rows, keys, dtype=BF)

    both = [biases(counts[0], counts[1]), biases(counts[1], counts[0])]

    def cross_forward(pieces):
        return run(
            functools.partial(cross_forward_kernel, cross_chunk, len(given)),
            "cross_forward",
            numbers,
            [by_place(language), by_place(vision), *given],
            pieces,
            [shape(counts[0], D), shape(counts[1], D), shape(every, D, dtype=BF), shape(every, D)]
            + [shape(every, D, dtype=BF)] * 4
            + [kept(counts[0], counts[1]), kept(counts[1], counts[0])]
            + [shape(VECTORS, D), shape(8, D)],
            [],
            [cross_chunk.held] + both + [cross_chunk.sems],
        )

    def self_forward(stream, inputs, vectors, pieces):
        count, chunk = counts[stream], self_chunks[stream]
        return run(
            functools.partial(self_forward_kernel, stream, chunk),
            f"self_forward_{stream}",
            numbers,
            [inputs, vectors],
            pieces,
            [shape(count, D)] * 2 + [shape(count, D, dtype=BF)] * 4 + [kept(count, count)],
            [],
            [chunk.held, biases(count, count), chunk.sems],
        )

    def feed(stream, inputs, vectors, up_bias, pieces):
        count, chunk = counts[stream], feed_chunks[stream]
        return run(
            functools.partial(feed_kernel, stream, chunk),
            f"feed_{stream}",
            numbers,
            [inputs, tangents[stream], vectors, up_bias],
            pieces,
            [shape(count, D, dtype=BF), shape(count, D), shape(8, D), shape(4, D)],
            chunk.targets,
            [chunk.held] * 2
            + [pltpu.VMEM((4, count, D), F32), pltpu.VMEM((4, count, D), BF)]
            + [pltpu.VMEM((count, D), F32)]
            + [chunk.sems] * 2,
        )

    def self_backward(stream, gradient, inputs, self_kept, vectors, pieces):
        count, chunk = counts[stream], self_chunks[stream]
        return run(
            functools.partial(self_backward_kernel, stream, chunk),
            f"self_backward_{stream}",
            numbers,
            [gradient, inputs, *self_kept, vectors],
            pieces,
            [shape(count, D), shape(8, D)],
            chunk.targets,
            [chunk.held] * 2 + [pltpu.VMEM((count, D), BF)] * 5 + [chunk.sems] * 2,
        )

    def cross_backward(gradients, cross_kept, vectors, smalls, pieces):
        chunk = cross_chunk
        return run(
            functools.partial(cross_backward_kernel, chunk),
            "cross_backward",
            numbers,
            [*gradients, *cross_kept, vectors, *smalls],
            pieces,
            [shape(counts[0], D), shape(counts[1], D)] + ([] if swaps else [shape(VECTORS, D), shape(8, D)]),
            chunk.targets,
            [chunk.held] * 2
            + [pltpu.VMEM((every, D), F32)] * 2
            + [pltpu.VMEM((VECTORS, D), F32)]
            + [pltpu.VMEM((every, D), BF)] * 5
            + [chunk.sems] * 2,
        )

    if swaps:
        order = Order()
        cross = Gather(order, cross_shard, [(0, 2 * local, rows + VECTORS)])
        own = Gather(order, own_shard, [(0, rows, 2 * rows)])
        feed_l, feed_v = [Gather(order, shard, [(0, rows, 2 * rows)]) for shard in feed_shards]
        cross.near()
        cross.own_core()
        order.did(own_shard)
        cross.far()
        own.near()
        cross.near_core()
        cross.far_core()
        made = cross_forward(cross.pieces())
        first_a, cross_kept, (vectors, up_bias) = made[:2], made[2:10], made[10:]
        order.ran(up_bias, own.near_x, own.near_y)

        own.far()
        own.own_core()
        own.near_core()
        feed_l.near()
        own.far_core()
        second_l = self_forward(0, first_a[0], order.use(vectors), own.pieces(0, (0,)))
        second_v = self_forward(1, after(first_a[1], second_l[0]), vectors, own.pieces(0, (1,)))
        order.ran(second_v[0], feed_l.near_x, feed_l.near_y)

        feed_l.far()
        feed_l.own_core()
        feed_l.near_core()
        feed_v.near()
        feed_l.far_core()
        fed_l = feed(0, second_l[0], order.use(vectors), up_bias, feed_l.pieces())
        order.ran(fed_l[2], feed_v.near_x, feed_v.near_y)

        feed_v.far()
        summed_l = lax.psum_scatter(fed_l[4], "fsdp", scatter_dimension=0)
        feed_v.own_core()
        feed_v.near_core()
        back_l = self_backward(0, fed_l[1], first_a[0], second_l[1:], order.use(vectors), own.pieces(0, (0,)))
        order.ran(back_l[1], *feed_v.far_parts[0], feed_v.own, *feed_v.cores)

        feed_v.far_core()
        sum_self_l = Reduce(order, *back_l[2:])
        fed_v = feed(1, second_v[0], order.use(vectors), up_bias, feed_v.pieces())
        order.ran(fed_v[2], *sum_self_l.gots)

        sum_self_l.far()
        sum_feed_v = Reduce(order, *fed_v[4:])
        back_v = self_backward(1, fed_v[1], first_a[1], second_v[1:], order.use(vectors), own.pieces(0, (1,)))
        order.ran(back_v[1], sum_self_l.from_x, sum_self_l.from_y, *sum_feed_v.gots)

        sum_feed_v.far()
        sum_self_l.near()
        sum_last = Reduce(order, *back_v[2:])
        smalls = [back_l[1], back_v[1], fed_l[2], fed_v[2], fed_l[3], fed_v[3]]
        made = cross_backward([back_l[0], back_v[0]], cross_kept, order.use(vectors), smalls, cross.pieces())
        gradients = made[:2]
        order.ran(
            made[1], sum_feed_v.from_x, sum_feed_v.from_y, *sum_self_l.from_x, *sum_self_l.from_y, *sum_last.gots
        )

        sum_last.join(Reduce(order, *made[2:]))
        sum_feed_v.near()
        sum_self_l.plane(1)
        sum_self_l.first()
        sum_last.far()
        sum_feed_l = Line(order)
        sum_feed_l.line([order.use(summed_l)])
        sum_feed_l.first()
        sum_self_l.second()
        sum_feed_v.plane(2)
        sum_feed_v.first()
        sum_last.near(2)
        sum_self_l.third()
        sum_feed_l.second()
        sum_feed_v.second(0)
        order.settle(*sum_self_l.three)
        sum_feed_l.third()
        sum_last.plane_side(0)
        sum_feed_v.second(1)
        sum_last.plane_side(1)
        sum_feed_v.third(0)
        sum_last.second(0)
        order.settle(*sum_feed_l.three)
        sum_feed_v.third(1)
        sum_last.second(1)
        order.settle(sum_feed_v.three[0])
        sum_last.third(0)
        order.settle(sum_feed_v.three[1])
        sum_last.third(1)
        feed_terms = [sum_feed_l.terms()] + [sum_feed_v.terms(number) for number in range(2)]
        feed_terms[0][0] = order.use(feed_terms[0][0])
        feed_grads = finish(finish_feed_kernel, feed_terms, [shape(*ffn_up.shape), shape(*ffn_down.shape)])
        leaves = [self_qkv, self_out, cross_qkv, cross_out, cross_bias, cross_gain[None], self_bias, self_gain]
        leaves += [ffn_up_bias, ffn_bias, ffn_gain]
        last_terms = [sum_self_l.terms()] + [sum_last.terms(number) for number in range(2)]
        last_terms[0][0] = after(last_terms[0][0], feed_grads[0])
        rest = finish(finish_rest_kernel, last_terms, [shape(*leaf.shape) for leaf in leaves])
        grads = [*rest[2:5], rest[5][0], *rest[:2], *rest[6:8], feed_grads[0], rest[8], feed_grads[1], *rest[9:]]
        outputs = fed_l[0], fed_v[0]
    else:
        cross_pieces = [gather(cross_shard)]
        self_pieces = [[gather(shard)] for shard in self_shards]
        feed_pieces = []
        for up, down in zip(up_shards, down_shards):
            down = lax.all_gather(down, "fsdp", axis=0, tiled=True).reshape(4, D, D)
            feed_pieces.append([jnp.concatenate([gather(up), down], axis=1)])
        made = cross_forward(cross_pieces)
        first_a, cross_kept, (vectors, up_bias) = made[:2], made[2:10], made[10:]
        second = [self_forward(s, first_a[s], vectors, self_pieces[s]) for s in range(2)]
        fed = [feed(s, second[s][0], vectors, up_bias, feed_pieces[s]) for s in range(2)]
        back = [self_backward(s, fed[s][1], first_a[s], second[s][1:], vectors, self_pieces[s]) for s in range(2)]
        smalls = [back[0][1], back[1][1], fed[0][2], fed[1][2], fed[0][3], fed[1][3]]
        made = cross_backward([back[0][0], back[1][0]], cross_kept, vectors, smalls, cross_pieces)
        gradients = made[:2]
        outputs = fed[0][0], fed[1][0]

        def whole(grad, by_owner=True):
            if by_owner:
                grad = grad.reshape(4, 4, D // 4, D).transpose(1, 0, 2, 3).reshape(4, D, D)
                own = lax.psum_scatter(grad, "fsdp", scatter_dimension=1, tiled=True)
            else:
                own = lax.psum_scatter(grad.reshape(4 * D, D), "fsdp", scatter_dimension=0, tiled=True)
            return widened(lax.psum(own, "dp")).reshape(4 * local, D)

        up_done = [whole(made_s[4][:, :D]) for made_s in fed]
        down_done = [whole(made_s[4][:, D:], False) for made_s in fed]
        self_done = [whole(made_s[2]) for made_s in back]
        cross_done = whole(made[4])
        small = lax.dynamic_slice(lax.psum(made[2], ("fsdp", "dp")), (0, rank * local), (NARROW, local))
        up_small = lax.psum(made[3], ("fsdp", "dp")).reshape(2, 4 * D)
        up_small = lax.dynamic_slice(up_small, (0, 4 * rank * local), (2, 4 * local))
        up_grads = [done.reshape(4, local, D).transpose(1, 0, 2).reshape(local, 4 * D) for done in up_done]
        grads = [cross_done[: 3 * local].reshape(3, local, D), cross_done[3 * local :], small[0:4], small[4]]
        grads += [jnp.stack([done[: 3 * local].reshape(3, local, D) for done in self_done])]
        grads += [jnp.stack([done[3 * local :] for done in self_done])]
        grads += [small[5:13].reshape(2, 4, local), small[13:15], jnp.stack(up_grads), up_small, jnp.stack(down_done)]
        grads += [small[15:19].reshape(2, 2, local), small[19:21]]

    return (*[by_item(rows) for rows in (*outputs, *gradients)], *grads)


def solution(mesh):
    return jax.shard_map(
        body,
        mesh=mesh,
        in_specs=(
            P(("fsdp", "dp"), None, None),
            P(("fsdp", "dp"), None, None),
            P(("fsdp", "dp"), None),
            P(None, "fsdp", None),
            P("fsdp", None),
            P(None, "fsdp"),
            P("fsdp"),
            P(None, None, "fsdp", None),
            P(None, "fsdp", None),
            P(None, None, "fsdp"),
            P(None, "fsdp"),
            P(None, "fsdp", None),
            P(None, "fsdp"),
            P(None, "fsdp", None),
            P(None, None, "fsdp"),
            P(None, "fsdp"),
            P(("fsdp", "dp"), None, None),
            P(("fsdp", "dp"), None, None),
        ),
        out_specs=(
            P(("fsdp", "dp"), None, None),
            P(("fsdp", "dp"), None, None),
            P(("fsdp", "dp"), None, None),
            P(("fsdp", "dp"), None, None),
            P(None, "fsdp", None),
            P("fsdp", None),
            P(None, "fsdp"),
            P("fsdp"),
            P(None, None, "fsdp", None),
            P(None, "fsdp", None),
            P(None, None, "fsdp"),
            P(None, "fsdp"),
            P(None, "fsdp", None),
            P(None, "fsdp"),
            P(None, "fsdp", None),
            P(None, None, "fsdp"),
            P(None, "fsdp"),
        ),
        check_vma=False,
    )
```

```python
import functools

import jax
import jax.numpy as jnp
from jax import lax
from jax.experimental import pallas as pl
from jax.experimental.pallas import tpu as pltpu
from jax.sharding import PartitionSpec as P

HEADS = 12
HEAD_DIM = 64
PAIR = 2 * HEAD_DIM
D = HEADS * HEAD_DIM
NARROW = 21
VECTORS = 32
BLOCK = 256
VMEM_MIB = dict(cross_forward=60, self_forward_0=60, self_forward_1=60, feed_0=60, feed_1=60)
VMEM_MIB.update(self_backward_0=60, self_backward_1=60, cross_backward=60)

epsilon = 1e-06
hidden_score = -1e30

BF = jnp.bfloat16
F32 = jnp.float32


def rounded(values):
    return values.astype(BF)


def widened(values):
    return values.astype(F32)


def shape(*sizes, dtype=F32):
    return jax.ShapeDtypeStruct(sizes, dtype)


def plus(*values):
    total = widened(values[0])
    for value in values[1:]:
        total = total + widened(value)
    return total


def mm(left, right):
    return jnp.dot(left, right, preferred_element_type=F32)


def mm_nt(left, right):
    return lax.dot_general(left, right, (((1,), (1,)), ((), ())), preferred_element_type=F32)


def mm_tn(left, right):
    return lax.dot_general(left, right, (((0,), (0,)), ((), ())), preferred_element_type=F32)


def flat(block):
    return block.reshape(block.shape[0] * block.shape[1], block.shape[2])


def column_sum(values):
    return jnp.sum(values, axis=0, keepdims=True)


def blocks():
    return [slice(start, start + BLOCK) for start in range(0, D, BLOCK)]


def norm_forward(total, gain, shift):
    centre = total - jnp.mean(total, axis=-1, keepdims=True)
    spread = jnp.mean(centre * centre, axis=-1, keepdims=True)
    return centre * lax.rsqrt(spread + epsilon) * gain + shift


def norm_backward(total, gradient, gain):
    centre = total - jnp.mean(total, axis=-1, keepdims=True)
    spread = jnp.mean(centre * centre, axis=-1, keepdims=True)
    scale = lax.rsqrt(spread + epsilon)
    unit = centre * scale
    inner = gradient * gain
    mean_inner = jnp.mean(inner, axis=-1, keepdims=True)
    mean_product = jnp.mean(inner * unit, axis=-1, keepdims=True)
    back = scale * (inner - mean_inner - unit * mean_product)
    return back, column_sum(gradient * unit), column_sum(gradient)


def place_of(extent, axis, items):
    number = lax.broadcasted_iota(jnp.int32, extent, axis).astype(F32)
    place = jnp.floor((number + 0.5) * (1.0 / items))
    return number - place * items, place


def present_item(extent, axis, counts):
    item, place = place_of(extent, axis, len(counts))
    limit = jnp.zeros_like(place)
    for number, count in enumerate(counts):
        limit = jnp.where(item == number, count.astype(F32), limit)
    return jnp.where(place < limit, item, -1.0)


def fill_bias(bias, items, counts=None):
    rows, keys = bias.shape
    key_item = place_of((1, keys), 1, items)[0] if counts is None else present_item((1, keys), 1, counts)
    bias[...] = jnp.where(place_of((rows, 1), 0, items)[0] == key_item, 0.0, hidden_score)


def attend(query, key, value, context, query_rows, key_rows, bias, kept):
    low = lax.broadcasted_iota(jnp.int32, (1, PAIR), 1) < HEAD_DIM
    for number in range(HEADS // 2):
        columns = slice(number * PAIR, (number + 1) * PAIR)
        rows, others = query_rows, key_rows
        queries = query[rows, columns] * HEAD_DIM ** (-0.5)
        keys = key[others, columns]
        values = value[others, columns]
        total = None
        for side, half in enumerate((low, ~low)):
            scores = mm_nt(jnp.where(half, queries, 0), keys) + bias[...]
            shifted = jnp.exp(scores - jnp.max(scores, axis=-1, keepdims=True))
            weight = rounded(shifted / jnp.sum(shifted, axis=-1, keepdims=True))
            kept[2 * number + side] = weight
            found = mm(weight, jnp.where(half, values, 0))
            total = found if total is None else total + found
        context[rows, columns] = rounded(total)


def attend_back(query, key, value, kept, d_context, query_rows, key_rows, d_query, d_key, d_value):
    low = lax.broadcasted_iota(jnp.int32, (1, PAIR), 1) < HEAD_DIM
    scale = HEAD_DIM ** (-0.5)
    for number in range(HEADS // 2):
        columns = slice(number * PAIR, (number + 1) * PAIR)
        rows, others = query_rows, key_rows
        queries = query[rows, columns] * scale
        keys = key[others, columns]
        values = value[others, columns]
        arriving = d_context[rows, columns]
        sums = [None] * 3
        for side, half in enumerate((low, ~low)):
            own_arriving = jnp.where(half, arriving, 0)
            weight = kept[2 * number + side]
            d_weight = mm_nt(own_arriving, values)
            weighed = d_weight * weight
            inner = jnp.sum(weighed, axis=-1, keepdims=True)
            d_scores = rounded(weighed - weight * inner)
            found = [
                mm(d_scores, jnp.where(half, keys * scale, 0)),
                mm_tn(d_scores, jnp.where(half, queries, 0)),
                mm_tn(weight, own_arriving),
            ]
            sums = [one if total is None else total + one for one, total in zip(found, sums)]
        d_query[rows, columns] = rounded(sums[0])
        d_key[others, columns] = rounded(sums[1])
        d_value[others, columns] = rounded(sums[2])


def shift_matrix(owner, local):
    row = lax.broadcasted_iota(jnp.int32, (128, D), 0)
    column = lax.broadcasted_iota(jnp.int32, (128, D), 1)
    return jnp.where((column == row + owner * local) & (row < local), 1.0, 0.0).astype(BF)


class Chunk:
    def __init__(self, owners, split_in, split_out, rows, spans, base=0, middle=None, cut=None):
        self.owners, self.split_in, self.split_out, self.rows, self.spans = owners, split_in, split_out, rows, spans
        self.base, self.middle, self.cut = base, middle, cut
        self.sources = (8 if middle is None else 10) if split_in else 1
        sizes = [rows] if cut is None else [cut, rows - cut]
        self.targets = [shape(owners, rows, D, dtype=BF)]
        if split_out:
            self.targets = [shape(4, size, D, dtype=BF) for size in sizes for _ in range(2)]
        self.held = pltpu.VMEM((owners, rows, D), BF)
        self.sems = pltpu.SemaphoreType.DMA((len(spans), owners))

    def load(self, me, sources, held, sems, order):
        copies = {}
        for number in order:
            start, size = self.spans[number]
            span = pl.ds(start, size)
            copies[number] = []
            for place in range(8 if self.split_in else 1):
                sem = sems.at[number, place]
                if not self.split_in:
                    copies[number].append(pltpu.make_async_copy(sources[0].at[:, span], held.at[:, span], sem))
                    continue
                pieces = [(start, size)]
                if place > 5 and self.middle is not None and start < self.middle < start + size:
                    pieces = [(start, self.middle - start), (self.middle, start + size - self.middle)]
                for first, count in pieces:
                    if place < 6:
                        source = sources[place].at[pl.ds(self.base + first, count)]
                    elif self.middle is None:
                        source = sources[place].at[pl.ds(first, count)]
                    else:
                        above = first >= self.middle
                        source = sources[place + 2 * above].at[pl.ds(first - self.middle * above, count)]
                    copies[number].append(pltpu.make_async_copy(source, held.at[me ^ place, pl.ds(first, count)], sem))
            for copy in copies[number]:
                copy.start()

        def wait(number):
            for copy in copies[number]:
                copy.wait()

        return wait

    def copy_out(self, me, grad, targets, sem, owner, span, action):
        if not self.split_out:
            span = pl.ds(*span)
            action(pltpu.make_async_copy(grad.at[owner, span], targets[0].at[owner, span], sem))
            return
        place = me ^ owner
        first, size = span
        second = self.cut is not None and first >= self.cut
        there = pl.ds(first - (self.cut if second else 0), size)
        span = pl.ds(first, size)
        for target, odd in zip(targets[2:] if second else targets, (0, 1)):

            @pl.when(lax.rem(place, 2) == odd)
            def _():
                action(pltpu.make_async_copy(grad.at[owner, span], target.at[place // 2, there], sem))

    def store(self, me, grad, targets, sems, number, owners=None):
        span = self.spans[number]
        owners = range(self.owners) if owners is None else owners
        for owner in owners:
            self.copy_out(me, grad, targets, sems.at[number, owner], owner, span, lambda copy: copy.start())

        def wait():
            for owner in owners:
                self.copy_out(me, grad, targets, sems.at[number, owner], owner, span, lambda copy: copy.wait())

        return wait

    def matrix(self, held, number, columns=slice(None)):
        start, size = self.spans[number]
        return flat(held[:, start : start + size, columns])

    def put(self, grad, number, columns, values):
        start, size = self.spans[number]
        grad[:, start : start + size, columns] = rounded(values).reshape(self.owners, size, values.shape[1])


def run(kernel, name, numbers, values, pieces, outs, targets, scratch):
    in_specs = [pl.BlockSpec(memory_space=pltpu.SMEM)]
    in_specs += [pl.BlockSpec(memory_space=pltpu.VMEM)] * len(values)
    in_specs += [pl.BlockSpec(memory_space=pl.ANY)] * len(pieces)
    out_specs = [pl.BlockSpec(memory_space=pltpu.VMEM)] * len(outs)
    out_specs += [pl.BlockSpec(memory_space=pl.ANY)] * len(targets)
    return pl.pallas_call(
        kernel,
        out_shape=outs + targets,
        in_specs=in_specs,
        out_specs=out_specs,
        scratch_shapes=scratch,
        compiler_params=pltpu.CompilerParams(vmem_limit_bytes=VMEM_MIB[name] * 1024 * 1024),
        cost_estimate=pl.CostEstimate(flops=0, bytes_accessed=1024, transcendentals=0),
        name=name,
    )(numbers, *values, *pieces)


class Refs:
    def __init__(self, refs):
        self.refs = list(refs)

    def take(self, count):
        taken, self.refs = self.refs[:count], self.refs[count:]
        return taken


def cross_forward_kernel(chunk, given, *refs):
    refs = Refs(refs)
    numbers, language, vision = refs.take(3)
    given = refs.take(given)
    sources = refs.take(chunk.sources)
    language_a, vision_a, rows_in, total, query, key, value, context, kept_l, kept_v, vectors, up_bias = refs.take(12)
    held, bias_l, bias_v, sems = refs.take(4)
    me = numbers[0]
    wait = chunk.load(me, sources, held, sems, [*range(4, len(chunk.spans)), *range(4)])
    split, every = language.shape[0], rows_in.shape[0]
    own = (slice(0, split), slice(split, every))
    rows_in[own[0]] = language[...]
    rows_in[own[1]] = vision[...]
    counts = [numbers[item] for item in range(1, numbers.shape[0])]
    fill_bias(bias_l, len(counts), counts)
    fill_bias(bias_v, len(counts))
    if chunk.split_in:
        local = D // 8
        wait(4)
        extra = slice(chunk.spans[4][0], chunk.rows)
        found = None
        for owner in range(8):
            moved = mm(held[owner, extra, :128], shift_matrix(owner, local))
            found = moved if found is None else found + moved
        vectors[...] = found
        for quarter in range(4):
            wide = [widened(held[2 * quarter + side, extra, : D // 2]) for side in range(2)]
            wide = jnp.concatenate(wide, axis=1)
            for stream in range(2):
                line = NARROW + stream
                up_bias[4 * stream + quarter : 4 * stream + quarter + 1, :] = wide[line : line + 1]
    else:
        vectors[...] = given[0][...]
        up_bias[...] = given[1][...]
    for number, target in enumerate((query, key, value)):
        wait(number)
        for columns in blocks():
            found = mm(rows_in[...], chunk.matrix(held, number, columns))
            if number != 1:
                line = number // 2
                found = found + vectors[line : line + 1, columns]
            target[:, columns] = rounded(found)
    attend(query, key, value, context, own[0], own[1], bias_l, kept_l)
    attend(query, key, value, context, own[1], own[0], bias_v, kept_v)
    wait(3)
    for columns in blocks():
        branch = mm(context[...], chunk.matrix(held, 3, columns)) + vectors[2:3, columns]
        total[:, columns] = widened(rows_in[:, columns]) + branch
    for rows, target in zip(own, (language_a, vision_a)):
        target[...] = norm_forward(total[rows], vectors[4:5], vectors[3:4])


def self_forward_kernel(stream, chunk, *refs):
    refs = Refs(refs)
    numbers, inputs, vectors = refs.take(3)
    sources = refs.take(chunk.sources)
    outputs, total, query, key, value, context, kept = refs.take(7)
    held, bias, sems = refs.take(3)
    wait = chunk.load(numbers[0], sources, held, sems, range(4))
    rows = inputs.shape[0]
    counts = [numbers[item] for item in range(1, numbers.shape[0])]
    fill_bias(bias, len(counts), counts if stream else None)
    first = 5 + 4 * stream
    low_inputs = rounded(inputs[...])
    for number, target in enumerate((query, key, value)):
        wait(number)
        for columns in blocks():
            found = mm(low_inputs, chunk.matrix(held, number, columns))
            if number != 1:
                line = first + number // 2
                found = found + vectors[line : line + 1, columns]
            target[:, columns] = rounded(found)
    every = slice(0, rows)
    attend(query, key, value, context, every, every, bias, kept)
    wait(3)
    for columns in blocks():
        branch = mm(context[...], chunk.matrix(held, 3, columns)) + vectors[first + 2 : first + 3, columns]
        total[:, columns] = inputs[:, columns] + branch
    gain = 13 + stream
    outputs[...] = norm_forward(total[...], vectors[gain : gain + 1], vectors[first + 3 : first + 4])


def feed_kernel(stream, chunk, *refs):
    refs = Refs(refs)
    numbers, inputs, cotangent, vectors, up_bias = refs.take(5)
    sources = refs.take(chunk.sources)
    outputs, d_inputs, small, d_up_bias = refs.take(4)
    targets = refs.take(len(chunk.targets))
    held, grad, slope, hidden, total, sems, out_sems = refs.take(7)
    me = numbers[0]
    wait = chunk.load(me, sources, held, sems, (0, 4, 1, 2, 3))
    owners = chunk.owners // 4
    local = D // chunk.owners
    line = 15 + 2 * stream
    gain = vectors[19 + stream : 20 + stream]
    low_inputs = rounded(inputs[...])

    def down_matrix(quarter):
        return flat(held[quarter * owners : (quarter + 1) * owners, 4 * local :, :])

    total[...] = inputs[...] + vectors[line : line + 1]
    for quarter in range(4):
        wait(quarter)
        for columns in blocks():
            before = mm(low_inputs, chunk.matrix(held, quarter, columns))
            before = before + up_bias[4 * stream + quarter : 4 * stream + quarter + 1, columns]
            spread = 0.5 * (1.0 + lax.erf(before * 0.5**0.5))
            slope[quarter, :, columns] = spread + before * jnp.exp(-0.5 * before * before) * (0.5 / 3.141592653589793) ** 0.5
            hidden[quarter, :, columns] = rounded(before * spread)
        if quarter == 0:
            wait(4)
        total[...] += mm(hidden[quarter], down_matrix(quarter))
    arriving = widened(cotangent[...])
    found = norm_forward(total[...], gain, vectors[line + 1 : line + 2])
    if stream:
        counts = [numbers[item] for item in range(1, numbers.shape[0])]
        mask = jnp.where(present_item((inputs.shape[0], 1), 0, counts) < 0, 0.0, 1.0)
        found = found * mask
        arriving = arriving * mask
    back, d_gain, d_shift = norm_backward(total[...], arriving, gain)
    outputs[...] = rounded(found)
    d_inputs[...] = back
    low_back = rounded(back)
    small[...] = jnp.zeros_like(small)
    small[0:1] = column_sum(widened(low_back))
    small[1:2] = d_shift
    small[2:3] = d_gain
    pending = []
    for quarter in range(4):
        d_hidden = mm_nt(low_back, down_matrix(quarter))
        d_before = rounded(d_hidden * slope[quarter])
        d_up_bias[quarter : quarter + 1, :] = column_sum(widened(d_before))
        for columns in blocks():
            found = rounded(mm_tn(hidden[quarter], low_back[:, columns]))
            grad[quarter * owners : (quarter + 1) * owners, 4 * local :, columns] = found.reshape(owners, 4 * local, BLOCK)
        pending.append(chunk.store(me, grad, targets, out_sems, 4, range(quarter * owners, (quarter + 1) * owners)))
        for columns in blocks():
            chunk.put(grad, quarter, columns, mm_tn(low_inputs, d_before[:, columns]))
        pending.append(chunk.store(me, grad, targets, out_sems, quarter))
        d_inputs[...] += mm_nt(d_before, chunk.matrix(held, quarter))
    for finish in pending:
        finish()


def layer_back(chunk, total, context, held, gain, d_norm, d_inputs, grad, d_context, low_back, wait):
    back, d_gain, d_shift = norm_backward(total, d_norm, gain)
    d_inputs[...] = back
    low_back[...] = rounded(back)
    wait(3)
    d_context[...] = rounded(mm_nt(low_back[...], chunk.matrix(held, 3)))
    for columns in blocks():
        chunk.put(grad, 3, columns, mm_tn(context[...], low_back[:, columns]))
    return d_gain, d_shift, column_sum(widened(low_back[...]))


def projections_back(chunk, low_inputs, held, grad, d_all, d_inputs, wait, store):
    pending = []
    for number, gradient in enumerate(d_all):
        for columns in blocks():
            chunk.put(grad, number, columns, mm_tn(low_inputs, gradient[:, columns]))
        pending.append(store(number))
    for number, gradient in enumerate(d_all):
        wait(number)
        d_inputs[...] += mm_nt(gradient[...], chunk.matrix(held, number))
    return pending


def self_backward_kernel(stream, chunk, *refs):
    refs = Refs(refs)
    numbers, d_outputs, inputs, total, query, key, value, context, kept, vectors = refs.take(10)
    sources = refs.take(chunk.sources)
    d_inputs, small = refs.take(2)
    targets = refs.take(len(chunk.targets))
    held, grad, d_context, low_back, d_query, d_key, d_value, sems, out_sems = refs.take(9)
    me = numbers[0]
    wait = chunk.load(me, sources, held, sems, (3, 0, 1, 2))
    store = functools.partial(chunk.store, me, grad, targets, out_sems)
    rows = inputs.shape[0]
    low_inputs = rounded(inputs[...])
    gain = vectors[13 + stream : 14 + stream]
    d_gain, d_shift, d_out = layer_back(
        chunk, total[...], context, held, gain, d_outputs[...], d_inputs, grad, d_context, low_back, wait
    )
    pending = [store(3)]
    every = slice(0, rows)
    attend_back(query, key, value, kept, d_context, every, every, d_query, d_key, d_value)
    pending += projections_back(chunk, low_inputs, held, grad, (d_query, d_key, d_value), d_inputs, wait, store)
    small[...] = jnp.zeros_like(small)
    lines = (column_sum(widened(d_query[...])), column_sum(widened(d_value[...])), d_out, d_shift, d_gain)
    for place, line in enumerate(lines):
        small[place : place + 1] = line
    for finish in pending:
        finish()


def cross_backward_kernel(chunk, *refs):
    refs = Refs(refs)
    numbers, d_language, d_vision, rows_in, total, query, key, value, context, kept_l, kept_v, vectors = refs.take(12)
    self_l, self_v, feed_l, feed_v = refs.take(4)
    ups = refs.take(2)
    sources = refs.take(chunk.sources)
    language_gradient, vision_gradient = refs.take(2)
    if not chunk.split_out:
        small_out, up_out = refs.take(2)
    targets = refs.take(len(chunk.targets))
    held, grad, d_norm, d_inputs, lines = refs.take(5)
    d_context, low_back, d_query, d_key, d_value, sems, out_sems = refs.take(7)
    me = numbers[0]
    wait = chunk.load(me, sources, held, sems, (3, 0, 1, 2))
    store = functools.partial(chunk.store, me, grad, targets, out_sems)
    split, every = language_gradient.shape[0], rows_in.shape[0]
    own = (slice(0, split), slice(split, every))
    d_norm[own[0]] = d_language[...]
    d_norm[own[1]] = d_vision[...]
    d_gain, d_shift, d_out = layer_back(
        chunk, total[...], context, held, vectors[4:5], d_norm[...], d_inputs, grad, d_context, low_back, wait
    )
    pending = [store(3)]
    attend_back(query, key, value, kept_l, d_context, own[0], own[1], d_query, d_key, d_value)
    attend_back(query, key, value, kept_v, d_context, own[1], own[0], d_query, d_key, d_value)
    found = (column_sum(widened(d_query[...])), column_sum(widened(d_value[...])), d_out, d_shift, d_gain)
    lines[...] = jnp.zeros_like(lines)
    for place, line in enumerate(found):
        lines[place : place + 1] = line
    moves = [(self_l, place, 5 + place) for place in range(4)] + [(self_v, place, 9 + place) for place in range(4)]
    moves += [(self_l, 4, 13), (self_v, 4, 14), (feed_l, 0, 15), (feed_l, 1, 16), (feed_v, 0, 17), (feed_v, 1, 18)]
    moves += [(feed_l, 2, 19), (feed_v, 2, 20)]
    for source, place, target in moves:
        lines[target : target + 1] = source[place : place + 1]
    if chunk.split_out:
        local = D // 8
        low_lines = rounded(lines[...])
        zeros = jnp.zeros((1, D // 2), F32)
        for owner in range(8):
            narrow = mm_nt(low_lines, shift_matrix(owner, local))
            block = jnp.concatenate([narrow, jnp.zeros((VECTORS, D - 128), F32)], axis=1)
            side = slice(owner % 2 * (D // 2), (owner % 2 + 1) * (D // 2))
            for stream in range(2):
                wide = ups[stream][owner // 2 : owner // 2 + 1, side]
                wide = jnp.concatenate([wide, zeros], axis=1)
                here = lax.broadcasted_iota(jnp.int32, (VECTORS, 1), 0) == NARROW + stream
                block = jnp.where(here, wide, block)
            grad[owner, chunk.spans[4][0] : chunk.rows, :] = rounded(block)
        pending += [store(4)]
    else:
        small_out[...] = lines[...]
        up_out[0:4] = ups[0][0:4]
        up_out[4:8] = ups[1][0:4]
    pending += projections_back(chunk, rows_in[...], held, grad, (d_query, d_key, d_value), d_inputs, wait, store)
    language_gradient[...] = d_inputs[own[0]]
    vision_gradient[...] = d_inputs[own[1]]
    for finish in pending:
        finish()


def finish_feed_kernel(*refs):
    refs = Refs(refs)
    terms_l, up_v, down_v = refs.take(4), refs.take(4), refs.take(4)
    up_grad, down_grad = refs.take(2)
    local = up_grad.shape[1]
    for quarter in range(4):
        rows, columns = slice(quarter * local, (quarter + 1) * local), slice(quarter * D, (quarter + 1) * D)
        up_grad[0, :, columns] = plus(*[term[rows] for term in terms_l])
        up_grad[1, :, columns] = plus(*[term[rows] for term in up_v])
    down_grad[0] = plus(*[term[4 * local :] for term in terms_l])
    down_grad[1] = plus(*[term[...] for term in down_v])


def finish_rest_kernel(*refs):
    refs = Refs(refs)
    terms_l = refs.take(4)
    sides = [refs.take(4) for _ in range(2)]
    self_qkv, self_out, qkv, out, bias, gain, self_bias, self_gain, up_bias, feed_bias, feed_gain = refs.take(11)
    local = out.shape[0]
    found = [plus(*[term[...] for term in terms]) for terms in sides]
    for stream in range(2):
        for number in range(4):
            target = self_out.at[stream] if number == 3 else self_qkv.at[stream, number]
            if stream:
                target[...] = found[number // 2][number % 2 * local : (number % 2 + 1) * local]
            else:
                target[...] = plus(*[term[number * local : (number + 1) * local] for term in terms_l])
    start = 2 * local
    for number in range(2):
        qkv[number] = found[0][start + number * local : start + (number + 1) * local]
    above = VECTORS // 2
    qkv[2, :above] = found[0][start + 2 * local :]
    qkv[2, above:] = found[1][start : start + local - above]
    out[...] = found[1][start + local - above : start + 2 * local - above]
    small = found[1][start + 2 * local - above :]
    bias[...] = small[0:4, :local]
    gain[...] = small[4:5, :local]
    for stream in range(2):
        self_bias[stream] = small[5 + 4 * stream : 9 + 4 * stream, :local]
        self_gain[stream : stream + 1] = small[13 + stream : 14 + stream, :local]
        feed_bias[stream] = small[15 + 2 * stream : 17 + 2 * stream, :local]
        feed_gain[stream : stream + 1] = small[19 + stream : 20 + stream, :local]
        up_bias[stream : stream + 1] = small[NARROW + stream : NARROW + stream + 1, : 4 * local]


def pack_cross_kernel(qkv, out, bias, gain, self_bias, self_gain, feed_bias, feed_gain, up_bias, shard, extra):
    local = out.shape[0]
    extra[...] = jnp.zeros_like(extra)
    extra[0:4, :local] = bias[...]
    extra[4:5, :local] = gain[...]
    for stream in range(2):
        extra[5 + 4 * stream : 9 + 4 * stream, :local] = self_bias[stream]
        extra[13 + stream : 14 + stream, :local] = self_gain[stream : stream + 1]
        extra[15 + 2 * stream : 17 + 2 * stream, :local] = feed_bias[stream]
        extra[19 + stream : 20 + stream, :local] = feed_gain[stream : stream + 1]
        extra[NARROW + stream : NARROW + stream + 1, : 4 * local] = up_bias[stream : stream + 1]
    for number in range(3):
        shard[number * local : (number + 1) * local] = rounded(qkv[number])
    shard[3 * local : 4 * local] = rounded(out[...])
    shard[4 * local :] = rounded(extra[...])


def pack_rest_kernel(token, qkv, out, up, down, own, feed_l, feed_v):
    local = out.shape[1]
    for stream, feed in enumerate((feed_l, feed_v)):
        for number in range(3):
            own[(4 * stream + number) * local : (4 * stream + number + 1) * local] = rounded(qkv[stream, number])
        own[(4 * stream + 3) * local : (4 * stream + 4) * local] = rounded(out[stream])
        for quarter in range(4):
            feed[quarter * local : (quarter + 1) * local] = rounded(up[stream, :, quarter * D : (quarter + 1) * D])
        feed[4 * local :] = rounded(down[stream])


def in_vmem(kernel, values, outs, scratch=()):
    return pl.pallas_call(
        kernel,
        out_shape=outs,
        in_specs=[pl.BlockSpec(memory_space=pltpu.VMEM)] * len(values),
        out_specs=[pl.BlockSpec(memory_space=pltpu.VMEM)] * len(outs),
        scratch_shapes=scratch,
        compiler_params=pltpu.CompilerParams(vmem_limit_bytes=60 * 1024 * 1024),
        cost_estimate=pl.CostEstimate(flops=0, bytes_accessed=1024, transcendentals=0),
        name=kernel.__name__,
    )(*values)


def finish(kernel, chunks, outs):
    return in_vmem(kernel, [term for chunk in chunks for term in chunk], outs)


def after(values, *others):
    return lax.optimization_barrier((values, *others))[0] if others else values


class Order:
    depths = {"x": 2, "y": 2, "core": 3, "one": 9, "two": 9, "three": 9}

    def __init__(self):
        self.kernel, self.last = [], []
        self.sent = {link: [] for link in self.depths}

    def ran(self, token, *beside):
        self.kernel, self.last = [token, *beside], []

    def use(self, values):
        return after(values, *self.kernel, *self.last)

    def settle(self, *values):
        self.last = [*self.last, *values]

    def did(self, values):
        self.last = [values]
        return values

    def send(self, link, values, axis, pairs, depth=None):
        sent, depth = self.sent[link], depth or self.depths[link]
        values = after(values, *self.kernel, *sent[max(len(sent) - depth, 0) : max(len(sent) - depth + 1, 0)])
        sent.append(lax.ppermute(values, axis, pairs))
        return sent[-1]

    def swap(self, link, values, depth=None):
        mask = {"core": 1, "x": 2, "y": 4}[link]
        return self.send(link, values, "fsdp", [(place, place ^ mask) for place in range(8)], depth)


def add_far_kernel(count, *refs):
    refs = Refs(refs)
    terms = [refs.take(2) for _ in range(count)]
    targets = refs.take(2)
    first = 0
    for keep, got in terms:
        rows = slice(first, first + keep.shape[2])
        first = rows.stop
        for side, target in enumerate(targets):
            target[rows] = rounded(plus(keep[0, side], got[0, side]))


def add_near_kernel(count, *refs):
    refs = Refs(refs)
    terms_x = [refs.take(2) for _ in range(count)]
    terms_y = [refs.take(2) for _ in range(count)]
    from_x, from_y, *targets = refs.refs
    joined = len(targets) == 2
    for number, (terms, side_more, more) in enumerate(((terms_x, 1, from_y), (terms_y, 0, from_x))):
        first = 0
        for keep, got in terms:
            rows = slice(first, first + keep.shape[2])
            first = rows.stop
            for side in range(2):
                extra = [more[rows]] if side == side_more else []
                target = targets[number].at[side] if joined else targets[2 * number + side].at[0]
                target[rows] = rounded(plus(keep[0, side], got[0, side], *extra))


def add_own_kernel(count, *refs):
    refs = Refs(refs)
    terms = [refs.take(2) for _ in range(count)]
    from_x, from_y = refs.take(2)
    first = 0
    for keep, got in terms:
        rows = slice(first, first + keep.shape[2])
        first = rows.stop
        for side in range(keep.shape[1]):
            target = refs.refs[0].at[side] if len(refs.refs) == 1 else refs.refs[side].at[0]
            target[rows] = rounded(plus(keep[0, side], got[0, side], from_x[side, rows], from_y[side, rows]))


def combine(kernel, places, keeps, gots, others, outs, side=None):
    half = keeps[0].shape[2]
    steps = half // 96 if half % 96 == 0 and len(keeps) == 1 else 1

    def spec(values, place=0):
        *more, rows, _ = values.shape
        if len(more) == 2:
            if side is not None:
                return pl.BlockSpec((1, 1, rows // steps, D), lambda block: (place, side, block, 0))
            return pl.BlockSpec((1, 2, rows // steps, D), lambda block: (place, 0, block, 0))
        return pl.BlockSpec((*more, rows // steps, D), lambda block: (*[0] * len(more), block, 0))

    terms = [term for keep, got in zip(keeps, gots) for term in (keep, got)]
    return pl.pallas_call(
        functools.partial(kernel, len(keeps)),
        grid=(steps,),
        in_specs=[spec(term, place) for place in places for term in terms] + [spec(leaf) for leaf in others],
        out_specs=[spec(leaf) for leaf in outs],
        out_shape=outs,
        compiler_params=pltpu.CompilerParams(vmem_limit_bytes=60 * 1024 * 1024),
        cost_estimate=pl.CostEstimate(flops=0, bytes_accessed=1024, transcendentals=0),
        name=kernel.__name__,
    )(*terms * len(places), *others)


class Gather:
    def __init__(self, order, shard, fars):
        self.order, self.shard, self.fars = order, shard, fars
        self.far_parts, self.far_cores = {}, {}

    def near(self, depth=1):
        self.near_x = self.order.swap("x", self.shard, depth)
        self.near_y = self.order.swap("y", self.shard, depth)

    def far(self, number=0):
        first, middle, last = self.fars[number]
        to_x = self.order.did(self.order.use(self.near_y)[first:middle])
        to_y = self.order.did(self.order.use(self.near_x)[middle:last])
        self.far_parts[number] = [self.order.swap("x", to_x), self.order.swap("y", to_y)]

    def own_core(self):
        self.own = self.order.swap("core", self.shard)

    def near_core(self):
        self.cores = [self.order.swap("core", piece) for piece in (self.near_x, self.near_y)]

    def far_core(self, number=0):
        self.far_cores[number] = [self.order.swap("core", piece) for piece in self.far_parts[number]]

    def pieces(self, number=0, sides=(0, 1)):
        pieces = [self.shard, self.own]
        for piece, core in zip((self.near_x, self.near_y), self.cores):
            pieces += [piece, core]
        for side in sides:
            pieces += [self.far_parts[number][side], self.far_cores[number][side]]
        return pieces


class Line:
    def __init__(self, order):
        self.order = order

    def line(self, own):
        self.own = own
        self.order.did(own[0])
        self.one, self.two, self.three = [[None] * len(own) for _ in range(3)]

    def first(self):
        self.one = [self.order.send("one", own, "dp", [(0, 1), (3, 2)]) for own in self.own]

    def second(self, number=0):
        own = self.order.did(rounded(plus(self.own[number], self.order.use(self.one[number]))))
        self.two[number] = self.order.send("two", own, "dp", [(1, 2), (2, 1)])

    def third(self, number=0):
        own = self.order.did(rounded(plus(self.own[number], self.order.use(self.two[number]))))
        self.three[number] = self.order.send("three", own, "dp", [(1, 0), (2, 3)])

    def terms(self, number=0):
        terms = self.own[number], self.one[number], self.two[number], self.three[number]
        return [term.reshape(-1, D) for term in terms]


class Reduce(Line):
    def __init__(self, order, keep, send):
        super().__init__(order)
        self.half = keep.shape[1] // 2
        self.keeps = [keep.reshape(4, 2, self.half, D)]
        self.gots = [order.swap("core", send).reshape(4, 2, self.half, D)]

    def join(self, other):
        self.half += other.half
        self.keeps += other.keeps
        self.gots += other.gots

    def far(self):
        outs = [shape(self.half, D, dtype=BF)] * 2
        gots = [self.order.use(got) for got in self.gots]
        to_x, to_y = combine(add_far_kernel, (3,), self.keeps, gots, [], outs)
        self.order.did(to_x)
        self.from_x, self.from_y = self.order.swap("x", to_x), self.order.swap("y", to_y)

    def near(self, parts=1):
        outs = [shape(2 // parts, self.half, D, dtype=BF)] * (2 * parts)
        others = [self.order.use(self.from_x), self.from_y]
        made = combine(add_near_kernel, (1, 2), self.keeps, self.gots, others, outs)
        self.order.did(made[0])
        arrived = [[], []]
        for part in range(parts):
            for number, link in enumerate("xy"):
                arrived[number].append(self.order.swap(link, made[parts * number + part]))
        self.from_x, self.from_y = arrived

    def plane(self, parts):
        others = [self.order.use(self.from_x[0]), self.from_y[0]]
        outs = [shape(2 // parts, self.half, D, dtype=BF)] * parts
        self.line(combine(add_own_kernel, (0,), self.keeps, self.gots, others, outs))

    def plane_side(self, side):
        if side == 0:
            self.own, self.one, self.two, self.three = [[None] * 2 for _ in range(4)]
        others = [self.order.use(self.from_x[side]), self.from_y[side]]
        outs = [shape(1, self.half, D, dtype=BF)]
        self.own[side] = combine(add_own_kernel, (0,), self.keeps, self.gots, others, outs, side)[0]
        self.order.did(self.own[side])
        self.one[side] = self.order.send("one", self.own[side], "dp", [(0, 1), (3, 2)])


def body(
    language,
    vision,
    region_mask,
    cross_qkv,
    cross_out,
    cross_bias,
    cross_gain,
    self_qkv,
    self_out,
    self_bias,
    self_gain,
    ffn_up,
    ffn_up_bias,
    ffn_down,
    ffn_bias,
    ffn_gain,
    language_cotangent,
    vision_cotangent,
):
    plane, line = lax.axis_size("fsdp"), lax.axis_size("dp")
    swaps = plane == 8 and line == 4
    rank = lax.axis_index("fsdp")
    items, words, _ = language.shape
    regions = vision.shape[1]
    local = cross_gain.shape[0]
    counts = (items * words, items * regions)
    every = sum(counts)
    by_place = lambda values: values.transpose(1, 0, 2).reshape(-1, D)
    by_item = lambda values: values.reshape(-1, items, D).transpose(1, 0, 2)
    tangents = (by_place(language_cotangent), by_place(vision_cotangent))
    numbers = jnp.concatenate([rank.astype(jnp.int32)[None], jnp.sum(region_mask, axis=1)])

    if swaps:
        leaves = [cross_qkv, cross_out, cross_bias, cross_gain[None], self_bias, self_gain, ffn_bias, ffn_gain, ffn_up_bias]
        scratch = [pltpu.VMEM((VECTORS, D), F32)]
        cross_shard = in_vmem(pack_cross_kernel, leaves, [shape(4 * local + VECTORS, D, dtype=BF)], scratch)[0]
        rest = [self_qkv, self_out, ffn_up, ffn_down]
        token = lax.slice(cross_shard, (4 * local, 0), (4 * local + 16, 128))
        own_shard, *feed_shards = in_vmem(pack_rest_kernel, [token, *rest], [shape(8 * local, D, dtype=BF)] * 3)
        rows = 4 * local
        spans = [(place * local, local) for place in range(4)]
        cross_chunk = Chunk(8, True, True, rows + VECTORS, spans + [(rows, VECTORS)], 0, 2 * local)
        self_chunks = [Chunk(8, True, True, rows, spans, stream * rows) for stream in range(2)]
        feed_chunks = [Chunk(8, True, out, 2 * rows, spans + [(rows, rows)], 0, rows) for out in (False, True)]
        given = []
    else:
        small = jnp.concatenate(
            [cross_bias, cross_gain[None], self_bias.reshape(8, local), self_gain, ffn_bias.reshape(4, local), ffn_gain]
        )
        self_shards = [rounded(jnp.concatenate([self_qkv[s].reshape(3 * local, D), self_out[s]])) for s in range(2)]
        up_shards = [rounded(ffn_up[s]).reshape(local, 4, D).transpose(1, 0, 2).reshape(4 * local, D) for s in range(2)]
        down_shards = [rounded(ffn_down[s]) for s in range(2)]

        def gather(shard):
            whole = lax.all_gather(shard.reshape(4, local, D), "fsdp", axis=1, tiled=True)
            return whole.reshape(4, 4, D // 4, D).transpose(1, 0, 2, 3).reshape(4, D, D)

        cross_shard = rounded(jnp.concatenate([cross_qkv.reshape(3 * local, D), cross_out]))
        spans = [(place * D // 4, D // 4) for place in range(4)]
        cross_chunk = Chunk(4, False, False, D, spans)
        self_chunks = [Chunk(4, False, False, D, spans)] * 2
        feed_chunks = [Chunk(4, False, False, 2 * D, spans + [(D, D)])] * 2
        vectors = widened(lax.all_gather(rounded(small), "fsdp", axis=1, tiled=True))
        up_bias = widened(lax.all_gather(rounded(ffn_up_bias), "fsdp", axis=1, tiled=True)).reshape(8, D)
        given = [jnp.pad(vectors, ((0, VECTORS - NARROW), (0, 0))), up_bias]

    def biases(rows, keys):
        return pltpu.VMEM((rows, keys), F32)

    def kept(rows, keys):
        return shape(HEADS, rows, keys, dtype=BF)

    both = [biases(counts[0], counts[1]), biases(counts[1], counts[0])]

    def cross_forward(pieces):
        return run(
            functools.partial(cross_forward_kernel, cross_chunk, len(given)),
            "cross_forward",
            numbers,
            [by_place(language), by_place(vision), *given],
            pieces,
            [shape(counts[0], D), shape(counts[1], D), shape(every, D, dtype=BF), shape(every, D)]
            + [shape(every, D, dtype=BF)] * 4
            + [kept(counts[0], counts[1]), kept(counts[1], counts[0])]
            + [shape(VECTORS, D), shape(8, D)],
            [],
            [cross_chunk.held] + both + [cross_chunk.sems],
        )

    def self_forward(stream, inputs, vectors, pieces):
        count, chunk = counts[stream], self_chunks[stream]
        return run(
            functools.partial(self_forward_kernel, stream, chunk),
            f"self_forward_{stream}",
            numbers,
            [inputs, vectors],
            pieces,
            [shape(count, D)] * 2 + [shape(count, D, dtype=BF)] * 4 + [kept(count, count)],
            [],
            [chunk.held, biases(count, count), chunk.sems],
        )

    def feed(stream, inputs, vectors, up_bias, pieces):
        count, chunk = counts[stream], feed_chunks[stream]
        return run(
            functools.partial(feed_kernel, stream, chunk),
            f"feed_{stream}",
            numbers,
            [inputs, tangents[stream], vectors, up_bias],
            pieces,
            [shape(count, D, dtype=BF), shape(count, D), shape(8, D), shape(4, D)],
            chunk.targets,
            [chunk.held] * 2
            + [pltpu.VMEM((4, count, D), F32), pltpu.VMEM((4, count, D), BF)]
            + [pltpu.VMEM((count, D), F32)]
            + [chunk.sems] * 2,
        )

    def self_backward(stream, gradient, inputs, self_kept, vectors, pieces):
        count, chunk = counts[stream], self_chunks[stream]
        return run(
            functools.partial(self_backward_kernel, stream, chunk),
            f"self_backward_{stream}",
            numbers,
            [gradient, inputs, *self_kept, vectors],
            pieces,
            [shape(count, D), shape(8, D)],
            chunk.targets,
            [chunk.held] * 2 + [pltpu.VMEM((count, D), BF)] * 5 + [chunk.sems] * 2,
        )

    def cross_backward(gradients, cross_kept, vectors, smalls, pieces):
        chunk = cross_chunk
        return run(
            functools.partial(cross_backward_kernel, chunk),
            "cross_backward",
            numbers,
            [*gradients, *cross_kept, vectors, *smalls],
            pieces,
            [shape(counts[0], D), shape(counts[1], D)] + ([] if swaps else [shape(VECTORS, D), shape(8, D)]),
            chunk.targets,
            [chunk.held] * 2
            + [pltpu.VMEM((every, D), F32)] * 2
            + [pltpu.VMEM((VECTORS, D), F32)]
            + [pltpu.VMEM((every, D), BF)] * 5
            + [chunk.sems] * 2,
        )

    if swaps:
        order = Order()
        cross = Gather(order, cross_shard, [(0, 2 * local, rows + VECTORS)])
        own = Gather(order, own_shard, [(0, rows, 2 * rows)])
        feed_l, feed_v = [Gather(order, shard, [(0, rows, 2 * rows)]) for shard in feed_shards]
        cross.near()
        cross.own_core()
        order.did(own_shard)
        cross.far()
        own.near()
        cross.near_core()
        cross.far_core()
        made = cross_forward(cross.pieces())
        first_a, cross_kept, (vectors, up_bias) = made[:2], made[2:10], made[10:]
        order.ran(up_bias, own.near_x, own.near_y)

        own.far()
        own.own_core()
        own.near_core()
        feed_l.near()
        own.far_core()
        second_l = self_forward(0, first_a[0], order.use(vectors), own.pieces(0, (0,)))
        second_v = self_forward(1, after(first_a[1], second_l[0]), vectors, own.pieces(0, (1,)))
        order.ran(second_v[0], feed_l.near_x, feed_l.near_y)

        feed_l.far()
        feed_l.own_core()
        feed_l.near_core()
        feed_v.near()
        feed_l.far_core()
        fed_l = feed(0, second_l[0], order.use(vectors), up_bias, feed_l.pieces())
        order.ran(fed_l[2])

        feed_v.own_core()
        back_l = self_backward(0, fed_l[1], first_a[0], second_l[1:], order.use(vectors), own.pieces(0, (0,)))
        order.ran(back_l[1], feed_v.near_x, feed_v.near_y, feed_v.own)
        summed_l = lax.psum_scatter(order.use(fed_l[4]), "fsdp", scatter_dimension=0)

        feed_v.far()
        feed_v.near_core()
        sum_self_l = Reduce(order, *back_l[2:])
        sum_self_l.far()
        feed_v.far_core()
        fed_v = feed(1, second_v[0], order.use(vectors), up_bias, feed_v.pieces())
        order.ran(fed_v[2], sum_self_l.from_x, sum_self_l.from_y)

        sum_self_l.near()
        sum_feed_v = Reduce(order, *fed_v[4:])
        back_v = self_backward(1, fed_v[1], first_a[1], second_v[1:], order.use(vectors), own.pieces(0, (1,)))
        order.ran(back_v[1], *sum_self_l.from_x, *sum_self_l.from_y, *sum_feed_v.gots)

        sum_feed_v.far()
        sum_last = Reduce(order, *back_v[2:])
        sum_self_l.plane(1)
        sum_self_l.first()
        smalls = [back_l[1], back_v[1], fed_l[2], fed_v[2], fed_l[3], fed_v[3]]
        made = cross_backward([back_l[0], back_v[0]], cross_kept, order.use(vectors), smalls, cross.pieces())
        gradients = made[:2]
        order.ran(made[1], sum_feed_v.from_x, sum_feed_v.from_y, *sum_self_l.one, *sum_last.gots)

        sum_feed_l = Line(order)
        sum_feed_l.line([order.use(summed_l)])
        sum_feed_l.first()
        sum_last.join(Reduce(order, *made[2:]))
        sum_feed_v.near()
        sum_self_l.second()
        sum_last.far()
        sum_feed_l.second()
        sum_self_l.third()
        sum_feed_v.plane(2)
        sum_feed_v.first()
        sum_last.near()
        sum_feed_v.second(0)
        sum_feed_l.third()
        sum_feed_v.second(1)
        sum_last.plane(2)
        sum_last.first()
        order.settle(*sum_self_l.three)
        sum_feed_v.third(0)
        order.settle(*sum_feed_l.three)
        sum_last.second(0)
        sum_feed_v.third(1)
        sum_last.second(1)
        order.settle(sum_feed_v.three[0])
        sum_last.third(0)
        order.settle(sum_feed_v.three[1])
        sum_last.third(1)
        feed_terms = [sum_feed_l.terms()] + [sum_feed_v.terms(number) for number in range(2)]
        feed_terms[0][0] = order.use(feed_terms[0][0])
        feed_grads = finish(finish_feed_kernel, feed_terms, [shape(*ffn_up.shape), shape(*ffn_down.shape)])
        leaves = [self_qkv, self_out, cross_qkv, cross_out, cross_bias, cross_gain[None], self_bias, self_gain]
        leaves += [ffn_up_bias, ffn_bias, ffn_gain]
        last_terms = [sum_self_l.terms()] + [sum_last.terms(number) for number in range(2)]
        last_terms[0][0] = after(last_terms[0][0], feed_grads[0])
        rest = finish(finish_rest_kernel, last_terms, [shape(*leaf.shape) for leaf in leaves])
        grads = [*rest[2:5], rest[5][0], *rest[:2], *rest[6:8], feed_grads[0], rest[8], feed_grads[1], *rest[9:]]
        outputs = fed_l[0], fed_v[0]
    else:
        cross_pieces = [gather(cross_shard)]
        self_pieces = [[gather(shard)] for shard in self_shards]
        feed_pieces = []
        for up, down in zip(up_shards, down_shards):
            down = lax.all_gather(down, "fsdp", axis=0, tiled=True).reshape(4, D, D)
            feed_pieces.append([jnp.concatenate([gather(up), down], axis=1)])
        made = cross_forward(cross_pieces)
        first_a, cross_kept, (vectors, up_bias) = made[:2], made[2:10], made[10:]
        second = [self_forward(s, first_a[s], vectors, self_pieces[s]) for s in range(2)]
        fed = [feed(s, second[s][0], vectors, up_bias, feed_pieces[s]) for s in range(2)]
        back = [self_backward(s, fed[s][1], first_a[s], second[s][1:], vectors, self_pieces[s]) for s in range(2)]
        smalls = [back[0][1], back[1][1], fed[0][2], fed[1][2], fed[0][3], fed[1][3]]
        made = cross_backward([back[0][0], back[1][0]], cross_kept, vectors, smalls, cross_pieces)
        gradients = made[:2]
        outputs = fed[0][0], fed[1][0]

        def whole(grad, by_owner=True):
            if by_owner:
                grad = grad.reshape(4, 4, D // 4, D).transpose(1, 0, 2, 3).reshape(4, D, D)
                own = lax.psum_scatter(grad, "fsdp", scatter_dimension=1, tiled=True)
            else:
                own = lax.psum_scatter(grad.reshape(4 * D, D), "fsdp", scatter_dimension=0, tiled=True)
            return widened(lax.psum(own, "dp")).reshape(4 * local, D)

        up_done = [whole(made_s[4][:, :D]) for made_s in fed]
        down_done = [whole(made_s[4][:, D:], False) for made_s in fed]
        self_done = [whole(made_s[2]) for made_s in back]
        cross_done = whole(made[4])
        small = lax.dynamic_slice(lax.psum(made[2], ("fsdp", "dp")), (0, rank * local), (NARROW, local))
        up_small = lax.psum(made[3], ("fsdp", "dp")).reshape(2, 4 * D)
        up_small = lax.dynamic_slice(up_small, (0, 4 * rank * local), (2, 4 * local))
        up_grads = [done.reshape(4, local, D).transpose(1, 0, 2).reshape(local, 4 * D) for done in up_done]
        grads = [cross_done[: 3 * local].reshape(3, local, D), cross_done[3 * local :], small[0:4], small[4]]
        grads += [jnp.stack([done[: 3 * local].reshape(3, local, D) for done in self_done])]
        grads += [jnp.stack([done[3 * local :] for done in self_done])]
        grads += [small[5:13].reshape(2, 4, local), small[13:15], jnp.stack(up_grads), up_small, jnp.stack(down_done)]
        grads += [small[15:19].reshape(2, 2, local), small[19:21]]

    return (*[by_item(rows) for rows in (*outputs, *gradients)], *grads)


def solution(mesh):
    return jax.shard_map(
        body,
        mesh=mesh,
        in_specs=(
            P(("fsdp", "dp"), None, None),
            P(("fsdp", "dp"), None, None),
            P(("fsdp", "dp"), None),
            P(None, "fsdp", None),
            P("fsdp", None),
            P(None, "fsdp"),
            P("fsdp"),
            P(None, None, "fsdp", None),
            P(None, "fsdp", None),
            P(None, None, "fsdp"),
            P(None, "fsdp"),
            P(None, "fsdp", None),
            P(None, "fsdp"),
            P(None, "fsdp", None),
            P(None, None, "fsdp"),
            P(None, "fsdp"),
            P(("fsdp", "dp"), None, None),
            P(("fsdp", "dp"), None, None),
        ),
        out_specs=(
            P(("fsdp", "dp"), None, None),
            P(("fsdp", "dp"), None, None),
            P(("fsdp", "dp"), None, None),
            P(("fsdp", "dp"), None, None),
            P(None, "fsdp", None),
            P("fsdp", None),
            P(None, "fsdp"),
            P("fsdp"),
            P(None, None, "fsdp", None),
            P(None, "fsdp", None),
            P(None, None, "fsdp"),
            P(None, "fsdp"),
            P(None, "fsdp", None),
            P(None, "fsdp"),
            P(None, "fsdp", None),
            P(None, None, "fsdp"),
            P(None, "fsdp"),
        ),
        check_vma=False,
    )
```

```python
import functools

import jax
import jax.numpy as jnp
from jax import lax
from jax.experimental import pallas as pl
from jax.experimental.pallas import tpu as pltpu
from jax.sharding import PartitionSpec as P

HEADS = 12
HEAD_DIM = 64
PAIR = 2 * HEAD_DIM
D = HEADS * HEAD_DIM
NARROW = 21
VECTORS = 32
BLOCK = 256
VMEM_MIB = dict(cross_forward=60, self_forward_0=60, self_forward_1=60, feed_0=60, feed_1=60)
VMEM_MIB.update(self_backward_0=60, self_backward_1=60, cross_backward=60)

epsilon = 1e-06
hidden_score = -1e30

BF = jnp.bfloat16
F32 = jnp.float32


def rounded(values):
    return values.astype(BF)


def widened(values):
    return values.astype(F32)


def shape(*sizes, dtype=F32):
    return jax.ShapeDtypeStruct(sizes, dtype)


def plus(*values):
    total = widened(values[0])
    for value in values[1:]:
        total = total + widened(value)
    return total


def mm(left, right):
    return jnp.dot(left, right, preferred_element_type=F32)


def mm_nt(left, right):
    return lax.dot_general(left, right, (((1,), (1,)), ((), ())), preferred_element_type=F32)


def mm_tn(left, right):
    return lax.dot_general(left, right, (((0,), (0,)), ((), ())), preferred_element_type=F32)


def flat(block):
    return block.reshape(block.shape[0] * block.shape[1], block.shape[2])


def column_sum(values):
    return jnp.sum(values, axis=0, keepdims=True)


def blocks():
    return [slice(start, start + BLOCK) for start in range(0, D, BLOCK)]


def norm_forward(total, gain, shift):
    centre = total - jnp.mean(total, axis=-1, keepdims=True)
    spread = jnp.mean(centre * centre, axis=-1, keepdims=True)
    return centre * lax.rsqrt(spread + epsilon) * gain + shift


def norm_backward(total, gradient, gain):
    centre = total - jnp.mean(total, axis=-1, keepdims=True)
    spread = jnp.mean(centre * centre, axis=-1, keepdims=True)
    scale = lax.rsqrt(spread + epsilon)
    unit = centre * scale
    inner = gradient * gain
    mean_inner = jnp.mean(inner, axis=-1, keepdims=True)
    mean_product = jnp.mean(inner * unit, axis=-1, keepdims=True)
    back = scale * (inner - mean_inner - unit * mean_product)
    return back, column_sum(gradient * unit), column_sum(gradient)


def place_of(extent, axis, items):
    number = lax.broadcasted_iota(jnp.int32, extent, axis).astype(F32)
    place = jnp.floor((number + 0.5) * (1.0 / items))
    return number - place * items, place


def present_item(extent, axis, counts):
    item, place = place_of(extent, axis, len(counts))
    limit = jnp.zeros_like(place)
    for number, count in enumerate(counts):
        limit = jnp.where(item == number, count.astype(F32), limit)
    return jnp.where(place < limit, item, -1.0)


def fill_bias(bias, items, counts=None):
    rows, keys = bias.shape
    key_item = place_of((1, keys), 1, items)[0] if counts is None else present_item((1, keys), 1, counts)
    bias[...] = jnp.where(place_of((rows, 1), 0, items)[0] == key_item, 0.0, hidden_score)


def attend(query, key, value, context, query_rows, key_rows, bias, kept):
    low = lax.broadcasted_iota(jnp.int32, (1, PAIR), 1) < HEAD_DIM
    for number in range(HEADS // 2):
        columns = slice(number * PAIR, (number + 1) * PAIR)
        rows, others = query_rows, key_rows
        queries = query[rows, columns] * HEAD_DIM ** (-0.5)
        keys = key[others, columns]
        values = value[others, columns]
        total = None
        for side, half in enumerate((low, ~low)):
            scores = mm_nt(jnp.where(half, queries, 0), keys) + bias[...]
            shifted = jnp.exp(scores - jnp.max(scores, axis=-1, keepdims=True))
            weight = rounded(shifted / jnp.sum(shifted, axis=-1, keepdims=True))
            kept[2 * number + side] = weight
            found = mm(weight, jnp.where(half, values, 0))
            total = found if total is None else total + found
        context[rows, columns] = rounded(total)


def attend_back(query, key, value, kept, d_context, query_rows, key_rows, d_query, d_key, d_value):
    low = lax.broadcasted_iota(jnp.int32, (1, PAIR), 1) < HEAD_DIM
    scale = HEAD_DIM ** (-0.5)
    for number in range(HEADS // 2):
        columns = slice(number * PAIR, (number + 1) * PAIR)
        rows, others = query_rows, key_rows
        queries = query[rows, columns] * scale
        keys = key[others, columns]
        values = value[others, columns]
        arriving = d_context[rows, columns]
        sums = [None] * 3
        for side, half in enumerate((low, ~low)):
            own_arriving = jnp.where(half, arriving, 0)
            weight = kept[2 * number + side]
            d_weight = mm_nt(own_arriving, values)
            weighed = d_weight * weight
            inner = jnp.sum(weighed, axis=-1, keepdims=True)
            d_scores = rounded(weighed - weight * inner)
            found = [
                mm(d_scores, jnp.where(half, keys * scale, 0)),
                mm_tn(d_scores, jnp.where(half, queries, 0)),
                mm_tn(weight, own_arriving),
            ]
            sums = [one if total is None else total + one for one, total in zip(found, sums)]
        d_query[rows, columns] = rounded(sums[0])
        d_key[others, columns] = rounded(sums[1])
        d_value[others, columns] = rounded(sums[2])


def shift_matrix(owner, local):
    row = lax.broadcasted_iota(jnp.int32, (128, D), 0)
    column = lax.broadcasted_iota(jnp.int32, (128, D), 1)
    return jnp.where((column == row + owner * local) & (row < local), 1.0, 0.0).astype(BF)


class Chunk:
    def __init__(self, owners, split_in, split_out, rows, spans, base=0, middle=None, cut=None):
        self.owners, self.split_in, self.split_out, self.rows, self.spans = owners, split_in, split_out, rows, spans
        self.base, self.middle, self.cut = base, middle, cut
        self.sources = (8 if middle is None else 10) if split_in else 1
        sizes = [rows] if cut is None else [cut, rows - cut]
        self.targets = [shape(owners, rows, D, dtype=BF)]
        if split_out:
            self.targets = [shape(4, size, D, dtype=BF) for size in sizes for _ in range(2)]
        self.held = pltpu.VMEM((owners, rows, D), BF)
        self.sems = pltpu.SemaphoreType.DMA((len(spans), owners))

    def load(self, me, sources, held, sems, order):
        copies = {}
        for number in order:
            start, size = self.spans[number]
            span = pl.ds(start, size)
            copies[number] = []
            for place in range(8 if self.split_in else 1):
                sem = sems.at[number, place]
                if not self.split_in:
                    copies[number].append(pltpu.make_async_copy(sources[0].at[:, span], held.at[:, span], sem))
                    continue
                pieces = [(start, size)]
                if place > 5 and self.middle is not None and start < self.middle < start + size:
                    pieces = [(start, self.middle - start), (self.middle, start + size - self.middle)]
                for first, count in pieces:
                    if place < 6:
                        source = sources[place].at[pl.ds(self.base + first, count)]
                    elif self.middle is None:
                        source = sources[place].at[pl.ds(first, count)]
                    else:
                        above = first >= self.middle
                        source = sources[place + 2 * above].at[pl.ds(first - self.middle * above, count)]
                    copies[number].append(pltpu.make_async_copy(source, held.at[me ^ place, pl.ds(first, count)], sem))
            for copy in copies[number]:
                copy.start()

        def wait(number):
            for copy in copies[number]:
                copy.wait()

        return wait

    def copy_out(self, me, grad, targets, sem, owner, span, action):
        if not self.split_out:
            span = pl.ds(*span)
            action(pltpu.make_async_copy(grad.at[owner, span], targets[0].at[owner, span], sem))
            return
        place = me ^ owner
        first, size = span
        second = self.cut is not None and first >= self.cut
        there = pl.ds(first - (self.cut if second else 0), size)
        span = pl.ds(first, size)
        for target, odd in zip(targets[2:] if second else targets, (0, 1)):

            @pl.when(lax.rem(place, 2) == odd)
            def _():
                action(pltpu.make_async_copy(grad.at[owner, span], target.at[place // 2, there], sem))

    def store(self, me, grad, targets, sems, number, owners=None):
        span = self.spans[number]
        owners = range(self.owners) if owners is None else owners
        for owner in owners:
            self.copy_out(me, grad, targets, sems.at[number, owner], owner, span, lambda copy: copy.start())

        def wait():
            for owner in owners:
                self.copy_out(me, grad, targets, sems.at[number, owner], owner, span, lambda copy: copy.wait())

        return wait

    def matrix(self, held, number, columns=slice(None)):
        start, size = self.spans[number]
        return flat(held[:, start : start + size, columns])

    def put(self, grad, number, columns, values):
        start, size = self.spans[number]
        grad[:, start : start + size, columns] = rounded(values).reshape(self.owners, size, values.shape[1])


def run(kernel, name, numbers, values, pieces, outs, targets, scratch):
    in_specs = [pl.BlockSpec(memory_space=pltpu.SMEM)]
    in_specs += [pl.BlockSpec(memory_space=pltpu.VMEM)] * len(values)
    in_specs += [pl.BlockSpec(memory_space=pl.ANY)] * len(pieces)
    out_specs = [pl.BlockSpec(memory_space=pltpu.VMEM)] * len(outs)
    out_specs += [pl.BlockSpec(memory_space=pl.ANY)] * len(targets)
    return pl.pallas_call(
        kernel,
        out_shape=outs + targets,
        in_specs=in_specs,
        out_specs=out_specs,
        scratch_shapes=scratch,
        compiler_params=pltpu.CompilerParams(vmem_limit_bytes=VMEM_MIB[name] * 1024 * 1024),
        cost_estimate=pl.CostEstimate(flops=0, bytes_accessed=1024, transcendentals=0),
        name=name,
    )(numbers, *values, *pieces)


class Refs:
    def __init__(self, refs):
        self.refs = list(refs)

    def take(self, count):
        taken, self.refs = self.refs[:count], self.refs[count:]
        return taken


def cross_forward_kernel(chunk, given, *refs):
    refs = Refs(refs)
    numbers, language, vision = refs.take(3)
    given = refs.take(given)
    sources = refs.take(chunk.sources)
    language_a, vision_a, rows_in, total, query, key, value, context, kept_l, kept_v, vectors, up_bias = refs.take(12)
    held, bias_l, bias_v, sems = refs.take(4)
    me = numbers[0]
    wait = chunk.load(me, sources, held, sems, [*range(4, len(chunk.spans)), *range(4)])
    split, every = language.shape[0], rows_in.shape[0]
    own = (slice(0, split), slice(split, every))
    rows_in[own[0]] = language[...]
    rows_in[own[1]] = vision[...]
    counts = [numbers[item] for item in range(1, numbers.shape[0])]
    fill_bias(bias_l, len(counts), counts)
    fill_bias(bias_v, len(counts))
    if chunk.split_in:
        local = D // 8
        wait(4)
        extra = slice(chunk.spans[4][0], chunk.rows)
        found = None
        for owner in range(8):
            moved = mm(held[owner, extra, :128], shift_matrix(owner, local))
            found = moved if found is None else found + moved
        vectors[...] = found
        for quarter in range(4):
            wide = [widened(held[2 * quarter + side, extra, : D // 2]) for side in range(2)]
            wide = jnp.concatenate(wide, axis=1)
            for stream in range(2):
                line = NARROW + stream
                up_bias[4 * stream + quarter : 4 * stream + quarter + 1, :] = wide[line : line + 1]
    else:
        vectors[...] = given[0][...]
        up_bias[...] = given[1][...]
    for number, target in enumerate((query, key, value)):
        wait(number)
        for columns in blocks():
            found = mm(rows_in[...], chunk.matrix(held, number, columns))
            if number != 1:
                line = number // 2
                found = found + vectors[line : line + 1, columns]
            target[:, columns] = rounded(found)
    attend(query, key, value, context, own[0], own[1], bias_l, kept_l)
    attend(query, key, value, context, own[1], own[0], bias_v, kept_v)
    wait(3)
    for columns in blocks():
        branch = mm(context[...], chunk.matrix(held, 3, columns)) + vectors[2:3, columns]
        total[:, columns] = widened(rows_in[:, columns]) + branch
    for rows, target in zip(own, (language_a, vision_a)):
        target[...] = norm_forward(total[rows], vectors[4:5], vectors[3:4])


def self_forward_kernel(stream, chunk, *refs):
    refs = Refs(refs)
    numbers, inputs, vectors = refs.take(3)
    sources = refs.take(chunk.sources)
    outputs, total, query, key, value, context, kept = refs.take(7)
    held, bias, sems = refs.take(3)
    wait = chunk.load(numbers[0], sources, held, sems, range(4))
    rows = inputs.shape[0]
    counts = [numbers[item] for item in range(1, numbers.shape[0])]
    fill_bias(bias, len(counts), counts if stream else None)
    first = 5 + 4 * stream
    low_inputs = rounded(inputs[...])
    for number, target in enumerate((query, key, value)):
        wait(number)
        for columns in blocks():
            found = mm(low_inputs, chunk.matrix(held, number, columns))
            if number != 1:
                line = first + number // 2
                found = found + vectors[line : line + 1, columns]
            target[:, columns] = rounded(found)
    every = slice(0, rows)
    attend(query, key, value, context, every, every, bias, kept)
    wait(3)
    for columns in blocks():
        branch = mm(context[...], chunk.matrix(held, 3, columns)) + vectors[first + 2 : first + 3, columns]
        total[:, columns] = inputs[:, columns] + branch
    gain = 13 + stream
    outputs[...] = norm_forward(total[...], vectors[gain : gain + 1], vectors[first + 3 : first + 4])


def feed_kernel(stream, chunk, *refs):
    refs = Refs(refs)
    numbers, inputs, cotangent, vectors, up_bias = refs.take(5)
    sources = refs.take(chunk.sources)
    outputs, d_inputs, small, d_up_bias = refs.take(4)
    targets = refs.take(len(chunk.targets))
    held, grad, slope, hidden, total, sems, out_sems = refs.take(7)
    me = numbers[0]
    wait = chunk.load(me, sources, held, sems, (0, 4, 1, 2, 3))
    owners = chunk.owners // 4
    local = D // chunk.owners
    line = 15 + 2 * stream
    gain = vectors[19 + stream : 20 + stream]
    low_inputs = rounded(inputs[...])

    def down_matrix(quarter):
        return flat(held[quarter * owners : (quarter + 1) * owners, 4 * local :, :])

    total[...] = inputs[...] + vectors[line : line + 1]
    for quarter in range(4):
        wait(quarter)
        for columns in blocks():
            before = mm(low_inputs, chunk.matrix(held, quarter, columns))
            before = before + up_bias[4 * stream + quarter : 4 * stream + quarter + 1, columns]
            spread = 0.5 * (1.0 + lax.erf(before * 0.5**0.5))
            slope[quarter, :, columns] = spread + before * jnp.exp(-0.5 * before * before) * (0.5 / 3.141592653589793) ** 0.5
            hidden[quarter, :, columns] = rounded(before * spread)
        if quarter == 0:
            wait(4)
        total[...] += mm(hidden[quarter], down_matrix(quarter))
    arriving = widened(cotangent[...])
    found = norm_forward(total[...], gain, vectors[line + 1 : line + 2])
    if stream:
        counts = [numbers[item] for item in range(1, numbers.shape[0])]
        mask = jnp.where(present_item((inputs.shape[0], 1), 0, counts) < 0, 0.0, 1.0)
        found = found * mask
        arriving = arriving * mask
    back, d_gain, d_shift = norm_backward(total[...], arriving, gain)
    outputs[...] = rounded(found)
    d_inputs[...] = back
    low_back = rounded(back)
    small[...] = jnp.zeros_like(small)
    small[0:1] = column_sum(widened(low_back))
    small[1:2] = d_shift
    small[2:3] = d_gain
    pending = []
    for quarter in range(4):
        d_hidden = mm_nt(low_back, down_matrix(quarter))
        d_before = rounded(d_hidden * slope[quarter])
        d_up_bias[quarter : quarter + 1, :] = column_sum(widened(d_before))
        for columns in blocks():
            found = rounded(mm_tn(hidden[quarter], low_back[:, columns]))
            grad[quarter * owners : (quarter + 1) * owners, 4 * local :, columns] = found.reshape(owners, 4 * local, BLOCK)
        pending.append(chunk.store(me, grad, targets, out_sems, 4, range(quarter * owners, (quarter + 1) * owners)))
        for columns in blocks():
            chunk.put(grad, quarter, columns, mm_tn(low_inputs, d_before[:, columns]))
        pending.append(chunk.store(me, grad, targets, out_sems, quarter))
        d_inputs[...] += mm_nt(d_before, chunk.matrix(held, quarter))
    for finish in pending:
        finish()


def layer_back(chunk, total, context, held, gain, d_norm, d_inputs, grad, d_context, low_back, wait):
    back, d_gain, d_shift = norm_backward(total, d_norm, gain)
    d_inputs[...] = back
    low_back[...] = rounded(back)
    wait(3)
    d_context[...] = rounded(mm_nt(low_back[...], chunk.matrix(held, 3)))
    for columns in blocks():
        chunk.put(grad, 3, columns, mm_tn(context[...], low_back[:, columns]))
    return d_gain, d_shift, column_sum(widened(low_back[...]))


def projections_back(chunk, low_inputs, held, grad, d_all, d_inputs, wait, store):
    pending = []
    for number, gradient in enumerate(d_all):
        for columns in blocks():
            chunk.put(grad, number, columns, mm_tn(low_inputs, gradient[:, columns]))
        pending.append(store(number))
    for number, gradient in enumerate(d_all):
        wait(number)
        d_inputs[...] += mm_nt(gradient[...], chunk.matrix(held, number))
    return pending


def self_backward_kernel(stream, chunk, *refs):
    refs = Refs(refs)
    numbers, d_outputs, inputs, total, query, key, value, context, kept, vectors = refs.take(10)
    sources = refs.take(chunk.sources)
    d_inputs, small = refs.take(2)
    targets = refs.take(len(chunk.targets))
    held, grad, d_context, low_back, d_query, d_key, d_value, sems, out_sems = refs.take(9)
    me = numbers[0]
    wait = chunk.load(me, sources, held, sems, (3, 0, 1, 2))
    store = functools.partial(chunk.store, me, grad, targets, out_sems)
    rows = inputs.shape[0]
    low_inputs = rounded(inputs[...])
    gain = vectors[13 + stream : 14 + stream]
    d_gain, d_shift, d_out = layer_back(
        chunk, total[...], context, held, gain, d_outputs[...], d_inputs, grad, d_context, low_back, wait
    )
    pending = [store(3)]
    every = slice(0, rows)
    attend_back(query, key, value, kept, d_context, every, every, d_query, d_key, d_value)
    pending += projections_back(chunk, low_inputs, held, grad, (d_query, d_key, d_value), d_inputs, wait, store)
    small[...] = jnp.zeros_like(small)
    lines = (column_sum(widened(d_query[...])), column_sum(widened(d_value[...])), d_out, d_shift, d_gain)
    for place, line in enumerate(lines):
        small[place : place + 1] = line
    for finish in pending:
        finish()


def cross_backward_kernel(chunk, *refs):
    refs = Refs(refs)
    numbers, d_language, d_vision, rows_in, total, query, key, value, context, kept_l, kept_v, vectors = refs.take(12)
    self_l, self_v, feed_l, feed_v = refs.take(4)
    ups = refs.take(2)
    sources = refs.take(chunk.sources)
    language_gradient, vision_gradient = refs.take(2)
    if not chunk.split_out:
        small_out, up_out = refs.take(2)
    targets = refs.take(len(chunk.targets))
    held, grad, d_norm, d_inputs, lines = refs.take(5)
    d_context, low_back, d_query, d_key, d_value, sems, out_sems = refs.take(7)
    me = numbers[0]
    wait = chunk.load(me, sources, held, sems, (3, 0, 1, 2))
    store = functools.partial(chunk.store, me, grad, targets, out_sems)
    split, every = language_gradient.shape[0], rows_in.shape[0]
    own = (slice(0, split), slice(split, every))
    d_norm[own[0]] = d_language[...]
    d_norm[own[1]] = d_vision[...]
    d_gain, d_shift, d_out = layer_back(
        chunk, total[...], context, held, vectors[4:5], d_norm[...], d_inputs, grad, d_context, low_back, wait
    )
    pending = [store(3)]
    attend_back(query, key, value, kept_l, d_context, own[0], own[1], d_query, d_key, d_value)
    attend_back(query, key, value, kept_v, d_context, own[1], own[0], d_query, d_key, d_value)
    found = (column_sum(widened(d_query[...])), column_sum(widened(d_value[...])), d_out, d_shift, d_gain)
    lines[...] = jnp.zeros_like(lines)
    for place, line in enumerate(found):
        lines[place : place + 1] = line
    moves = [(self_l, place, 5 + place) for place in range(4)] + [(self_v, place, 9 + place) for place in range(4)]
    moves += [(self_l, 4, 13), (self_v, 4, 14), (feed_l, 0, 15), (feed_l, 1, 16), (feed_v, 0, 17), (feed_v, 1, 18)]
    moves += [(feed_l, 2, 19), (feed_v, 2, 20)]
    for source, place, target in moves:
        lines[target : target + 1] = source[place : place + 1]
    if chunk.split_out:
        local = D // 8
        low_lines = rounded(lines[...])
        zeros = jnp.zeros((1, D // 2), F32)
        for owner in range(8):
            narrow = mm_nt(low_lines, shift_matrix(owner, local))
            block = jnp.concatenate([narrow, jnp.zeros((VECTORS, D - 128), F32)], axis=1)
            side = slice(owner % 2 * (D // 2), (owner % 2 + 1) * (D // 2))
            for stream in range(2):
                wide = ups[stream][owner // 2 : owner // 2 + 1, side]
                wide = jnp.concatenate([wide, zeros], axis=1)
                here = lax.broadcasted_iota(jnp.int32, (VECTORS, 1), 0) == NARROW + stream
                block = jnp.where(here, wide, block)
            grad[owner, chunk.spans[4][0] : chunk.rows, :] = rounded(block)
        pending += [store(4)]
    else:
        small_out[...] = lines[...]
        up_out[0:4] = ups[0][0:4]
        up_out[4:8] = ups[1][0:4]
    pending += projections_back(chunk, rows_in[...], held, grad, (d_query, d_key, d_value), d_inputs, wait, store)
    language_gradient[...] = d_inputs[own[0]]
    vision_gradient[...] = d_inputs[own[1]]
    for finish in pending:
        finish()


def finish_feed_kernel(*refs):
    refs = Refs(refs)
    terms_l, up_v, down_v = refs.take(4), refs.take(4), refs.take(4)
    up_grad, down_grad = refs.take(2)
    local = up_grad.shape[1]
    for quarter in range(4):
        rows, columns = slice(quarter * local, (quarter + 1) * local), slice(quarter * D, (quarter + 1) * D)
        up_grad[0, :, columns] = plus(*[term[rows] for term in terms_l])
        up_grad[1, :, columns] = plus(*[term[rows] for term in up_v])
    down_grad[0] = plus(*[term[4 * local :] for term in terms_l])
    down_grad[1] = plus(*[term[...] for term in down_v])


def finish_rest_kernel(*refs):
    refs = Refs(refs)
    terms_l = refs.take(4)
    sides = [refs.take(4) for _ in range(2)]
    self_qkv, self_out, qkv, out, bias, gain, self_bias, self_gain, up_bias, feed_bias, feed_gain = refs.take(11)
    local = out.shape[0]
    found = [plus(*[term[...] for term in terms]) for terms in sides]
    for stream in range(2):
        for number in range(4):
            target = self_out.at[stream] if number == 3 else self_qkv.at[stream, number]
            if stream:
                target[...] = found[number // 2][number % 2 * local : (number % 2 + 1) * local]
            else:
                target[...] = plus(*[term[number * local : (number + 1) * local] for term in terms_l])
    start = 2 * local
    for number in range(2):
        qkv[number] = found[0][start + number * local : start + (number + 1) * local]
    above = VECTORS // 2
    qkv[2, :above] = found[0][start + 2 * local :]
    qkv[2, above:] = found[1][start : start + local - above]
    out[...] = found[1][start + local - above : start + 2 * local - above]
    small = found[1][start + 2 * local - above :]
    bias[...] = small[0:4, :local]
    gain[...] = small[4:5, :local]
    for stream in range(2):
        self_bias[stream] = small[5 + 4 * stream : 9 + 4 * stream, :local]
        self_gain[stream : stream + 1] = small[13 + stream : 14 + stream, :local]
        feed_bias[stream] = small[15 + 2 * stream : 17 + 2 * stream, :local]
        feed_gain[stream : stream + 1] = small[19 + stream : 20 + stream, :local]
        up_bias[stream : stream + 1] = small[NARROW + stream : NARROW + stream + 1, : 4 * local]


def pack_cross_kernel(qkv, out, bias, gain, self_bias, self_gain, feed_bias, feed_gain, up_bias, shard, extra):
    local = out.shape[0]
    extra[...] = jnp.zeros_like(extra)
    extra[0:4, :local] = bias[...]
    extra[4:5, :local] = gain[...]
    for stream in range(2):
        extra[5 + 4 * stream : 9 + 4 * stream, :local] = self_bias[stream]
        extra[13 + stream : 14 + stream, :local] = self_gain[stream : stream + 1]
        extra[15 + 2 * stream : 17 + 2 * stream, :local] = feed_bias[stream]
        extra[19 + stream : 20 + stream, :local] = feed_gain[stream : stream + 1]
        extra[NARROW + stream : NARROW + stream + 1, : 4 * local] = up_bias[stream : stream + 1]
    for number in range(3):
        shard[number * local : (number + 1) * local] = rounded(qkv[number])
    shard[3 * local : 4 * local] = rounded(out[...])
    shard[4 * local :] = rounded(extra[...])


def pack_rest_kernel(token, qkv, out, up, down, own, feed_l, feed_v):
    local = out.shape[1]
    for stream, feed in enumerate((feed_l, feed_v)):
        for number in range(3):
            own[(4 * stream + number) * local : (4 * stream + number + 1) * local] = rounded(qkv[stream, number])
        own[(4 * stream + 3) * local : (4 * stream + 4) * local] = rounded(out[stream])
        for quarter in range(4):
            feed[quarter * local : (quarter + 1) * local] = rounded(up[stream, :, quarter * D : (quarter + 1) * D])
        feed[4 * local :] = rounded(down[stream])


def in_vmem(kernel, values, outs, scratch=()):
    return pl.pallas_call(
        kernel,
        out_shape=outs,
        in_specs=[pl.BlockSpec(memory_space=pltpu.VMEM)] * len(values),
        out_specs=[pl.BlockSpec(memory_space=pltpu.VMEM)] * len(outs),
        scratch_shapes=scratch,
        compiler_params=pltpu.CompilerParams(vmem_limit_bytes=60 * 1024 * 1024),
        cost_estimate=pl.CostEstimate(flops=0, bytes_accessed=1024, transcendentals=0),
        name=kernel.__name__,
    )(*values)


def finish(kernel, chunks, outs):
    return in_vmem(kernel, [term for chunk in chunks for term in chunk], outs)


def after(values, *others):
    return lax.optimization_barrier((values, *others))[0] if others else values


class Order:
    depths = {"x": 2, "y": 2, "core": 3, "one": 9, "two": 9, "three": 9}

    def __init__(self):
        self.kernel, self.last = [], []
        self.sent = {link: [] for link in self.depths}

    def ran(self, token, *beside):
        self.kernel, self.last = [token, *beside], []

    def use(self, values):
        return after(values, *self.kernel, *self.last)

    def settle(self, *values):
        self.last = [*self.last, *values]

    def did(self, values):
        self.last = [values]
        return values

    def send(self, link, values, axis, pairs, depth=None):
        sent, depth = self.sent[link], depth or self.depths[link]
        values = after(values, *self.kernel, *sent[max(len(sent) - depth, 0) : max(len(sent) - depth + 1, 0)])
        sent.append(lax.ppermute(values, axis, pairs))
        return sent[-1]

    def swap(self, link, values, depth=None):
        mask = {"core": 1, "x": 2, "y": 4}[link]
        return self.send(link, values, "fsdp", [(place, place ^ mask) for place in range(8)], depth)


def add_far_kernel(count, *refs):
    refs = Refs(refs)
    terms = [refs.take(2) for _ in range(count)]
    targets = refs.take(2)
    first = 0
    for keep, got in terms:
        rows = slice(first, first + keep.shape[2])
        first = rows.stop
        for side, target in enumerate(targets):
            target[rows] = rounded(plus(keep[0, side], got[0, side]))


def add_near_kernel(count, *refs):
    refs = Refs(refs)
    terms_x = [refs.take(2) for _ in range(count)]
    terms_y = [refs.take(2) for _ in range(count)]
    from_x, from_y, *targets = refs.refs
    joined = len(targets) == 2
    for number, (terms, side_more, more) in enumerate(((terms_x, 1, from_y), (terms_y, 0, from_x))):
        first = 0
        for keep, got in terms:
            rows = slice(first, first + keep.shape[2])
            first = rows.stop
            for side in range(2):
                extra = [more[rows]] if side == side_more else []
                target = targets[number].at[side] if joined else targets[2 * number + side].at[0]
                target[rows] = rounded(plus(keep[0, side], got[0, side], *extra))


def add_own_kernel(count, *refs):
    refs = Refs(refs)
    terms = [refs.take(2) for _ in range(count)]
    from_x, from_y = refs.take(2)
    first = 0
    for keep, got in terms:
        rows = slice(first, first + keep.shape[2])
        first = rows.stop
        for side in range(keep.shape[1]):
            target = refs.refs[0].at[side] if len(refs.refs) == 1 else refs.refs[side].at[0]
            target[rows] = rounded(plus(keep[0, side], got[0, side], from_x[side, rows], from_y[side, rows]))


def combine(kernel, places, keeps, gots, others, outs, side=None):
    half = keeps[0].shape[2]
    steps = half // 96 if half % 96 == 0 and len(keeps) == 1 else 1

    def spec(values, place=0):
        *more, rows, _ = values.shape
        if len(more) == 2:
            if side is not None:
                return pl.BlockSpec((1, 1, rows // steps, D), lambda block: (place, side, block, 0))
            return pl.BlockSpec((1, 2, rows // steps, D), lambda block: (place, 0, block, 0))
        return pl.BlockSpec((*more, rows // steps, D), lambda block: (*[0] * len(more), block, 0))

    terms = [term for keep, got in zip(keeps, gots) for term in (keep, got)]
    return pl.pallas_call(
        functools.partial(kernel, len(keeps)),
        grid=(steps,),
        in_specs=[spec(term, place) for place in places for term in terms] + [spec(leaf) for leaf in others],
        out_specs=[spec(leaf) for leaf in outs],
        out_shape=outs,
        compiler_params=pltpu.CompilerParams(vmem_limit_bytes=60 * 1024 * 1024),
        cost_estimate=pl.CostEstimate(flops=0, bytes_accessed=1024, transcendentals=0),
        name=kernel.__name__,
    )(*terms * len(places), *others)


class Gather:
    def __init__(self, order, shard, fars):
        self.order, self.shard, self.fars = order, shard, fars
        self.far_parts, self.far_cores = {}, {}

    def near(self, depth=1):
        self.near_x = self.order.swap("x", self.shard, depth)
        self.near_y = self.order.swap("y", self.shard, depth)

    def far(self, number=0):
        first, middle, last = self.fars[number]
        to_x = self.order.did(self.order.use(self.near_y)[first:middle])
        to_y = self.order.did(self.order.use(self.near_x)[middle:last])
        self.far_parts[number] = [self.order.swap("x", to_x), self.order.swap("y", to_y)]

    def own_core(self):
        self.own = self.order.swap("core", self.shard)

    def near_core(self):
        self.cores = [self.order.swap("core", piece) for piece in (self.near_x, self.near_y)]

    def far_core(self, number=0):
        self.far_cores[number] = [self.order.swap("core", self.order.use(piece)) for piece in self.far_parts[number]]

    def pieces(self, number=0, sides=(0, 1)):
        pieces = [self.shard, self.own]
        for piece, core in zip((self.near_x, self.near_y), self.cores):
            pieces += [piece, core]
        for side in sides:
            pieces += [self.far_parts[number][side], self.far_cores[number][side]]
        return pieces


class Line:
    def __init__(self, order):
        self.order = order

    def line(self, own):
        self.own = own
        self.order.did(own[0])
        self.one, self.two, self.three = [[None] * len(own) for _ in range(3)]

    def first(self):
        self.one = [self.order.send("one", own, "dp", [(0, 1), (3, 2)]) for own in self.own]

    def second(self, number=0):
        own = self.order.did(rounded(plus(self.own[number], self.order.use(self.one[number]))))
        self.two[number] = self.order.send("two", own, "dp", [(1, 2), (2, 1)])

    def third(self, number=0):
        own = self.order.did(rounded(plus(self.own[number], self.order.use(self.two[number]))))
        self.three[number] = self.order.send("three", own, "dp", [(1, 0), (2, 3)])

    def terms(self, number=0):
        terms = self.own[number], self.one[number], self.two[number], self.three[number]
        return [term.reshape(-1, D) for term in terms]


class Reduce(Line):
    def __init__(self, order, keep, send):
        super().__init__(order)
        self.half = keep.shape[1] // 2
        self.keeps = [keep.reshape(4, 2, self.half, D)]
        self.gots = [order.swap("core", send).reshape(4, 2, self.half, D)]

    def join(self, other):
        self.half += other.half
        self.keeps += other.keeps
        self.gots += other.gots

    def far(self):
        outs = [shape(self.half, D, dtype=BF)] * 2
        gots = [self.order.use(got) for got in self.gots]
        to_x, to_y = combine(add_far_kernel, (3,), self.keeps, gots, [], outs)
        self.order.did(to_x)
        self.from_x, self.from_y = self.order.swap("x", to_x), self.order.swap("y", to_y)

    def near(self, parts=1):
        outs = [shape(2 // parts, self.half, D, dtype=BF)] * (2 * parts)
        others = [self.order.use(self.from_x), self.from_y]
        made = combine(add_near_kernel, (1, 2), self.keeps, self.gots, others, outs)
        self.order.did(made[0])
        arrived = [[], []]
        for part in range(parts):
            for number, link in enumerate("xy"):
                arrived[number].append(self.order.swap(link, made[parts * number + part]))
        self.from_x, self.from_y = arrived

    def plane(self, parts):
        others = [self.order.use(self.from_x[0]), self.from_y[0]]
        outs = [shape(2 // parts, self.half, D, dtype=BF)] * parts
        self.line(combine(add_own_kernel, (0,), self.keeps, self.gots, others, outs))

    def plane_side(self, side):
        if side == 0:
            self.own, self.one, self.two, self.three = [[None] * 2 for _ in range(4)]
        others = [self.order.use(self.from_x[side]), self.from_y[side]]
        outs = [shape(1, self.half, D, dtype=BF)]
        self.own[side] = combine(add_own_kernel, (0,), self.keeps, self.gots, others, outs, side)[0]
        self.order.did(self.own[side])
        self.one[side] = self.order.send("one", self.own[side], "dp", [(0, 1), (3, 2)])


def body(
    language,
    vision,
    region_mask,
    cross_qkv,
    cross_out,
    cross_bias,
    cross_gain,
    self_qkv,
    self_out,
    self_bias,
    self_gain,
    ffn_up,
    ffn_up_bias,
    ffn_down,
    ffn_bias,
    ffn_gain,
    language_cotangent,
    vision_cotangent,
):
    plane, line = lax.axis_size("fsdp"), lax.axis_size("dp")
    swaps = plane == 8 and line == 4
    rank = lax.axis_index("fsdp")
    items, words, _ = language.shape
    regions = vision.shape[1]
    local = cross_gain.shape[0]
    counts = (items * words, items * regions)
    every = sum(counts)
    by_place = lambda values: values.transpose(1, 0, 2).reshape(-1, D)
    by_item = lambda values: values.reshape(-1, items, D).transpose(1, 0, 2)
    tangents = (by_place(language_cotangent), by_place(vision_cotangent))
    numbers = jnp.concatenate([rank.astype(jnp.int32)[None], jnp.sum(region_mask, axis=1)])

    if swaps:
        leaves = [cross_qkv, cross_out, cross_bias, cross_gain[None], self_bias, self_gain, ffn_bias, ffn_gain, ffn_up_bias]
        scratch = [pltpu.VMEM((VECTORS, D), F32)]
        cross_shard = in_vmem(pack_cross_kernel, leaves, [shape(4 * local + VECTORS, D, dtype=BF)], scratch)[0]
        rest = [self_qkv, self_out, ffn_up, ffn_down]
        token = lax.slice(cross_shard, (4 * local, 0), (4 * local + 16, 128))
        own_shard, *feed_shards = in_vmem(pack_rest_kernel, [token, *rest], [shape(8 * local, D, dtype=BF)] * 3)
        rows = 4 * local
        spans = [(place * local, local) for place in range(4)]
        cross_chunk = Chunk(8, True, True, rows + VECTORS, spans + [(rows, VECTORS)], 0, 2 * local)
        self_chunks = [Chunk(8, True, True, rows, spans, stream * rows) for stream in range(2)]
        feed_chunks = [Chunk(8, True, out, 2 * rows, spans + [(rows, rows)], 0, rows) for out in (False, True)]
        given = []
    else:
        small = jnp.concatenate(
            [cross_bias, cross_gain[None], self_bias.reshape(8, local), self_gain, ffn_bias.reshape(4, local), ffn_gain]
        )
        self_shards = [rounded(jnp.concatenate([self_qkv[s].reshape(3 * local, D), self_out[s]])) for s in range(2)]
        up_shards = [rounded(ffn_up[s]).reshape(local, 4, D).transpose(1, 0, 2).reshape(4 * local, D) for s in range(2)]
        down_shards = [rounded(ffn_down[s]) for s in range(2)]

        def gather(shard):
            whole = lax.all_gather(shard.reshape(4, local, D), "fsdp", axis=1, tiled=True)
            return whole.reshape(4, 4, D // 4, D).transpose(1, 0, 2, 3).reshape(4, D, D)

        cross_shard = rounded(jnp.concatenate([cross_qkv.reshape(3 * local, D), cross_out]))
        spans = [(place * D // 4, D // 4) for place in range(4)]
        cross_chunk = Chunk(4, False, False, D, spans)
        self_chunks = [Chunk(4, False, False, D, spans)] * 2
        feed_chunks = [Chunk(4, False, False, 2 * D, spans + [(D, D)])] * 2
        vectors = widened(lax.all_gather(rounded(small), "fsdp", axis=1, tiled=True))
        up_bias = widened(lax.all_gather(rounded(ffn_up_bias), "fsdp", axis=1, tiled=True)).reshape(8, D)
        given = [jnp.pad(vectors, ((0, VECTORS - NARROW), (0, 0))), up_bias]

    def biases(rows, keys):
        return pltpu.VMEM((rows, keys), F32)

    def kept(rows, keys):
        return shape(HEADS, rows, keys, dtype=BF)

    both = [biases(counts[0], counts[1]), biases(counts[1], counts[0])]

    def cross_forward(pieces):
        return run(
            functools.partial(cross_forward_kernel, cross_chunk, len(given)),
            "cross_forward",
            numbers,
            [by_place(language), by_place(vision), *given],
            pieces,
            [shape(counts[0], D), shape(counts[1], D), shape(every, D, dtype=BF), shape(every, D)]
            + [shape(every, D, dtype=BF)] * 4
            + [kept(counts[0], counts[1]), kept(counts[1], counts[0])]
            + [shape(VECTORS, D), shape(8, D)],
            [],
            [cross_chunk.held] + both + [cross_chunk.sems],
        )

    def self_forward(stream, inputs, vectors, pieces):
        count, chunk = counts[stream], self_chunks[stream]
        return run(
            functools.partial(self_forward_kernel, stream, chunk),
            f"self_forward_{stream}",
            numbers,
            [inputs, vectors],
            pieces,
            [shape(count, D)] * 2 + [shape(count, D, dtype=BF)] * 4 + [kept(count, count)],
            [],
            [chunk.held, biases(count, count), chunk.sems],
        )

    def feed(stream, inputs, vectors, up_bias, pieces):
        count, chunk = counts[stream], feed_chunks[stream]
        return run(
            functools.partial(feed_kernel, stream, chunk),
            f"feed_{stream}",
            numbers,
            [inputs, tangents[stream], vectors, up_bias],
            pieces,
            [shape(count, D, dtype=BF), shape(count, D), shape(8, D), shape(4, D)],
            chunk.targets,
            [chunk.held] * 2
            + [pltpu.VMEM((4, count, D), F32), pltpu.VMEM((4, count, D), BF)]
            + [pltpu.VMEM((count, D), F32)]
            + [chunk.sems] * 2,
        )

    def self_backward(stream, gradient, inputs, self_kept, vectors, pieces):
        count, chunk = counts[stream], self_chunks[stream]
        return run(
            functools.partial(self_backward_kernel, stream, chunk),
            f"self_backward_{stream}",
            numbers,
            [gradient, inputs, *self_kept, vectors],
            pieces,
            [shape(count, D), shape(8, D)],
            chunk.targets,
            [chunk.held] * 2 + [pltpu.VMEM((count, D), BF)] * 5 + [chunk.sems] * 2,
        )

    def cross_backward(gradients, cross_kept, vectors, smalls, pieces):
        chunk = cross_chunk
        return run(
            functools.partial(cross_backward_kernel, chunk),
            "cross_backward",
            numbers,
            [*gradients, *cross_kept, vectors, *smalls],
            pieces,
            [shape(counts[0], D), shape(counts[1], D)] + ([] if swaps else [shape(VECTORS, D), shape(8, D)]),
            chunk.targets,
            [chunk.held] * 2
            + [pltpu.VMEM((every, D), F32)] * 2
            + [pltpu.VMEM((VECTORS, D), F32)]
            + [pltpu.VMEM((every, D), BF)] * 5
            + [chunk.sems] * 2,
        )

    if swaps:
        order = Order()
        cross = Gather(order, cross_shard, [(0, 2 * local, rows + VECTORS)])
        own = Gather(order, own_shard, [(0, rows, 2 * rows)])
        feed_l, feed_v = [Gather(order, shard, [(0, rows, 2 * rows)]) for shard in feed_shards]
        cross.near()
        cross.own_core()
        order.did(own_shard)
        cross.far()
        own.near()
        cross.near_core()
        cross.far_core()
        made = cross_forward(cross.pieces())
        first_a, cross_kept, (vectors, up_bias) = made[:2], made[2:10], made[10:]
        order.ran(up_bias, own.near_x, own.near_y)

        own.far()
        own.own_core()
        own.near_core()
        feed_l.near()
        own.far_core()
        second_l = self_forward(0, first_a[0], order.use(vectors), own.pieces(0, (0,)))
        second_v = self_forward(1, after(first_a[1], second_l[0]), vectors, own.pieces(0, (1,)))
        order.ran(second_v[0], feed_l.near_x, feed_l.near_y)

        feed_l.far()
        feed_l.own_core()
        feed_l.near_core()
        feed_v.near()
        feed_l.far_core()
        fed_l = feed(0, second_l[0], order.use(vectors), up_bias, feed_l.pieces())
        order.ran(fed_l[2])

        feed_v.own_core()
        back_l = self_backward(0, fed_l[1], first_a[0], second_l[1:], order.use(vectors), own.pieces(0, (0,)))
        order.ran(back_l[1], feed_v.near_x, feed_v.near_y, feed_v.own)
        summed_l = lax.psum_scatter(order.use(fed_l[4]), "fsdp", scatter_dimension=0)

        feed_v.far()
        feed_v.near_core()
        sum_self_l = Reduce(order, *back_l[2:])
        sum_self_l.far()
        feed_v.far_core()
        fed_v = feed(1, second_v[0], order.use(vectors), up_bias, feed_v.pieces())
        order.ran(fed_v[2], sum_self_l.from_x, sum_self_l.from_y)

        sum_self_l.near()
        sum_feed_v = Reduce(order, *fed_v[4:])
        back_v = self_backward(1, fed_v[1], first_a[1], second_v[1:], order.use(vectors), own.pieces(0, (1,)))
        order.ran(back_v[1], *sum_self_l.from_x, *sum_self_l.from_y, *sum_feed_v.gots)

        sum_feed_v.far()
        sum_last = Reduce(order, *back_v[2:])
        sum_self_l.plane(1)
        sum_self_l.first()
        smalls = [back_l[1], back_v[1], fed_l[2], fed_v[2], fed_l[3], fed_v[3]]
        made = cross_backward([back_l[0], back_v[0]], cross_kept, order.use(vectors), smalls, cross.pieces())
        gradients = made[:2]
        order.ran(made[1], sum_feed_v.from_x, sum_feed_v.from_y, *sum_self_l.one, *sum_last.gots)

        sum_feed_l = Line(order)
        sum_feed_l.line([order.use(summed_l)])
        sum_feed_l.first()
        sum_last.join(Reduce(order, *made[2:]))
        sum_feed_v.near()
        sum_self_l.second()
        sum_last.far()
        sum_feed_l.second()
        sum_self_l.third()
        sum_feed_v.plane(2)
        sum_feed_v.first()
        sum_last.near()
        sum_feed_v.second(0)
        sum_feed_l.third()
        sum_feed_v.second(1)
        sum_last.plane(2)
        sum_last.first()
        sum_feed_v.third(0)
        order.settle(*sum_feed_l.three)
        sum_last.second(0)
        order.settle(*sum_self_l.three)
        sum_feed_v.third(1)
        sum_last.second(1)
        order.settle(sum_feed_v.three[0])
        sum_last.third(0)
        order.settle(sum_feed_v.three[1])
        sum_last.third(1)
        feed_terms = [sum_feed_l.terms()] + [sum_feed_v.terms(number) for number in range(2)]
        feed_terms[0][0] = order.use(feed_terms[0][0])
        feed_grads = finish(finish_feed_kernel, feed_terms, [shape(*ffn_up.shape), shape(*ffn_down.shape)])
        leaves = [self_qkv, self_out, cross_qkv, cross_out, cross_bias, cross_gain[None], self_bias, self_gain]
        leaves += [ffn_up_bias, ffn_bias, ffn_gain]
        last_terms = [sum_self_l.terms()] + [sum_last.terms(number) for number in range(2)]
        last_terms[0][0] = after(last_terms[0][0], feed_grads[0])
        rest = finish(finish_rest_kernel, last_terms, [shape(*leaf.shape) for leaf in leaves])
        grads = [*rest[2:5], rest[5][0], *rest[:2], *rest[6:8], feed_grads[0], rest[8], feed_grads[1], *rest[9:]]
        outputs = fed_l[0], fed_v[0]
    else:
        cross_pieces = [gather(cross_shard)]
        self_pieces = [[gather(shard)] for shard in self_shards]
        feed_pieces = []
        for up, down in zip(up_shards, down_shards):
            down = lax.all_gather(down, "fsdp", axis=0, tiled=True).reshape(4, D, D)
            feed_pieces.append([jnp.concatenate([gather(up), down], axis=1)])
        made = cross_forward(cross_pieces)
        first_a, cross_kept, (vectors, up_bias) = made[:2], made[2:10], made[10:]
        second = [self_forward(s, first_a[s], vectors, self_pieces[s]) for s in range(2)]
        fed = [feed(s, second[s][0], vectors, up_bias, feed_pieces[s]) for s in range(2)]
        back = [self_backward(s, fed[s][1], first_a[s], second[s][1:], vectors, self_pieces[s]) for s in range(2)]
        smalls = [back[0][1], back[1][1], fed[0][2], fed[1][2], fed[0][3], fed[1][3]]
        made = cross_backward([back[0][0], back[1][0]], cross_kept, vectors, smalls, cross_pieces)
        gradients = made[:2]
        outputs = fed[0][0], fed[1][0]

        def whole(grad, by_owner=True):
            if by_owner:
                grad = grad.reshape(4, 4, D // 4, D).transpose(1, 0, 2, 3).reshape(4, D, D)
                own = lax.psum_scatter(grad, "fsdp", scatter_dimension=1, tiled=True)
            else:
                own = lax.psum_scatter(grad.reshape(4 * D, D), "fsdp", scatter_dimension=0, tiled=True)
            return widened(lax.psum(own, "dp")).reshape(4 * local, D)

        up_done = [whole(made_s[4][:, :D]) for made_s in fed]
        down_done = [whole(made_s[4][:, D:], False) for made_s in fed]
        self_done = [whole(made_s[2]) for made_s in back]
        cross_done = whole(made[4])
        small = lax.dynamic_slice(lax.psum(made[2], ("fsdp", "dp")), (0, rank * local), (NARROW, local))
        up_small = lax.psum(made[3], ("fsdp", "dp")).reshape(2, 4 * D)
        up_small = lax.dynamic_slice(up_small, (0, 4 * rank * local), (2, 4 * local))
        up_grads = [done.reshape(4, local, D).transpose(1, 0, 2).reshape(local, 4 * D) for done in up_done]
        grads = [cross_done[: 3 * local].reshape(3, local, D), cross_done[3 * local :], small[0:4], small[4]]
        grads += [jnp.stack([done[: 3 * local].reshape(3, local, D) for done in self_done])]
        grads += [jnp.stack([done[3 * local :] for done in self_done])]
        grads += [small[5:13].reshape(2, 4, local), small[13:15], jnp.stack(up_grads), up_small, jnp.stack(down_done)]
        grads += [small[15:19].reshape(2, 2, local), small[19:21]]

    return (*[by_item(rows) for rows in (*outputs, *gradients)], *grads)


def solution(mesh):
    return jax.shard_map(
        body,
        mesh=mesh,
        in_specs=(
            P(("fsdp", "dp"), None, None),
            P(("fsdp", "dp"), None, None),
            P(("fsdp", "dp"), None),
            P(None, "fsdp", None),
            P("fsdp", None),
            P(None, "fsdp"),
            P("fsdp"),
            P(None, None, "fsdp", None),
            P(None, "fsdp", None),
            P(None, None, "fsdp"),
            P(None, "fsdp"),
            P(None, "fsdp", None),
            P(None, "fsdp"),
            P(None, "fsdp", None),
            P(None, None, "fsdp"),
            P(None, "fsdp"),
            P(("fsdp", "dp"), None, None),
            P(("fsdp", "dp"), None, None),
        ),
        out_specs=(
            P(("fsdp", "dp"), None, None),
            P(("fsdp", "dp"), None, None),
            P(("fsdp", "dp"), None, None),
            P(("fsdp", "dp"), None, None),
            P(None, "fsdp", None),
            P("fsdp", None),
            P(None, "fsdp"),
            P("fsdp"),
            P(None, None, "fsdp", None),
            P(None, "fsdp", None),
            P(None, None, "fsdp"),
            P(None, "fsdp"),
            P(None, "fsdp", None),
            P(None, "fsdp"),
            P(None, "fsdp", None),
            P(None, None, "fsdp"),
            P(None, "fsdp"),
        ),
        check_vma=False,
    )
```

```python
import functools

import jax
import jax.numpy as jnp
from jax import lax
from jax.experimental import pallas as pl
from jax.experimental.pallas import tpu as pltpu
from jax.sharding import PartitionSpec as P

HEADS = 12
HEAD_DIM = 64
PAIR = 2 * HEAD_DIM
D = HEADS * HEAD_DIM
NARROW = 21
VECTORS = 32
BLOCK = 256
VMEM_MIB = dict(cross_forward=60, self_forward_0=60, self_forward_1=60, feed_0=60, feed_1=60)
VMEM_MIB.update(self_backward_0=60, self_backward_1=60, cross_backward=60)

epsilon = 1e-06
hidden_score = -1e30

BF = jnp.bfloat16
F32 = jnp.float32


def rounded(values):
    return values.astype(BF)


def widened(values):
    return values.astype(F32)


def shape(*sizes, dtype=F32):
    return jax.ShapeDtypeStruct(sizes, dtype)


def plus(*values):
    total = widened(values[0])
    for value in values[1:]:
        total = total + widened(value)
    return total


def mm(left, right):
    return jnp.dot(left, right, preferred_element_type=F32)


def mm_nt(left, right):
    return lax.dot_general(left, right, (((1,), (1,)), ((), ())), preferred_element_type=F32)


def mm_tn(left, right):
    return lax.dot_general(left, right, (((0,), (0,)), ((), ())), preferred_element_type=F32)


def flat(block):
    return block.reshape(block.shape[0] * block.shape[1], block.shape[2])


def column_sum(values):
    return jnp.sum(values, axis=0, keepdims=True)


def blocks():
    return [slice(start, start + BLOCK) for start in range(0, D, BLOCK)]


def norm_forward(total, gain, shift):
    centre = total - jnp.mean(total, axis=-1, keepdims=True)
    spread = jnp.mean(centre * centre, axis=-1, keepdims=True)
    return centre * lax.rsqrt(spread + epsilon) * gain + shift


def norm_backward(total, gradient, gain):
    centre = total - jnp.mean(total, axis=-1, keepdims=True)
    spread = jnp.mean(centre * centre, axis=-1, keepdims=True)
    scale = lax.rsqrt(spread + epsilon)
    unit = centre * scale
    inner = gradient * gain
    mean_inner = jnp.mean(inner, axis=-1, keepdims=True)
    mean_product = jnp.mean(inner * unit, axis=-1, keepdims=True)
    back = scale * (inner - mean_inner - unit * mean_product)
    return back, column_sum(gradient * unit), column_sum(gradient)


def place_of(extent, axis, items):
    number = lax.broadcasted_iota(jnp.int32, extent, axis).astype(F32)
    place = jnp.floor((number + 0.5) * (1.0 / items))
    return number - place * items, place


def present_item(extent, axis, counts):
    item, place = place_of(extent, axis, len(counts))
    limit = jnp.zeros_like(place)
    for number, count in enumerate(counts):
        limit = jnp.where(item == number, count.astype(F32), limit)
    return jnp.where(place < limit, item, -1.0)


def fill_bias(bias, items, counts=None):
    rows, keys = bias.shape
    key_item = place_of((1, keys), 1, items)[0] if counts is None else present_item((1, keys), 1, counts)
    bias[...] = jnp.where(place_of((rows, 1), 0, items)[0] == key_item, 0.0, hidden_score)


def attend(query, key, value, context, query_rows, key_rows, bias, kept):
    low = lax.broadcasted_iota(jnp.int32, (1, PAIR), 1) < HEAD_DIM
    for number in range(HEADS // 2):
        columns = slice(number * PAIR, (number + 1) * PAIR)
        rows, others = query_rows, key_rows
        queries = query[rows, columns] * HEAD_DIM ** (-0.5)
        keys = key[others, columns]
        values = value[others, columns]
        total = None
        for side, half in enumerate((low, ~low)):
            scores = mm_nt(jnp.where(half, queries, 0), keys) + bias[...]
            shifted = jnp.exp(scores - jnp.max(scores, axis=-1, keepdims=True))
            weight = rounded(shifted / jnp.sum(shifted, axis=-1, keepdims=True))
            kept[2 * number + side] = weight
            found = mm(weight, jnp.where(half, values, 0))
            total = found if total is None else total + found
        context[rows, columns] = rounded(total)


def attend_back(query, key, value, kept, d_context, query_rows, key_rows, d_query, d_key, d_value):
    low = lax.broadcasted_iota(jnp.int32, (1, PAIR), 1) < HEAD_DIM
    scale = HEAD_DIM ** (-0.5)
    for number in range(HEADS // 2):
        columns = slice(number * PAIR, (number + 1) * PAIR)
        rows, others = query_rows, key_rows
        queries = query[rows, columns] * scale
        keys = key[others, columns]
        values = value[others, columns]
        arriving = d_context[rows, columns]
        sums = [None] * 3
        for side, half in enumerate((low, ~low)):
            own_arriving = jnp.where(half, arriving, 0)
            weight = kept[2 * number + side]
            d_weight = mm_nt(own_arriving, values)
            weighed = d_weight * weight
            inner = jnp.sum(weighed, axis=-1, keepdims=True)
            d_scores = rounded(weighed - weight * inner)
            found = [
                mm(d_scores, jnp.where(half, keys * scale, 0)),
                mm_tn(d_scores, jnp.where(half, queries, 0)),
                mm_tn(weight, own_arriving),
            ]
            sums = [one if total is None else total + one for one, total in zip(found, sums)]
        d_query[rows, columns] = rounded(sums[0])
        d_key[others, columns] = rounded(sums[1])
        d_value[others, columns] = rounded(sums[2])


def shift_matrix(owner, local):
    row = lax.broadcasted_iota(jnp.int32, (128, D), 0)
    column = lax.broadcasted_iota(jnp.int32, (128, D), 1)
    return jnp.where((column == row + owner * local) & (row < local), 1.0, 0.0).astype(BF)


class Chunk:
    def __init__(self, owners, split_in, split_out, rows, spans, base=0, middle=None, cut=None):
        self.owners, self.split_in, self.split_out, self.rows, self.spans = owners, split_in, split_out, rows, spans
        self.base, self.middle, self.cut = base, middle, cut
        self.sources = (8 if middle is None else 10) if split_in else 1
        sizes = [rows] if cut is None else [cut, rows - cut]
        self.targets = [shape(owners, rows, D, dtype=BF)]
        if split_out:
            self.targets = [shape(4, size, D, dtype=BF) for size in sizes for _ in range(2)]
        self.held = pltpu.VMEM((owners, rows, D), BF)
        self.sems = pltpu.SemaphoreType.DMA((len(spans), owners))

    def load(self, me, sources, held, sems, order):
        copies = {}
        for number in order:
            start, size = self.spans[number]
            span = pl.ds(start, size)
            copies[number] = []
            for place in range(8 if self.split_in else 1):
                sem = sems.at[number, place]
                if not self.split_in:
                    copies[number].append(pltpu.make_async_copy(sources[0].at[:, span], held.at[:, span], sem))
                    continue
                pieces = [(start, size)]
                if place > 5 and self.middle is not None and start < self.middle < start + size:
                    pieces = [(start, self.middle - start), (self.middle, start + size - self.middle)]
                for first, count in pieces:
                    if place < 6:
                        source = sources[place].at[pl.ds(self.base + first, count)]
                    elif self.middle is None:
                        source = sources[place].at[pl.ds(first, count)]
                    else:
                        above = first >= self.middle
                        source = sources[place + 2 * above].at[pl.ds(first - self.middle * above, count)]
                    copies[number].append(pltpu.make_async_copy(source, held.at[me ^ place, pl.ds(first, count)], sem))
            for copy in copies[number]:
                copy.start()

        def wait(number):
            for copy in copies[number]:
                copy.wait()

        return wait

    def copy_out(self, me, grad, targets, sem, owner, span, action):
        if not self.split_out:
            span = pl.ds(*span)
            action(pltpu.make_async_copy(grad.at[owner, span], targets[0].at[owner, span], sem))
            return
        place = me ^ owner
        first, size = span
        second = self.cut is not None and first >= self.cut
        there = pl.ds(first - (self.cut if second else 0), size)
        span = pl.ds(first, size)
        for target, odd in zip(targets[2:] if second else targets, (0, 1)):

            @pl.when(lax.rem(place, 2) == odd)
            def _():
                action(pltpu.make_async_copy(grad.at[owner, span], target.at[place // 2, there], sem))

    def store(self, me, grad, targets, sems, number, owners=None):
        span = self.spans[number]
        owners = range(self.owners) if owners is None else owners
        for owner in owners:
            self.copy_out(me, grad, targets, sems.at[number, owner], owner, span, lambda copy: copy.start())

        def wait():
            for owner in owners:
                self.copy_out(me, grad, targets, sems.at[number, owner], owner, span, lambda copy: copy.wait())

        return wait

    def matrix(self, held, number, columns=slice(None)):
        start, size = self.spans[number]
        return flat(held[:, start : start + size, columns])

    def put(self, grad, number, columns, values):
        start, size = self.spans[number]
        grad[:, start : start + size, columns] = rounded(values).reshape(self.owners, size, values.shape[1])


def run(kernel, name, numbers, values, pieces, outs, targets, scratch):
    in_specs = [pl.BlockSpec(memory_space=pltpu.SMEM)]
    in_specs += [pl.BlockSpec(memory_space=pltpu.VMEM)] * len(values)
    in_specs += [pl.BlockSpec(memory_space=pl.ANY)] * len(pieces)
    out_specs = [pl.BlockSpec(memory_space=pltpu.VMEM)] * len(outs)
    out_specs += [pl.BlockSpec(memory_space=pl.ANY)] * len(targets)
    return pl.pallas_call(
        kernel,
        out_shape=outs + targets,
        in_specs=in_specs,
        out_specs=out_specs,
        scratch_shapes=scratch,
        compiler_params=pltpu.CompilerParams(vmem_limit_bytes=VMEM_MIB[name] * 1024 * 1024),
        cost_estimate=pl.CostEstimate(flops=0, bytes_accessed=1024, transcendentals=0),
        name=name,
    )(numbers, *values, *pieces)


class Refs:
    def __init__(self, refs):
        self.refs = list(refs)

    def take(self, count):
        taken, self.refs = self.refs[:count], self.refs[count:]
        return taken


def cross_forward_kernel(chunk, given, *refs):
    refs = Refs(refs)
    numbers, language, vision = refs.take(3)
    given = refs.take(given)
    sources = refs.take(chunk.sources)
    language_a, vision_a, rows_in, total, query, key, value, context, kept_l, kept_v, vectors, up_bias = refs.take(12)
    held, bias_l, bias_v, sems = refs.take(4)
    me = numbers[0]
    wait = chunk.load(me, sources, held, sems, [*range(4, len(chunk.spans)), *range(4)])
    split, every = language.shape[0], rows_in.shape[0]
    own = (slice(0, split), slice(split, every))
    rows_in[own[0]] = language[...]
    rows_in[own[1]] = vision[...]
    counts = [numbers[item] for item in range(1, numbers.shape[0])]
    fill_bias(bias_l, len(counts), counts)
    fill_bias(bias_v, len(counts))
    if chunk.split_in:
        local = D // 8
        wait(4)
        extra = slice(chunk.spans[4][0], chunk.rows)
        found = None
        for owner in range(8):
            moved = mm(held[owner, extra, :128], shift_matrix(owner, local))
            found = moved if found is None else found + moved
        vectors[...] = found
        for quarter in range(4):
            wide = [widened(held[2 * quarter + side, extra, : D // 2]) for side in range(2)]
            wide = jnp.concatenate(wide, axis=1)
            for stream in range(2):
                line = NARROW + stream
                up_bias[4 * stream + quarter : 4 * stream + quarter + 1, :] = wide[line : line + 1]
    else:
        vectors[...] = given[0][...]
        up_bias[...] = given[1][...]
    for number, target in enumerate((query, key, value)):
        wait(number)
        for columns in blocks():
            found = mm(rows_in[...], chunk.matrix(held, number, columns))
            if number != 1:
                line = number // 2
                found = found + vectors[line : line + 1, columns]
            target[:, columns] = rounded(found)
    attend(query, key, value, context, own[0], own[1], bias_l, kept_l)
    attend(query, key, value, context, own[1], own[0], bias_v, kept_v)
    wait(3)
    for columns in blocks():
        branch = mm(context[...], chunk.matrix(held, 3, columns)) + vectors[2:3, columns]
        total[:, columns] = widened(rows_in[:, columns]) + branch
    for rows, target in zip(own, (language_a, vision_a)):
        target[...] = norm_forward(total[rows], vectors[4:5], vectors[3:4])


def self_forward_kernel(stream, chunk, *refs):
    refs = Refs(refs)
    numbers, inputs, vectors = refs.take(3)
    sources = refs.take(chunk.sources)
    outputs, total, query, key, value, context, kept = refs.take(7)
    held, bias, sems = refs.take(3)
    wait = chunk.load(numbers[0], sources, held, sems, range(4))
    rows = inputs.shape[0]
    counts = [numbers[item] for item in range(1, numbers.shape[0])]
    fill_bias(bias, len(counts), counts if stream else None)
    first = 5 + 4 * stream
    low_inputs = rounded(inputs[...])
    for number, target in enumerate((query, key, value)):
        wait(number)
        for columns in blocks():
            found = mm(low_inputs, chunk.matrix(held, number, columns))
            if number != 1:
                line = first + number // 2
                found = found + vectors[line : line + 1, columns]
            target[:, columns] = rounded(found)
    every = slice(0, rows)
    attend(query, key, value, context, every, every, bias, kept)
    wait(3)
    for columns in blocks():
        branch = mm(context[...], chunk.matrix(held, 3, columns)) + vectors[first + 2 : first + 3, columns]
        total[:, columns] = inputs[:, columns] + branch
    gain = 13 + stream
    outputs[...] = norm_forward(total[...], vectors[gain : gain + 1], vectors[first + 3 : first + 4])


def feed_kernel(stream, chunk, *refs):
    refs = Refs(refs)
    numbers, inputs, cotangent, vectors, up_bias = refs.take(5)
    sources = refs.take(chunk.sources)
    outputs, d_inputs, small, d_up_bias = refs.take(4)
    targets = refs.take(len(chunk.targets))
    held, grad, slope, hidden, total, sems, out_sems = refs.take(7)
    me = numbers[0]
    wait = chunk.load(me, sources, held, sems, (0, 4, 1, 2, 3))
    owners = chunk.owners // 4
    local = D // chunk.owners
    line = 15 + 2 * stream
    gain = vectors[19 + stream : 20 + stream]
    low_inputs = rounded(inputs[...])

    def down_matrix(quarter):
        return flat(held[quarter * owners : (quarter + 1) * owners, 4 * local :, :])

    total[...] = inputs[...] + vectors[line : line + 1]
    for quarter in range(4):
        wait(quarter)
        for columns in blocks():
            before = mm(low_inputs, chunk.matrix(held, quarter, columns))
            before = before + up_bias[4 * stream + quarter : 4 * stream + quarter + 1, columns]
            spread = 0.5 * (1.0 + lax.erf(before * 0.5**0.5))
            slope[quarter, :, columns] = spread + before * jnp.exp(-0.5 * before * before) * (0.5 / 3.141592653589793) ** 0.5
            hidden[quarter, :, columns] = rounded(before * spread)
        if quarter == 0:
            wait(4)
        total[...] += mm(hidden[quarter], down_matrix(quarter))
    arriving = widened(cotangent[...])
    found = norm_forward(total[...], gain, vectors[line + 1 : line + 2])
    if stream:
        counts = [numbers[item] for item in range(1, numbers.shape[0])]
        mask = jnp.where(present_item((inputs.shape[0], 1), 0, counts) < 0, 0.0, 1.0)
        found = found * mask
        arriving = arriving * mask
    back, d_gain, d_shift = norm_backward(total[...], arriving, gain)
    outputs[...] = rounded(found)
    d_inputs[...] = back
    low_back = rounded(back)
    small[...] = jnp.zeros_like(small)
    small[0:1] = column_sum(widened(low_back))
    small[1:2] = d_shift
    small[2:3] = d_gain
    pending = []
    for quarter in range(4):
        d_hidden = mm_nt(low_back, down_matrix(quarter))
        d_before = rounded(d_hidden * slope[quarter])
        d_up_bias[quarter : quarter + 1, :] = column_sum(widened(d_before))
        for columns in blocks():
            found = rounded(mm_tn(hidden[quarter], low_back[:, columns]))
            grad[quarter * owners : (quarter + 1) * owners, 4 * local :, columns] = found.reshape(owners, 4 * local, BLOCK)
        pending.append(chunk.store(me, grad, targets, out_sems, 4, range(quarter * owners, (quarter + 1) * owners)))
        for columns in blocks():
            chunk.put(grad, quarter, columns, mm_tn(low_inputs, d_before[:, columns]))
        pending.append(chunk.store(me, grad, targets, out_sems, quarter))
        d_inputs[...] += mm_nt(d_before, chunk.matrix(held, quarter))
    for finish in pending:
        finish()


def layer_back(chunk, total, context, held, gain, d_norm, d_inputs, grad, d_context, low_back, wait):
    back, d_gain, d_shift = norm_backward(total, d_norm, gain)
    d_inputs[...] = back
    low_back[...] = rounded(back)
    wait(3)
    d_context[...] = rounded(mm_nt(low_back[...], chunk.matrix(held, 3)))
    for columns in blocks():
        chunk.put(grad, 3, columns, mm_tn(context[...], low_back[:, columns]))
    return d_gain, d_shift, column_sum(widened(low_back[...]))


def projections_back(chunk, low_inputs, held, grad, d_all, d_inputs, wait, store):
    pending = []
    for number, gradient in enumerate(d_all):
        for columns in blocks():
            chunk.put(grad, number, columns, mm_tn(low_inputs, gradient[:, columns]))
        pending.append(store(number))
    for number, gradient in enumerate(d_all):
        wait(number)
        d_inputs[...] += mm_nt(gradient[...], chunk.matrix(held, number))
    return pending


def self_backward_kernel(stream, chunk, *refs):
    refs = Refs(refs)
    numbers, d_outputs, inputs, total, query, key, value, context, kept, vectors = refs.take(10)
    sources = refs.take(chunk.sources)
    d_inputs, small = refs.take(2)
    targets = refs.take(len(chunk.targets))
    held, grad, d_context, low_back, d_query, d_key, d_value, sems, out_sems = refs.take(9)
    me = numbers[0]
    wait = chunk.load(me, sources, held, sems, (3, 0, 1, 2))
    store = functools.partial(chunk.store, me, grad, targets, out_sems)
    rows = inputs.shape[0]
    low_inputs = rounded(inputs[...])
    gain = vectors[13 + stream : 14 + stream]
    d_gain, d_shift, d_out = layer_back(
        chunk, total[...], context, held, gain, d_outputs[...], d_inputs, grad, d_context, low_back, wait
    )
    pending = [store(3)]
    every = slice(0, rows)
    attend_back(query, key, value, kept, d_context, every, every, d_query, d_key, d_value)
    pending += projections_back(chunk, low_inputs, held, grad, (d_query, d_key, d_value), d_inputs, wait, store)
    small[...] = jnp.zeros_like(small)
    lines = (column_sum(widened(d_query[...])), column_sum(widened(d_value[...])), d_out, d_shift, d_gain)
    for place, line in enumerate(lines):
        small[place : place + 1] = line
    for finish in pending:
        finish()


def cross_backward_kernel(chunk, *refs):
    refs = Refs(refs)
    numbers, d_language, d_vision, rows_in, total, query, key, value, context, kept_l, kept_v, vectors = refs.take(12)
    self_l, self_v, feed_l, feed_v = refs.take(4)
    ups = refs.take(2)
    sources = refs.take(chunk.sources)
    language_gradient, vision_gradient = refs.take(2)
    if not chunk.split_out:
        small_out, up_out = refs.take(2)
    targets = refs.take(len(chunk.targets))
    held, grad, d_norm, d_inputs, lines = refs.take(5)
    d_context, low_back, d_query, d_key, d_value, sems, out_sems = refs.take(7)
    me = numbers[0]
    wait = chunk.load(me, sources, held, sems, (3, 0, 1, 2))
    store = functools.partial(chunk.store, me, grad, targets, out_sems)
    split, every = language_gradient.shape[0], rows_in.shape[0]
    own = (slice(0, split), slice(split, every))
    d_norm[own[0]] = d_language[...]
    d_norm[own[1]] = d_vision[...]
    d_gain, d_shift, d_out = layer_back(
        chunk, total[...], context, held, vectors[4:5], d_norm[...], d_inputs, grad, d_context, low_back, wait
    )
    pending = [store(3)]
    attend_back(query, key, value, kept_l, d_context, own[0], own[1], d_query, d_key, d_value)
    attend_back(query, key, value, kept_v, d_context, own[1], own[0], d_query, d_key, d_value)
    found = (column_sum(widened(d_query[...])), column_sum(widened(d_value[...])), d_out, d_shift, d_gain)
    lines[...] = jnp.zeros_like(lines)
    for place, line in enumerate(found):
        lines[place : place + 1] = line
    moves = [(self_l, place, 5 + place) for place in range(4)] + [(self_v, place, 9 + place) for place in range(4)]
    moves += [(self_l, 4, 13), (self_v, 4, 14), (feed_l, 0, 15), (feed_l, 1, 16), (feed_v, 0, 17), (feed_v, 1, 18)]
    moves += [(feed_l, 2, 19), (feed_v, 2, 20)]
    for source, place, target in moves:
        lines[target : target + 1] = source[place : place + 1]
    if chunk.split_out:
        local = D // 8
        low_lines = rounded(lines[...])
        zeros = jnp.zeros((1, D // 2), F32)
        for owner in range(8):
            narrow = mm_nt(low_lines, shift_matrix(owner, local))
            block = jnp.concatenate([narrow, jnp.zeros((VECTORS, D - 128), F32)], axis=1)
            side = slice(owner % 2 * (D // 2), (owner % 2 + 1) * (D // 2))
            for stream in range(2):
                wide = ups[stream][owner // 2 : owner // 2 + 1, side]
                wide = jnp.concatenate([wide, zeros], axis=1)
                here = lax.broadcasted_iota(jnp.int32, (VECTORS, 1), 0) == NARROW + stream
                block = jnp.where(here, wide, block)
            grad[owner, chunk.spans[4][0] : chunk.rows, :] = rounded(block)
        pending += [store(4)]
    else:
        small_out[...] = lines[...]
        up_out[0:4] = ups[0][0:4]
        up_out[4:8] = ups[1][0:4]
    pending += projections_back(chunk, rows_in[...], held, grad, (d_query, d_key, d_value), d_inputs, wait, store)
    language_gradient[...] = d_inputs[own[0]]
    vision_gradient[...] = d_inputs[own[1]]
    for finish in pending:
        finish()


def finish_feed_kernel(*refs):
    refs = Refs(refs)
    terms_l, up_v, down_v = refs.take(4), refs.take(4), refs.take(4)
    up_grad, down_grad = refs.take(2)
    local = up_grad.shape[1]
    for quarter in range(4):
        rows, columns = slice(quarter * local, (quarter + 1) * local), slice(quarter * D, (quarter + 1) * D)
        up_grad[0, :, columns] = plus(*[term[rows] for term in terms_l])
        up_grad[1, :, columns] = plus(*[term[rows] for term in up_v])
    down_grad[0] = plus(*[term[4 * local :] for term in terms_l])
    down_grad[1] = plus(*[term[...] for term in down_v])


def finish_rest_kernel(*refs):
    refs = Refs(refs)
    terms_l = refs.take(4)
    sides = [refs.take(4) for _ in range(2)]
    self_qkv, self_out, qkv, out, bias, gain, self_bias, self_gain, up_bias, feed_bias, feed_gain = refs.take(11)
    local = out.shape[0]
    found = [plus(*[term[...] for term in terms]) for terms in sides]
    for stream in range(2):
        for number in range(4):
            target = self_out.at[stream] if number == 3 else self_qkv.at[stream, number]
            if stream:
                target[...] = found[number // 2][number % 2 * local : (number % 2 + 1) * local]
            else:
                target[...] = plus(*[term[number * local : (number + 1) * local] for term in terms_l])
    start = 2 * local
    for number in range(2):
        qkv[number] = found[0][start + number * local : start + (number + 1) * local]
    above = VECTORS // 2
    qkv[2, :above] = found[0][start + 2 * local :]
    qkv[2, above:] = found[1][start : start + local - above]
    out[...] = found[1][start + local - above : start + 2 * local - above]
    small = found[1][start + 2 * local - above :]
    bias[...] = small[0:4, :local]
    gain[...] = small[4:5, :local]
    for stream in range(2):
        self_bias[stream] = small[5 + 4 * stream : 9 + 4 * stream, :local]
        self_gain[stream : stream + 1] = small[13 + stream : 14 + stream, :local]
        feed_bias[stream] = small[15 + 2 * stream : 17 + 2 * stream, :local]
        feed_gain[stream : stream + 1] = small[19 + stream : 20 + stream, :local]
        up_bias[stream : stream + 1] = small[NARROW + stream : NARROW + stream + 1, : 4 * local]


def pack_cross_kernel(qkv, out, bias, gain, self_bias, self_gain, feed_bias, feed_gain, up_bias, shard, extra):
    local = out.shape[0]
    extra[...] = jnp.zeros_like(extra)
    extra[0:4, :local] = bias[...]
    extra[4:5, :local] = gain[...]
    for stream in range(2):
        extra[5 + 4 * stream : 9 + 4 * stream, :local] = self_bias[stream]
        extra[13 + stream : 14 + stream, :local] = self_gain[stream : stream + 1]
        extra[15 + 2 * stream : 17 + 2 * stream, :local] = feed_bias[stream]
        extra[19 + stream : 20 + stream, :local] = feed_gain[stream : stream + 1]
        extra[NARROW + stream : NARROW + stream + 1, : 4 * local] = up_bias[stream : stream + 1]
    for number in range(3):
        shard[number * local : (number + 1) * local] = rounded(qkv[number])
    shard[3 * local : 4 * local] = rounded(out[...])
    shard[4 * local :] = rounded(extra[...])


def pack_rest_kernel(token, qkv, out, up, down, own, feed_l, feed_v):
    local = out.shape[1]
    for stream, feed in enumerate((feed_l, feed_v)):
        for number in range(3):
            own[(4 * stream + number) * local : (4 * stream + number + 1) * local] = rounded(qkv[stream, number])
        own[(4 * stream + 3) * local : (4 * stream + 4) * local] = rounded(out[stream])
        for quarter in range(4):
            feed[quarter * local : (quarter + 1) * local] = rounded(up[stream, :, quarter * D : (quarter + 1) * D])
        feed[4 * local :] = rounded(down[stream])


def in_vmem(kernel, values, outs, scratch=()):
    return pl.pallas_call(
        kernel,
        out_shape=outs,
        in_specs=[pl.BlockSpec(memory_space=pltpu.VMEM)] * len(values),
        out_specs=[pl.BlockSpec(memory_space=pltpu.VMEM)] * len(outs),
        scratch_shapes=scratch,
        compiler_params=pltpu.CompilerParams(vmem_limit_bytes=60 * 1024 * 1024),
        cost_estimate=pl.CostEstimate(flops=0, bytes_accessed=1024, transcendentals=0),
        name=kernel.__name__,
    )(*values)


def finish(kernel, chunks, outs):
    return in_vmem(kernel, [term for chunk in chunks for term in chunk], outs)


def after(values, *others):
    return lax.optimization_barrier((values, *others))[0] if others else values


class Order:
    depths = {"x": 2, "y": 2, "core": 3, "one": 9, "two": 9, "three": 9}

    def __init__(self):
        self.kernel, self.last = [], []
        self.sent = {link: [] for link in self.depths}

    def ran(self, token, *beside):
        self.kernel, self.last = [token, *beside], []

    def use(self, values):
        return after(values, *self.kernel, *self.last)

    def settle(self, *values):
        self.last = [*self.last, *values]

    def did(self, values):
        self.last = [values]
        return values

    def send(self, link, values, axis, pairs, depth=None):
        sent, depth = self.sent[link], depth or self.depths[link]
        values = after(values, *self.kernel, *sent[max(len(sent) - depth, 0) : max(len(sent) - depth + 1, 0)])
        sent.append(lax.ppermute(values, axis, pairs))
        return sent[-1]

    def swap(self, link, values, depth=None):
        mask = {"core": 1, "x": 2, "y": 4}[link]
        return self.send(link, values, "fsdp", [(place, place ^ mask) for place in range(8)], depth)


def add_far_kernel(count, *refs):
    refs = Refs(refs)
    terms = [refs.take(2) for _ in range(count)]
    targets = refs.take(2)
    first = 0
    for keep, got in terms:
        rows = slice(first, first + keep.shape[2])
        first = rows.stop
        for side, target in enumerate(targets):
            target[rows] = rounded(plus(keep[0, side], got[0, side]))


def add_near_kernel(count, *refs):
    refs = Refs(refs)
    terms_x = [refs.take(2) for _ in range(count)]
    terms_y = [refs.take(2) for _ in range(count)]
    from_x, from_y, *targets = refs.refs
    joined = len(targets) == 2
    for number, (terms, side_more, more) in enumerate(((terms_x, 1, from_y), (terms_y, 0, from_x))):
        first = 0
        for keep, got in terms:
            rows = slice(first, first + keep.shape[2])
            first = rows.stop
            for side in range(2):
                extra = [more[rows]] if side == side_more else []
                target = targets[number].at[side] if joined else targets[2 * number + side].at[0]
                target[rows] = rounded(plus(keep[0, side], got[0, side], *extra))


def add_own_kernel(count, *refs):
    refs = Refs(refs)
    terms = [refs.take(2) for _ in range(count)]
    from_x, from_y = refs.take(2)
    first = 0
    for keep, got in terms:
        rows = slice(first, first + keep.shape[2])
        first = rows.stop
        for side in range(keep.shape[1]):
            target = refs.refs[0].at[side] if len(refs.refs) == 1 else refs.refs[side].at[0]
            target[rows] = rounded(plus(keep[0, side], got[0, side], from_x[side, rows], from_y[side, rows]))


def combine(kernel, places, keeps, gots, others, outs, side=None):
    half = keeps[0].shape[2]
    steps = half // 192 if half % 192 == 0 and len(keeps) == 1 else 1

    def spec(values, place=0):
        *more, rows, _ = values.shape
        if len(more) == 2:
            if side is not None:
                return pl.BlockSpec((1, 1, rows // steps, D), lambda block: (place, side, block, 0))
            return pl.BlockSpec((1, 2, rows // steps, D), lambda block: (place, 0, block, 0))
        return pl.BlockSpec((*more, rows // steps, D), lambda block: (*[0] * len(more), block, 0))

    terms = [term for keep, got in zip(keeps, gots) for term in (keep, got)]
    return pl.pallas_call(
        functools.partial(kernel, len(keeps)),
        grid=(steps,),
        in_specs=[spec(term, place) for place in places for term in terms] + [spec(leaf) for leaf in others],
        out_specs=[spec(leaf) for leaf in outs],
        out_shape=outs,
        compiler_params=pltpu.CompilerParams(vmem_limit_bytes=60 * 1024 * 1024),
        cost_estimate=pl.CostEstimate(flops=0, bytes_accessed=1024, transcendentals=0),
        name=kernel.__name__,
    )(*terms * len(places), *others)


class Gather:
    def __init__(self, order, shard, fars):
        self.order, self.shard, self.fars = order, shard, fars
        self.far_parts, self.far_cores = {}, {}

    def near(self, depth=1):
        self.near_x = self.order.swap("x", self.shard, depth)
        self.near_y = self.order.swap("y", self.shard, depth)

    def far(self, number=0):
        first, middle, last = self.fars[number]
        to_x = self.order.did(self.order.use(self.near_y)[first:middle])
        to_y = self.order.did(self.order.use(self.near_x)[middle:last])
        self.far_parts[number] = [self.order.swap("x", to_x), self.order.swap("y", to_y)]

    def own_core(self):
        self.own = self.order.swap("core", self.shard)

    def near_core(self):
        self.cores = [self.order.swap("core", piece) for piece in (self.near_x, self.near_y)]

    def far_core(self, number=0):
        self.far_cores[number] = [self.order.swap("core", self.order.use(piece)) for piece in self.far_parts[number]]

    def pieces(self, number=0, sides=(0, 1)):
        pieces = [self.shard, self.own]
        for piece, core in zip((self.near_x, self.near_y), self.cores):
            pieces += [piece, core]
        for side in sides:
            pieces += [self.far_parts[number][side], self.far_cores[number][side]]
        return pieces


class Line:
    def __init__(self, order):
        self.order = order

    def line(self, own):
        self.own = own
        self.order.did(own[0])
        self.one, self.two, self.three = [[None] * len(own) for _ in range(3)]

    def first(self):
        self.one = [self.order.send("one", own, "dp", [(0, 1), (3, 2)]) for own in self.own]

    def second(self, number=0):
        own = self.order.did(rounded(plus(self.own[number], self.order.use(self.one[number]))))
        self.two[number] = self.order.send("two", own, "dp", [(1, 2), (2, 1)])

    def third(self, number=0):
        own = self.order.did(rounded(plus(self.own[number], self.order.use(self.two[number]))))
        self.three[number] = self.order.send("three", own, "dp", [(1, 0), (2, 3)])

    def terms(self, number=0):
        terms = self.own[number], self.one[number], self.two[number], self.three[number]
        return [term.reshape(-1, D) for term in terms]


class Reduce(Line):
    def __init__(self, order, keep, send):
        super().__init__(order)
        self.half = keep.shape[1] // 2
        self.keeps = [keep.reshape(4, 2, self.half, D)]
        self.gots = [order.swap("core", send).reshape(4, 2, self.half, D)]

    def join(self, other):
        self.half += other.half
        self.keeps += other.keeps
        self.gots += other.gots

    def far(self):
        outs = [shape(self.half, D, dtype=BF)] * 2
        gots = [self.order.use(got) for got in self.gots]
        to_x, to_y = combine(add_far_kernel, (3,), self.keeps, gots, [], outs)
        self.order.did(to_x)
        self.from_x, self.from_y = self.order.swap("x", to_x), self.order.swap("y", to_y)

    def near(self, parts=1):
        outs = [shape(2 // parts, self.half, D, dtype=BF)] * (2 * parts)
        others = [self.order.use(self.from_x), self.from_y]
        made = combine(add_near_kernel, (1, 2), self.keeps, self.gots, others, outs)
        self.order.did(made[0])
        arrived = [[], []]
        for part in range(parts):
            for number, link in enumerate("xy"):
                arrived[number].append(self.order.swap(link, made[parts * number + part]))
        self.from_x, self.from_y = arrived

    def plane(self, parts):
        others = [self.order.use(self.from_x[0]), self.from_y[0]]
        outs = [shape(2 // parts, self.half, D, dtype=BF)] * parts
        self.line(combine(add_own_kernel, (0,), self.keeps, self.gots, others, outs))

    def plane_side(self, side):
        if side == 0:
            self.own, self.one, self.two, self.three = [[None] * 2 for _ in range(4)]
        others = [self.order.use(self.from_x[side]), self.from_y[side]]
        outs = [shape(1, self.half, D, dtype=BF)]
        self.own[side] = combine(add_own_kernel, (0,), self.keeps, self.gots, others, outs, side)[0]
        self.order.did(self.own[side])
        self.one[side] = self.order.send("one", self.own[side], "dp", [(0, 1), (3, 2)])


def body(
    language,
    vision,
    region_mask,
    cross_qkv,
    cross_out,
    cross_bias,
    cross_gain,
    self_qkv,
    self_out,
    self_bias,
    self_gain,
    ffn_up,
    ffn_up_bias,
    ffn_down,
    ffn_bias,
    ffn_gain,
    language_cotangent,
    vision_cotangent,
):
    plane, line = lax.axis_size("fsdp"), lax.axis_size("dp")
    swaps = plane == 8 and line == 4
    rank = lax.axis_index("fsdp")
    items, words, _ = language.shape
    regions = vision.shape[1]
    local = cross_gain.shape[0]
    counts = (items * words, items * regions)
    every = sum(counts)
    by_place = lambda values: values.transpose(1, 0, 2).reshape(-1, D)
    by_item = lambda values: values.reshape(-1, items, D).transpose(1, 0, 2)
    tangents = (by_place(language_cotangent), by_place(vision_cotangent))
    numbers = jnp.concatenate([rank.astype(jnp.int32)[None], jnp.sum(region_mask, axis=1)])

    if swaps:
        leaves = [cross_qkv, cross_out, cross_bias, cross_gain[None], self_bias, self_gain, ffn_bias, ffn_gain, ffn_up_bias]
        scratch = [pltpu.VMEM((VECTORS, D), F32)]
        cross_shard = in_vmem(pack_cross_kernel, leaves, [shape(4 * local + VECTORS, D, dtype=BF)], scratch)[0]
        rest = [self_qkv, self_out, ffn_up, ffn_down]
        token = lax.slice(cross_shard, (4 * local, 0), (4 * local + 16, 128))
        own_shard, *feed_shards = in_vmem(pack_rest_kernel, [token, *rest], [shape(8 * local, D, dtype=BF)] * 3)
        rows = 4 * local
        spans = [(place * local, local) for place in range(4)]
        cross_chunk = Chunk(8, True, True, rows + VECTORS, spans + [(rows, VECTORS)], 0, 2 * local)
        self_chunks = [Chunk(8, True, True, rows, spans, stream * rows) for stream in range(2)]
        feed_chunks = [Chunk(8, True, out, 2 * rows, spans + [(rows, rows)], 0, rows) for out in (False, True)]
        given = []
    else:
        small = jnp.concatenate(
            [cross_bias, cross_gain[None], self_bias.reshape(8, local), self_gain, ffn_bias.reshape(4, local), ffn_gain]
        )
        self_shards = [rounded(jnp.concatenate([self_qkv[s].reshape(3 * local, D), self_out[s]])) for s in range(2)]
        up_shards = [rounded(ffn_up[s]).reshape(local, 4, D).transpose(1, 0, 2).reshape(4 * local, D) for s in range(2)]
        down_shards = [rounded(ffn_down[s]) for s in range(2)]

        def gather(shard):
            whole = lax.all_gather(shard.reshape(4, local, D), "fsdp", axis=1, tiled=True)
            return whole.reshape(4, 4, D // 4, D).transpose(1, 0, 2, 3).reshape(4, D, D)

        cross_shard = rounded(jnp.concatenate([cross_qkv.reshape(3 * local, D), cross_out]))
        spans = [(place * D // 4, D // 4) for place in range(4)]
        cross_chunk = Chunk(4, False, False, D, spans)
        self_chunks = [Chunk(4, False, False, D, spans)] * 2
        feed_chunks = [Chunk(4, False, False, 2 * D, spans + [(D, D)])] * 2
        vectors = widened(lax.all_gather(rounded(small), "fsdp", axis=1, tiled=True))
        up_bias = widened(lax.all_gather(rounded(ffn_up_bias), "fsdp", axis=1, tiled=True)).reshape(8, D)
        given = [jnp.pad(vectors, ((0, VECTORS - NARROW), (0, 0))), up_bias]

    def biases(rows, keys):
        return pltpu.VMEM((rows, keys), F32)

    def kept(rows, keys):
        return shape(HEADS, rows, keys, dtype=BF)

    both = [biases(counts[0], counts[1]), biases(counts[1], counts[0])]

    def cross_forward(pieces):
        return run(
            functools.partial(cross_forward_kernel, cross_chunk, len(given)),
            "cross_forward",
            numbers,
            [by_place(language), by_place(vision), *given],
            pieces,
            [shape(counts[0], D), shape(counts[1], D), shape(every, D, dtype=BF), shape(every, D)]
            + [shape(every, D, dtype=BF)] * 4
            + [kept(counts[0], counts[1]), kept(counts[1], counts[0])]
            + [shape(VECTORS, D), shape(8, D)],
            [],
            [cross_chunk.held] + both + [cross_chunk.sems],
        )

    def self_forward(stream, inputs, vectors, pieces):
        count, chunk = counts[stream], self_chunks[stream]
        return run(
            functools.partial(self_forward_kernel, stream, chunk),
            f"self_forward_{stream}",
            numbers,
            [inputs, vectors],
            pieces,
            [shape(count, D)] * 2 + [shape(count, D, dtype=BF)] * 4 + [kept(count, count)],
            [],
            [chunk.held, biases(count, count), chunk.sems],
        )

    def feed(stream, inputs, vectors, up_bias, pieces):
        count, chunk = counts[stream], feed_chunks[stream]
        return run(
            functools.partial(feed_kernel, stream, chunk),
            f"feed_{stream}",
            numbers,
            [inputs, tangents[stream], vectors, up_bias],
            pieces,
            [shape(count, D, dtype=BF), shape(count, D), shape(8, D), shape(4, D)],
            chunk.targets,
            [chunk.held] * 2
            + [pltpu.VMEM((4, count, D), F32), pltpu.VMEM((4, count, D), BF)]
            + [pltpu.VMEM((count, D), F32)]
            + [chunk.sems] * 2,
        )

    def self_backward(stream, gradient, inputs, self_kept, vectors, pieces):
        count, chunk = counts[stream], self_chunks[stream]
        return run(
            functools.partial(self_backward_kernel, stream, chunk),
            f"self_backward_{stream}",
            numbers,
            [gradient, inputs, *self_kept, vectors],
            pieces,
            [shape(count, D), shape(8, D)],
            chunk.targets,
            [chunk.held] * 2 + [pltpu.VMEM((count, D), BF)] * 5 + [chunk.sems] * 2,
        )

    def cross_backward(gradients, cross_kept, vectors, smalls, pieces):
        chunk = cross_chunk
        return run(
            functools.partial(cross_backward_kernel, chunk),
            "cross_backward",
            numbers,
            [*gradients, *cross_kept, vectors, *smalls],
            pieces,
            [shape(counts[0], D), shape(counts[1], D)] + ([] if swaps else [shape(VECTORS, D), shape(8, D)]),
            chunk.targets,
            [chunk.held] * 2
            + [pltpu.VMEM((every, D), F32)] * 2
            + [pltpu.VMEM((VECTORS, D), F32)]
            + [pltpu.VMEM((every, D), BF)] * 5
            + [chunk.sems] * 2,
        )

    if swaps:
        order = Order()
        cross = Gather(order, cross_shard, [(0, 2 * local, rows + VECTORS)])
        own = Gather(order, own_shard, [(0, rows, 2 * rows)])
        feed_l, feed_v = [Gather(order, shard, [(0, rows, 2 * rows)]) for shard in feed_shards]
        cross.near()
        cross.own_core()
        order.did(own_shard)
        cross.far()
        own.near()
        cross.near_core()
        cross.far_core()
        made = cross_forward(cross.pieces())
        first_a, cross_kept, (vectors, up_bias) = made[:2], made[2:10], made[10:]
        order.ran(up_bias, own.near_x, own.near_y)

        own.far()
        own.own_core()
        own.near_core()
        feed_l.near()
        own.far_core()
        second_l = self_forward(0, first_a[0], order.use(vectors), own.pieces(0, (0,)))
        second_v = self_forward(1, after(first_a[1], second_l[0]), vectors, own.pieces(0, (1,)))
        order.ran(second_v[0], feed_l.near_x, feed_l.near_y)

        feed_l.far()
        feed_l.own_core()
        feed_l.near_core()
        feed_v.near()
        feed_l.far_core()
        fed_l = feed(0, second_l[0], order.use(vectors), up_bias, feed_l.pieces())
        order.ran(fed_l[2])

        feed_v.own_core()
        back_l = self_backward(0, fed_l[1], first_a[0], second_l[1:], order.use(vectors), own.pieces(0, (0,)))
        order.ran(back_l[1], feed_v.near_x, feed_v.near_y, feed_v.own)
        summed_l = lax.psum_scatter(order.use(fed_l[4]), "fsdp", scatter_dimension=0)

        feed_v.far()
        feed_v.near_core()
        sum_self_l = Reduce(order, *back_l[2:])
        sum_self_l.far()
        feed_v.far_core()
        fed_v = feed(1, second_v[0], order.use(vectors), up_bias, feed_v.pieces())
        order.ran(fed_v[2], sum_self_l.from_x, sum_self_l.from_y)

        sum_self_l.near()
        sum_feed_v = Reduce(order, *fed_v[4:])
        back_v = self_backward(1, fed_v[1], first_a[1], second_v[1:], order.use(vectors), own.pieces(0, (1,)))
        order.ran(back_v[1], *sum_self_l.from_x, *sum_self_l.from_y, *sum_feed_v.gots)

        sum_feed_v.far()
        sum_last = Reduce(order, *back_v[2:])
        sum_self_l.plane(1)
        sum_self_l.first()
        smalls = [back_l[1], back_v[1], fed_l[2], fed_v[2], fed_l[3], fed_v[3]]
        made = cross_backward([back_l[0], back_v[0]], cross_kept, order.use(vectors), smalls, cross.pieces())
        gradients = made[:2]
        order.ran(made[1], sum_feed_v.from_x, sum_feed_v.from_y, *sum_self_l.one, *sum_last.gots)

        sum_feed_l = Line(order)
        sum_feed_l.line([order.use(summed_l)])
        sum_feed_l.first()
        sum_last.join(Reduce(order, *made[2:]))
        sum_feed_v.near()
        sum_self_l.second()
        sum_last.far()
        sum_feed_l.second()
        sum_self_l.third()
        sum_feed_v.plane(2)
        sum_feed_v.first()
        sum_last.near()
        sum_feed_v.second(0)
        sum_feed_l.third()
        sum_feed_v.second(1)
        sum_last.plane(2)
        sum_last.first()
        sum_feed_v.third(0)
        order.settle(*sum_feed_l.three)
        sum_last.second(0)
        order.settle(*sum_self_l.three)
        sum_feed_v.third(1)
        sum_last.second(1)
        order.settle(sum_feed_v.three[0])
        sum_last.third(0)
        order.settle(sum_feed_v.three[1])
        sum_last.third(1)
        feed_terms = [sum_feed_l.terms()] + [sum_feed_v.terms(number) for number in range(2)]
        feed_terms[0][0] = order.use(feed_terms[0][0])
        feed_grads = finish(finish_feed_kernel, feed_terms, [shape(*ffn_up.shape), shape(*ffn_down.shape)])
        leaves = [self_qkv, self_out, cross_qkv, cross_out, cross_bias, cross_gain[None], self_bias, self_gain]
        leaves += [ffn_up_bias, ffn_bias, ffn_gain]
        last_terms = [sum_self_l.terms()] + [sum_last.terms(number) for number in range(2)]
        last_terms[0][0] = after(last_terms[0][0], feed_grads[0])
        rest = finish(finish_rest_kernel, last_terms, [shape(*leaf.shape) for leaf in leaves])
        grads = [*rest[2:5], rest[5][0], *rest[:2], *rest[6:8], feed_grads[0], rest[8], feed_grads[1], *rest[9:]]
        outputs = fed_l[0], fed_v[0]
    else:
        cross_pieces = [gather(cross_shard)]
        self_pieces = [[gather(shard)] for shard in self_shards]
        feed_pieces = []
        for up, down in zip(up_shards, down_shards):
            down = lax.all_gather(down, "fsdp", axis=0, tiled=True).reshape(4, D, D)
            feed_pieces.append([jnp.concatenate([gather(up), down], axis=1)])
        made = cross_forward(cross_pieces)
        first_a, cross_kept, (vectors, up_bias) = made[:2], made[2:10], made[10:]
        second = [self_forward(s, first_a[s], vectors, self_pieces[s]) for s in range(2)]
        fed = [feed(s, second[s][0], vectors, up_bias, feed_pieces[s]) for s in range(2)]
        back = [self_backward(s, fed[s][1], first_a[s], second[s][1:], vectors, self_pieces[s]) for s in range(2)]
        smalls = [back[0][1], back[1][1], fed[0][2], fed[1][2], fed[0][3], fed[1][3]]
        made = cross_backward([back[0][0], back[1][0]], cross_kept, vectors, smalls, cross_pieces)
        gradients = made[:2]
        outputs = fed[0][0], fed[1][0]

        def whole(grad, by_owner=True):
            if by_owner:
                grad = grad.reshape(4, 4, D // 4, D).transpose(1, 0, 2, 3).reshape(4, D, D)
                own = lax.psum_scatter(grad, "fsdp", scatter_dimension=1, tiled=True)
            else:
                own = lax.psum_scatter(grad.reshape(4 * D, D), "fsdp", scatter_dimension=0, tiled=True)
            return widened(lax.psum(own, "dp")).reshape(4 * local, D)

        up_done = [whole(made_s[4][:, :D]) for made_s in fed]
        down_done = [whole(made_s[4][:, D:], False) for made_s in fed]
        self_done = [whole(made_s[2]) for made_s in back]
        cross_done = whole(made[4])
        small = lax.dynamic_slice(lax.psum(made[2], ("fsdp", "dp")), (0, rank * local), (NARROW, local))
        up_small = lax.psum(made[3], ("fsdp", "dp")).reshape(2, 4 * D)
        up_small = lax.dynamic_slice(up_small, (0, 4 * rank * local), (2, 4 * local))
        up_grads = [done.reshape(4, local, D).transpose(1, 0, 2).reshape(local, 4 * D) for done in up_done]
        grads = [cross_done[: 3 * local].reshape(3, local, D), cross_done[3 * local :], small[0:4], small[4]]
        grads += [jnp.stack([done[: 3 * local].reshape(3, local, D) for done in self_done])]
        grads += [jnp.stack([done[3 * local :] for done in self_done])]
        grads += [small[5:13].reshape(2, 4, local), small[13:15], jnp.stack(up_grads), up_small, jnp.stack(down_done)]
        grads += [small[15:19].reshape(2, 2, local), small[19:21]]

    return (*[by_item(rows) for rows in (*outputs, *gradients)], *grads)


def solution(mesh):
    return jax.shard_map(
        body,
        mesh=mesh,
        in_specs=(
            P(("fsdp", "dp"), None, None),
            P(("fsdp", "dp"), None, None),
            P(("fsdp", "dp"), None),
            P(None, "fsdp", None),
            P("fsdp", None),
            P(None, "fsdp"),
            P("fsdp"),
            P(None, None, "fsdp", None),
            P(None, "fsdp", None),
            P(None, None, "fsdp"),
            P(None, "fsdp"),
            P(None, "fsdp", None),
            P(None, "fsdp"),
            P(None, "fsdp", None),
            P(None, None, "fsdp"),
            P(None, "fsdp"),
            P(("fsdp", "dp"), None, None),
            P(("fsdp", "dp"), None, None),
        ),
        out_specs=(
            P(("fsdp", "dp"), None, None),
            P(("fsdp", "dp"), None, None),
            P(("fsdp", "dp"), None, None),
            P(("fsdp", "dp"), None, None),
            P(None, "fsdp", None),
            P("fsdp", None),
            P(None, "fsdp"),
            P("fsdp"),
            P(None, None, "fsdp", None),
            P(None, "fsdp", None),
            P(None, None, "fsdp"),
            P(None, "fsdp"),
            P(None, "fsdp", None),
            P(None, "fsdp"),
            P(None, "fsdp", None),
            P(None, None, "fsdp"),
            P(None, "fsdp"),
        ),
        check_vma=False,
    )
```
